32 devices in a mesh: wide: 8 (over y, x, core), narrow: 4 (over z).
Axes of the slice: x: 2, y: 2, z: 4, core: 2. Of those that a mesh axis runs over, the one named last changes fastest.
Arguments:
- features: bfloat16 [32768, 512], P(('wide', 'narrow')), may hold values from -240 to 240
- presence: int32 [32768, 8], P(('wide', 'narrow')), may hold values 0 or 1
- first_params: bfloat16 [1196032], P(('wide', 'narrow')), may hold values from -4 to 4
- second_params: bfloat16 [880640], P(('wide', 'narrow')), may hold values from -4 to 4
- cotangent: bfloat16 [32768, 128], P(('wide', 'narrow')), may hold values from -6 to 6
Outputs:
- towers: float32 [32768, 128], P(('wide', 'narrow'))
- input_grad: float32 [32768, 512], P(('wide', 'narrow'))
- first_grad: float32 [1196032], P(('wide', 'narrow'))
- second_grad: float32 [880640], P(('wide', 'narrow'))
The draws below stay inside these ranges and needn't reach their ends.
All inputs are finite; a program needn't handle non-finite values. No bound on the sum of `presence` on one device may be relied on, other than what follows from the above.
Results may differ from the reference program's by a relative error of at most 0.0093.
Values may be sent and summed in bfloat16 or wider, within the bound.
No kernel may reach another device: no remote copies, remote signals or barrier semaphores. Data moves between devices by JAX's collectives and lax.ppermute only.
A program may use at most 192 MiB of HBM per device.

```python
import math
import jax
import jax.numpy as jnp
from jax import lax

FIELDS = 8
FIELD_W = 64
D = 512
H = 256
TOWER1 = 128
TOWER2 = 64
TOKENS = 32768
FLAT1 = 1196032
FLAT2 = 880640


def layout_values(base, pieces):
    scales = []
    offsets = []
    used = 0
    for amount, scale_now, offset_now in pieces:
        scales.append(jnp.full((amount,), scale_now, jnp.float32))
        offsets.append(jnp.full((amount,), offset_now, jnp.float32))
        used += amount
    remaining = base.shape[0] - used
    scales.append(jnp.ones((remaining,), jnp.float32))
    offsets.append(jnp.zeros((remaining,), jnp.float32))
    return jnp.concatenate(offsets) + jnp.concatenate(scales) * base


def first_layout():
    return [(D, 0.25, 1.0), (D, 0.3, 0.0), (6 * D * H, D ** (-0.5), 0.0), (6 * H, 0.3, 0.0), (6 * H * H, H ** (-0.5), 0.0), (6 * H, 0.3, 0.0), (6 * H, 0.25, 1.0), (6 * H, 0.3, 0.0), (14 * D, 0.75 * D ** (-0.5), 0.0)]


def second_layout():
    return [(6 * H * H, H ** (-0.5), 0.0), (6 * H, 0.3, 0.0), (6 * H * H, H ** (-0.5), 0.0), (6 * H, 0.3, 0.0), (6 * H, 0.25, 1.0), (6 * H, 0.3, 0.0), (8 * H, 1.4 * H ** (-0.5), 0.0), (2 * H * TOWER1, H ** (-0.5), 0.0), (2 * TOWER1, 0.3, 0.0), (2 * TOWER1 * TOWER2, TOWER1 ** (-0.5), 0.0), (2 * TOWER2, 0.3, 0.0)]


def draw_first_params(key, part):
    key = jax.random.fold_in(key, 11)
    base = jnp.clip(jax.random.normal(key, (FLAT1,), jnp.float32), -4.0, 4.0)
    return layout_values(base, first_layout()).astype(jnp.bfloat16)


def draw_second_params(key, part):
    key = jax.random.fold_in(key, 13)
    base = jnp.clip(jax.random.normal(key, (FLAT2,), jnp.float32), -4.0, 4.0)
    return layout_values(base, second_layout()).astype(jnp.bfloat16)


def draw_features(key, part):
    key = jax.random.fold_in(key, 5)
    key_base, key_column = jax.random.split(key, 2)
    positions = jnp.arange(TOKENS, dtype=jnp.float32)
    rising = 1.0 + 2.0 * positions / max(TOKENS - 1, 1)
    column_scale = jnp.exp(jax.random.uniform(key_column, (D,), jnp.float32, 0.0, math.log(10.0)))
    base = jnp.clip(jax.random.normal(key_base, (TOKENS, D), jnp.float32), -4.0, 4.0)
    row_scale = rising
    values = column_scale[None, :] * (row_scale[:, None] * base)
    return values.astype(jnp.bfloat16)


def place_ends(values, rng, smallest, high):
    longest = values.shape.index(max(values.shape))
    spots = []
    for shift in (0, 1):
        where = [jax.random.randint(jax.random.fold_in(rng, axis), (), 0, length) for axis, length in enumerate(values.shape)]
        where[longest] = (where[longest] + shift) % values.shape[longest]
        spots.append(tuple(where))
    return values.at[spots[0]].set(smallest).at[spots[1]].set(high)


def shard_levels(stream_key, dims, cuts, smallest, high):
    def one(dim, blocks):
        heights = jax.random.uniform(jax.random.fold_in(jax.random.fold_in(stream_key, 6), dim), (blocks,), jnp.float32, smallest / len(cuts), high / len(cuts))
        return jnp.repeat(jnp.exp(heights), dims[dim] // blocks).reshape((-1,) + (1,) * (len(dims) - dim - 1))

    factor_of = one(*cuts[0])
    for cut in cuts[1:]:
        factor_of = factor_of * one(*cut)
    return factor_of


def gaussian(stream_key, dims, spread, reach, cuts=(), kind=jnp.bfloat16):
    array = spread * jax.random.normal(stream_key, dims, jnp.float32)
    if cuts:
        array = array * shard_levels(stream_key, dims, cuts, -0.22, 0.18)
    return jnp.clip(array, -reach, reach).astype(kind)


def setup_inputs(seed: int = 0) -> dict:
    seeds = jax.random.split(jax.random.key(seed), 6)
    features = draw_features(jax.random.fold_in(seeds[5], 71), 0)
    presence = place_ends((jax.random.randint(seeds[1], (TOKENS, FIELDS), 0, 8) < 7).astype(jnp.int32), jax.random.fold_in(seeds[1], 1), 0, 1)
    first_params = draw_first_params(jax.random.fold_in(seeds[5], 71), 0)
    second_params = draw_second_params(jax.random.fold_in(seeds[5], 71), 0)
    cotangent = gaussian(seeds[4], (TOKENS, 2 * TOWER2), 1.0, 6.0, ((0, 32),))
    return {"features": features, "presence": presence, "first_params": first_params, "second_params": second_params, "cotangent": cotangent}


@jax.custom_vjp
def low(v):
    return lax.optimization_barrier(v.astype(jnp.bfloat16)).astype(jnp.float32)

@jax.custom_vjp
def low_back(v):
    return v

def low_keep(v):
    return (low(v), None)

def low_pass(kept, grad):
    return (grad,)

def back_keep(v):
    return (v, None)

def back_low(kept, grad):
    return (low(grad),)
low.defvjp(low_keep, low_pass)
low_back.defvjp(back_keep, back_low)
EPSILON = 1e-05
HIGHEST = lax.Precision.HIGHEST

def cut_pieces(flat_vector, shapes):
    pieces = []
    offset = 0
    for shape_now in shapes:
        amount = math.prod(shape_now)
        pieces.append(flat_vector[offset:offset + amount].reshape(shape_now))
        offset += amount
    return pieces

def first_shapes():
    return [(D,), (D,), (6, D, H), (6, H), (6, H, H), (6, H), (6, H), (6, H), (D, 14)]

def second_shapes():
    return [(6, H, H), (6, H), (6, H, H), (6, H), (6, H), (6, H), (2, H, 4), (2, H, TOWER1), (2, TOWER1), (2, TOWER1, TOWER2), (2, TOWER2)]

def mix_parts(weights, parts):
    running = weights[:, 0:1] * parts[0]
    for position in range(1, len(parts)):
        running = running + weights[:, position:position + 1] * parts[position]
    return running

def expert_layer(inputs, expert_in, in_bias, expert_out, out_bias, norm_gain, norm_bias):
    groups = inputs.shape[0]
    per_group = 6 // groups
    width_in = expert_in.shape[1]
    weight_in = expert_in.reshape(groups, per_group, width_in, H)
    weight_out = expert_out.reshape(groups, per_group, H, H)
    pre_act = jnp.einsum('grd,gedh->gerh', inputs, weight_in, precision=HIGHEST) + in_bias.reshape(groups, per_group, 1, H)
    pre_act = low_back(pre_act)
    active = low(jax.nn.silu(pre_act))
    post_act = jnp.einsum('gerh,gehk->gerk', active, weight_out, precision=HIGHEST) + out_bias.reshape(groups, per_group, 1, H)
    post_act = low_back(post_act)
    centred = post_act - lax.optimization_barrier(jnp.mean(post_act, axis=-1, keepdims=True))
    normal_out = centred * lax.rsqrt(lax.optimization_barrier(jnp.mean(centred * centred, axis=-1, keepdims=True)) + EPSILON)
    result = normal_out * norm_gain.reshape(groups, per_group, 1, H) + norm_bias.reshape(groups, per_group, 1, H)
    return result.reshape(6, inputs.shape[1], H)

def block_forward(row_block, column_mean, inv_scale, first_full, second_full):
    in_gain, in_bias, expert_in, expert_in_bias, expert_out, expert_out_bias, norm_gain, norm_bias, gate_table = cut_pieces(first_full, first_shapes())
    normed = (row_block - column_mean) * inv_scale
    level_input = low(normed * in_gain + in_bias)
    outputs_one = expert_layer(level_input[None], expert_in, expert_in_bias, expert_out, expert_out_bias, norm_gain, norm_bias)
    logits_one = low_back(jnp.dot(level_input, gate_table, precision=HIGHEST))
    gate_a = jax.nn.softmax(logits_one[:, 0:4], axis=-1)
    gate_b = jax.nn.softmax(logits_one[:, 4:8], axis=-1)
    gate_s = jax.nn.softmax(logits_one[:, 8:14], axis=-1)
    mixed_a = mix_parts(gate_a, [outputs_one[0], outputs_one[1], outputs_one[4], outputs_one[5]])
    mixed_b = mix_parts(gate_b, [outputs_one[2], outputs_one[3], outputs_one[4], outputs_one[5]])
    mixed_s = mix_parts(gate_s, [outputs_one[member] for member in range(6)])
    second_input = low(jnp.stack([mixed_a, mixed_b, mixed_s]))
    expert_in_two, in_bias_two, expert_out_two, out_bias_two, norm_gain_two, norm_bias_two, gate_table_two, tower_in, tower_in_bias, tower_out, tower_out_bias = cut_pieces(second_full, second_shapes())
    outputs_two = expert_layer(second_input, expert_in_two, in_bias_two, expert_out_two, out_bias_two, norm_gain_two, norm_bias_two)
    results = []
    for task_index in range(2):
        logits_two = low_back(jnp.dot(second_input[task_index], gate_table_two[task_index], precision=HIGHEST))
        probabilities = jax.nn.softmax(logits_two, axis=-1)
        combined = low(mix_parts(probabilities, [outputs_two[2 * task_index], outputs_two[2 * task_index + 1], outputs_two[4], outputs_two[5]]))
        tower_pre = low_back(jnp.dot(combined, tower_in[task_index], precision=HIGHEST) + tower_in_bias[task_index])
        tower_act = low(jax.nn.silu(tower_pre))
        results.append(jnp.dot(tower_act, tower_out[task_index], precision=HIGHEST) + tower_out_bias[task_index])
    return jnp.concatenate(results, axis=1)

def reference(features, presence, first_params, second_params, cotangent):
    mask_full = jnp.repeat(presence.astype(jnp.float32), FIELD_W, axis=1)
    block_rows = math.gcd(TOKENS, 4096)
    step_function = jax.checkpoint(block_forward)

    def forward(inputs, first_full, second_full):
        masked = inputs * mask_full
        column_mean = lax.optimization_barrier(jnp.mean(masked, axis=0))
        variance = lax.optimization_barrier(jnp.mean(jnp.square(masked - column_mean), axis=0))
        inv_scale = lax.rsqrt(variance + EPSILON)
        stacked = masked.reshape(TOKENS // block_rows, block_rows, D)
        outputs = lax.map(lambda row_block: step_function(row_block, column_mean, inv_scale, first_full, second_full), stacked)
        return outputs.reshape(TOKENS, 2 * TOWER2)
    towers, pullback = jax.vjp(forward, features.astype(jnp.float32), first_params.astype(jnp.float32), second_params.astype(jnp.float32))
    input_grad, first_grad, second_grad = pullback(cotangent.astype(jnp.float32))
    return (towers, input_grad, first_grad, second_grad)
```

```python
import functools
import math

import jax
import jax.numpy as jnp
from jax import lax
from jax.experimental import pallas as pl
from jax.experimental.pallas import tpu as pltpu
from jax.sharding import PartitionSpec as P

H = 256
TOWER1 = 128
TOWER2 = 64
LANES = 128
EPSILON = 1e-05
AXES = ("wide", "narrow")
F32 = jnp.float32
BF16 = jnp.bfloat16
GROUPS_ONE = ((0, 4), (4, 8), (8, 14))
MEMBERS_ONE = ((0, 1, 4, 5), (2, 3, 4, 5), (0, 1, 2, 3, 4, 5))
GROUPS_TWO = ((0, 4), (4, 8))
MEMBERS_TWO = ((0, 1, 4, 5), (2, 3, 4, 5))
VMEM_LIMIT = 56 * 1024 * 1024


def up(value, step):
    return -(-value // step) * step


def mm(left, right):
    return jnp.dot(left, right, preferred_element_type=F32)


def mm_nt(left, right):
    return lax.dot_general(left, right, (((1,), (1,)), ((), ())), preferred_element_type=F32)


def mm_tn(left, right):
    return lax.dot_general(left, right, (((0,), (0,)), ((), ())), preferred_element_type=F32)


def sigmoid(values):
    return 0.5 * jnp.tanh(0.5 * values) + 0.5


def group_softmax(logits, groups):
    lane = lax.broadcasted_iota(jnp.int32, logits.shape, 1)
    spread = jnp.zeros_like(logits)
    for low, high in groups:
        inside = (lane >= low) & (lane < high)
        peak = jnp.max(jnp.where(inside, logits, -jnp.inf), axis=1, keepdims=True)
        spread = jnp.where(inside, logits - peak, spread)
    raw = jnp.exp(spread)
    result = jnp.zeros_like(logits)
    for low, high in groups:
        inside = (lane >= low) & (lane < high)
        total = jnp.sum(jnp.where(inside, raw, 0.0), axis=1, keepdims=True)
        result = jnp.where(inside, raw / total, result)
    return result


def group_softmax_back(probs, grads, groups):
    lane = lax.broadcasted_iota(jnp.int32, probs.shape, 1)
    product = probs * grads
    result = jnp.zeros_like(probs)
    for low, high in groups:
        inside = (lane >= low) & (lane < high)
        total = jnp.sum(jnp.where(inside, product, 0.0), axis=1, keepdims=True)
        result = jnp.where(inside, product - probs * total, result)
    return result


def into_lane(columns):
    rows = columns[0].shape[0]
    lane = lax.broadcasted_iota(jnp.int32, (rows, LANES), 1)
    result = jnp.zeros((rows, LANES), F32)
    for position, column in enumerate(columns):
        result = jnp.where(lane == position, column, result)
    return result


def mix_parts(weights, low, members, outputs):
    running = None
    for position, member in enumerate(members):
        term = weights[:, low + position : low + position + 1] * outputs[member]
        running = term if running is None else running + term
    return running


def row_sum(values):
    return jnp.sum(values, axis=1, keepdims=True)


def column_sum(values):
    return jnp.sum(values, axis=0, keepdims=True)


def norm_forward(post):
    centred = post - row_sum(post) * (1.0 / H)
    scale = lax.rsqrt(row_sum(centred * centred) * (1.0 / H) + EPSILON)
    return centred * scale, scale


def norm_backward(scaled, normal, scale):
    mean_one = row_sum(scaled) * (1.0 / H)
    mean_two = row_sum(scaled * normal) * (1.0 / H)
    return scale * (scaled - mean_one - normal * mean_two)


def first_layout(width):
    names = (
        ("in_gain", width),
        ("in_bias", width),
        ("expert_in", 6 * width * H),
        ("expert_in_bias", 6 * H),
        ("expert_out", 6 * H * H),
        ("expert_out_bias", 6 * H),
        ("norm_gain", 6 * H),
        ("norm_bias", 6 * H),
        ("gate", 14 * width),
    )
    return place_names(names)


def second_layout():
    names = (
        ("expert_in", 6 * H * H),
        ("expert_in_bias", 6 * H),
        ("expert_out", 6 * H * H),
        ("expert_out_bias", 6 * H),
        ("norm_gain", 6 * H),
        ("norm_bias", 6 * H),
        ("gate", 2 * H * 4),
        ("tower_in", 2 * H * TOWER1),
        ("tower_in_bias", 2 * TOWER1),
        ("tower_out", 2 * TOWER1 * TOWER2),
        ("tower_out_bias", 2 * TOWER2),
    )
    return place_names(names)


def place_names(names):
    rows = {}
    offset = 0
    for name, amount in names:
        rows[name] = offset // LANES
        offset += amount
    return rows, offset // LANES


def spread_pieces(me, count, rows, piece_refs, flat_ref):
    slot = 0
    for ref in piece_refs:
        for index in range(ref.shape[0]):
            owner = lax.bitwise_xor(me, jnp.int32(slot)) if count > 1 else 0
            flat_ref[pl.ds(owner * rows, rows), :] = ref[index, :rows, :].astype(F32)
            slot += 1


def wide_rows(flat_ref, row, amount):
    return jnp.concatenate(
        [flat_ref[pl.ds(row, amount, stride=2), :], flat_ref[pl.ds(row + 1, amount, stride=2), :]],
        axis=1,
    )


def put_wide_rows(flat_ref, row, amount, value):
    flat_ref[pl.ds(row, amount, stride=2), :] = value[:, :LANES]
    flat_ref[pl.ds(row + 1, amount, stride=2), :] = value[:, LANES:]


def collect_pieces(me, count, rows, flat_ref, out_ref):
    for slot in range(count):
        owner = lax.bitwise_xor(me, jnp.int32(slot)) if count > 1 else 0
        out_ref[slot, :rows, :] = flat_ref[pl.ds(owner * rows, rows), :].astype(BF16)


def gate_masks(width, columns, rows):
    period = columns // math.gcd(columns, LANES)
    item = lax.broadcasted_iota(jnp.int32, (width, LANES), 0)
    lane = lax.broadcasted_iota(jnp.int32, (width, LANES), 1)
    lane_a = lax.broadcasted_iota(jnp.int32, (LANES, LANES), 0)
    lane_b = lax.broadcasted_iota(jnp.int32, (LANES, LANES), 1)
    classes = []
    for kind in range(period):
        first = (item * columns) // LANES
        last = (item * columns + columns - 1) // LANES
        row = jnp.where(first % period == kind, first, last)
        match = (row % period == kind) & (row < rows) & ((row * LANES + lane) // columns == item)
        pattern = ((kind * LANES + lane_a) % columns == lane_b).astype(F32).astype(BF16)
        classes.append((row, match, pattern))
    return classes


def table_from_rows(flat, width, columns):
    rows = flat.shape[0]
    result = jnp.zeros((width, LANES), F32)
    index = lax.broadcasted_iota(jnp.int32, (width, rows), 1)
    for row, match, pattern in gate_masks(width, columns, rows):
        pick = (index == row[:, :1]).astype(F32).astype(BF16)
        chosen = mm(pick, flat)
        result = result + mm(jnp.where(match, chosen, 0.0).astype(BF16), pattern)
    return result


def rows_from_table(table, rows, columns):
    width = table.shape[0]
    result = jnp.zeros((rows, LANES), F32)
    index = lax.broadcasted_iota(jnp.int32, (width, rows), 1)
    for row, match, pattern in gate_masks(width, columns, rows):
        pick = (index == row[:, :1]).astype(F32).astype(BF16)
        moved = jnp.where(match, mm_nt(table, pattern), 0.0).astype(BF16)
        result = result + mm_tn(pick, moved)
    return result


def full_spec():
    return pl.BlockSpec(memory_space=pltpu.VMEM)


def tile_spec(shape, tile, dim):
    block = tuple(tile if index == dim else size for index, size in enumerate(shape))
    return pl.BlockSpec(
        block, lambda step: tuple(step if index == dim else 0 for index in range(len(shape)))
    )


def scalar_spec():
    return pl.BlockSpec(memory_space=pltpu.SMEM)


def run_kernel(kernel, grid, in_specs, out_specs, out_shape, scratch, args, flops, nbytes):
    return pl.pallas_call(
        kernel,
        grid=(grid,),
        in_specs=in_specs,
        out_specs=out_specs,
        out_shape=out_shape,
        scratch_shapes=scratch,
        compiler_params=pltpu.CompilerParams(
            dimension_semantics=("arbitrary",), vmem_limit_bytes=VMEM_LIMIT
        ),
        cost_estimate=pl.CostEstimate(flops=flops, bytes_accessed=nbytes, transcendentals=0),
    )(*args)


def spread_presence(presence, width):
    fields = presence.shape[1]
    field = lax.broadcasted_iota(jnp.int32, (fields, width), 0)
    column = lax.broadcasted_iota(jnp.int32, (fields, width), 1)
    pick = (column // (width // fields) == field).astype(F32).astype(BF16)
    return mm(presence.astype(F32).astype(BF16), pick)


def stats_kernel(features_ref, presence_ref, masked_ref, stats_ref):
    rows, width = features_ref.shape
    mask = spread_presence(presence_ref[...], width)
    masked = features_ref[...].astype(F32) * mask
    masked_ref[...] = masked.astype(BF16)
    mean = column_sum(masked) * (1.0 / rows)
    spread = masked - mean
    moment = column_sum(spread * spread)
    for index in range(width // LANES):
        part = slice(index * LANES, (index + 1) * LANES)
        stats_ref[index : index + 1, :] = mean[:, part]
        stats_ref[width // LANES + index : width // LANES + index + 1, :] = moment[:, part]


def from_lanes(block):
    return jnp.concatenate([block[index : index + 1, :] for index in range(block.shape[0])], axis=1)


def level_one_forward(
    count,
    rows,
    total_rows,
    n_pieces,
    me_ref,
    masked_ref,
    stats_ref,
    *rest,
):
    piece_refs = rest[:n_pieces]
    (
        level_ref,
        active_ref,
        slope_ref,
        normal_ref,
        scale_ref,
        probs_ref,
        mixed_ref,
        w_in_ref,
        w_out_ref,
        small_ref,
        gate_ref,
        entry_ref,
        flat_ref,
    ) = rest[n_pieces:]
    width = masked_ref.shape[1]
    where_row, _ = first_layout(width)

    @pl.when(pl.program_id(0) == 0)
    def _():
        spread_pieces(me_ref[0], count, rows, piece_refs, flat_ref)
        for e in range(6):
            w_in_ref[e] = wide_rows(flat_ref, where_row["expert_in"] + e * 2 * width, width).astype(
                BF16
            )
            w_out_ref[e] = wide_rows(flat_ref, where_row["expert_out"] + e * 2 * H, H).astype(BF16)
        for index, name in enumerate(
            ("expert_in_bias", "expert_out_bias", "norm_gain", "norm_bias")
        ):
            small_ref[index, :6, :] = wide_rows(flat_ref, where_row[name], 6)
        gate_flat = flat_ref[pl.ds(where_row["gate"], 14 * width // LANES), :].astype(BF16)
        gate_ref[...] = table_from_rows(gate_flat, width, 14).astype(BF16)
        lanes = width // LANES
        entry_ref[0:1, :] = from_lanes(stats_ref[0:lanes, :])
        variance = from_lanes(stats_ref[lanes : 2 * lanes, :]) * (1.0 / total_rows)
        entry_ref[1:2, :] = lax.rsqrt(variance + EPSILON)
        entry_ref[2:3, :] = from_lanes(flat_ref[0:lanes, :])
        entry_ref[3:4, :] = from_lanes(flat_ref[lanes : 2 * lanes, :])

    normed = (masked_ref[...].astype(F32) - entry_ref[0:1, :]) * entry_ref[1:2, :]
    level = (normed * entry_ref[2:3, :] + entry_ref[3:4, :]).astype(BF16)
    level_ref[...] = level
    probs = group_softmax(mm(level, gate_ref[...]), GROUPS_ONE)
    probs_ref[...] = probs
    outputs = []
    scales = []
    for e in range(6):
        pre = mm(level, w_in_ref[e]) + small_ref[0, e : e + 1, :]
        gate = sigmoid(pre)
        silu = pre * gate
        active = silu.astype(BF16)
        active_ref[e] = active
        slope_ref[e] = (gate + silu * (1.0 - gate)).astype(BF16)
        post = mm(active, w_out_ref[e]) + small_ref[1, e : e + 1, :]
        normal, scale = norm_forward(post)
        normal_ref[e] = normal.astype(BF16)
        scales.append(scale)
        outputs.append(normal * small_ref[2, e : e + 1, :] + small_ref[3, e : e + 1, :])
    scale_ref[...] = into_lane(scales)
    for index, (low, _) in enumerate(GROUPS_ONE):
        mixed_ref[index] = mix_parts(probs, low, MEMBERS_ONE[index], outputs).astype(BF16)


def level_two(count, rows, n_pieces, me_ref, mixed_ref, cotangent_ref, *rest):
    piece_refs = rest[:n_pieces]
    (
        towers_ref,
        mixed_grad_ref,
        grads_ref,
        flat_ref,
        w_in_ref,
        w_out_ref,
        small_ref,
        gate_ref,
        tower_in_ref,
        tower_out_ref,
        tower_tmp_ref,
        tower_small_ref,
        g_in_ref,
        g_out_ref,
        g_small_ref,
        g_gate_ref,
        g_tower_in_ref,
        g_tower_out_ref,
        g_tower_small_ref,
    ) = rest[n_pieces:]
    where_row, used_rows = second_layout()
    lane_h = lax.broadcasted_iota(jnp.int32, (H, LANES), 1)

    @pl.when(pl.program_id(0) == 0)
    def _():
        spread_pieces(me_ref[0], count, rows, piece_refs, flat_ref)
        for e in range(6):
            w_in_ref[e] = wide_rows(flat_ref, where_row["expert_in"] + e * 2 * H, H).astype(BF16)
            w_out_ref[e] = wide_rows(flat_ref, where_row["expert_out"] + e * 2 * H, H).astype(BF16)
        for index, name in enumerate(
            ("expert_in_bias", "expert_out_bias", "norm_gain", "norm_bias")
        ):
            small_ref[index, :6, :] = wide_rows(flat_ref, where_row[name], 6)
        gate_rows = H * 4 // LANES
        shift_a = lax.broadcasted_iota(jnp.int32, (LANES, LANES), 0)
        shift_b = lax.broadcasted_iota(jnp.int32, (LANES, LANES), 1)
        shift = ((shift_a + 4 == shift_b) & (shift_a < 4)).astype(F32).astype(BF16)
        tables = []
        for task in range(2):
            piece = flat_ref[pl.ds(where_row["gate"] + task * gate_rows, gate_rows), :].astype(BF16)
            tables.append(table_from_rows(piece, H, 4).astype(BF16))
        gate_ref[...] = (tables[0].astype(F32) + mm(tables[1], shift)).astype(BF16)
        zero = jnp.zeros((TOWER1, TOWER2), F32)
        for task in range(2):
            tower_in_ref[task] = flat_ref[pl.ds(where_row["tower_in"] + task * H, H), :].astype(
                BF16
            )
            packed = flat_ref[
                pl.ds(where_row["tower_out"] + task * TOWER1 // 2, TOWER1 // 2), :
            ]
            spot = task * TOWER1
            for half in range(2):
                part = packed[:, half * TOWER2 : (half + 1) * TOWER2]
                pair = [part, zero[: TOWER1 // 2]]
                if task == 1:
                    pair.reverse()
                tower_tmp_ref[pl.ds(spot + half, TOWER1 // 2, stride=2), :] = jnp.concatenate(
                    pair, axis=1
                )
        tower_out_ref[...] = tower_tmp_ref[...].astype(BF16)
        tower_small_ref[0:1, :] = from_lanes(flat_ref[pl.ds(where_row["tower_in_bias"], 2), :])
        tower_small_ref[1:2, :LANES] = flat_ref[pl.ds(where_row["tower_out_bias"], 1), :]
        for ref in (
            g_in_ref,
            g_out_ref,
            g_small_ref,
            g_gate_ref,
            g_tower_in_ref,
            g_tower_out_ref,
            g_tower_small_ref,
        ):
            ref[...] = jnp.zeros(ref.shape, F32)

    inputs = [mixed_ref[index] for index in range(3)]
    tile = inputs[0].shape[0]
    lane = lax.broadcasted_iota(jnp.int32, (tile, LANES), 1)
    actives, slopes, normals, scales, outputs = [], [], [], [], []
    for e in range(6):
        pre = mm(inputs[e // 2], w_in_ref[e]) + small_ref[0, e : e + 1, :]
        gate = sigmoid(pre)
        silu = pre * gate
        active = silu.astype(BF16)
        post = mm(active, w_out_ref[e]) + small_ref[1, e : e + 1, :]
        normal, scale = norm_forward(post)
        actives.append(active)
        slopes.append((gate + silu * (1.0 - gate)).astype(BF16))
        normals.append(normal)
        scales.append(scale)
        outputs.append(normal * small_ref[2, e : e + 1, :] + small_ref[3, e : e + 1, :])
    logits = jnp.where(lane < 4, mm(inputs[0], gate_ref[...]), mm(inputs[1], gate_ref[...]))
    probs = group_softmax(logits, GROUPS_TWO)
    combined = [
        mix_parts(probs, 4 * task, MEMBERS_TWO[task], outputs).astype(BF16) for task in range(2)
    ]
    tower_pre = (
        jnp.concatenate([mm(combined[task], tower_in_ref[task]) for task in range(2)], axis=1)
        + tower_small_ref[0:1, :]
    )
    tower_gate = sigmoid(tower_pre)
    tower_silu = tower_pre * tower_gate
    tower_active = tower_silu.astype(BF16)
    towers_ref[...] = mm(tower_active, tower_out_ref[...]) + tower_small_ref[1:2, :LANES]

    cotangent = cotangent_ref[...]
    g_tower_out_ref[...] += mm_tn(tower_active, cotangent)
    g_tower_small_ref[1:2, :LANES] += column_sum(cotangent.astype(F32))
    tower_slope = tower_gate + tower_silu * (1.0 - tower_gate)
    tower_grad = (mm_nt(cotangent, tower_out_ref[...]) * tower_slope).astype(BF16)
    g_tower_small_ref[0:1, :] += column_sum(tower_grad.astype(F32))
    combined_grads = []
    for task in range(2):
        part = tower_grad[:, task * TOWER1 : (task + 1) * TOWER1]
        g_tower_in_ref[task] += mm_tn(combined[task], part)
        combined_grads.append(mm_nt(part, tower_in_ref[task]))
    prob_grads = into_lane(
        [
            row_sum(combined_grads[task] * outputs[member])
            for task in range(2)
            for member in MEMBERS_TWO[task]
        ]
    )
    logit_grad = group_softmax_back(probs, prob_grads, GROUPS_TWO)
    logit_parts = [
        jnp.where(lane < 4, logit_grad, 0.0).astype(BF16),
        jnp.where((lane >= 4) & (lane < 8), logit_grad, 0.0).astype(BF16),
    ]
    g_gate_ref[...] += mm_tn(inputs[0], logit_parts[0]) + mm_tn(inputs[1], logit_parts[1])
    input_grads = [mm_nt(logit_parts[task], gate_ref[...]) for task in range(2)] + [None]
    for e in range(6):
        out_grad = None
        for task in range(2):
            if e in MEMBERS_TWO[task]:
                column = 4 * task + MEMBERS_TWO[task].index(e)
                term = probs[:, column : column + 1] * combined_grads[task]
                out_grad = term if out_grad is None else out_grad + term
        g_small_ref[2, e : e + 1, :] += column_sum(out_grad * normals[e])
        g_small_ref[3, e : e + 1, :] += column_sum(out_grad)
        post_grad = norm_backward(out_grad * small_ref[2, e : e + 1, :], normals[e], scales[e])
        post_grad = post_grad.astype(BF16)
        g_out_ref[e] += mm_tn(actives[e], post_grad)
        g_small_ref[1, e : e + 1, :] += column_sum(post_grad.astype(F32))
        pre_grad = (mm_nt(post_grad, w_out_ref[e]) * slopes[e].astype(F32)).astype(BF16)
        g_in_ref[e] += mm_tn(inputs[e // 2], pre_grad)
        g_small_ref[0, e : e + 1, :] += column_sum(pre_grad.astype(F32))
        term = mm_nt(pre_grad, w_in_ref[e])
        input_grads[e // 2] = term if input_grads[e // 2] is None else input_grads[e // 2] + term
    for index in range(3):
        mixed_grad_ref[index] = input_grads[index]

    @pl.when(pl.program_id(0) == pl.num_programs(0) - 1)
    def _():
        for e in range(6):
            put_wide_rows(flat_ref, where_row["expert_in"] + e * 2 * H, H, g_in_ref[e])
            put_wide_rows(flat_ref, where_row["expert_out"] + e * 2 * H, H, g_out_ref[e])
        for index, name in enumerate(
            ("expert_in_bias", "expert_out_bias", "norm_gain", "norm_bias")
        ):
            put_wide_rows(flat_ref, where_row[name], 6, g_small_ref[index, :6, :])
        gate_rows = H * 4 // LANES
        shift_a = lax.broadcasted_iota(jnp.int32, (LANES, LANES), 0)
        shift_b = lax.broadcasted_iota(jnp.int32, (LANES, LANES), 1)
        shift = ((shift_a == shift_b + 4) & (shift_b < 4)).astype(F32).astype(BF16)
        table = jnp.where(lane_h < 8, g_gate_ref[...], 0.0).astype(BF16)
        tables = [
            jnp.where(lane_h < 4, table.astype(F32), 0.0).astype(BF16),
            mm(table, shift).astype(BF16),
        ]
        for task in range(2):
            flat_ref[pl.ds(where_row["gate"] + task * gate_rows, gate_rows), :] = rows_from_table(
                tables[task], gate_rows, 4
            )
            flat_ref[pl.ds(where_row["tower_in"] + task * H, H), :] = g_tower_in_ref[task]
            spot = task * TOWER1
            flat_ref[pl.ds(where_row["tower_out"] + task * TOWER1 // 2, TOWER1 // 2), :] = (
                jnp.concatenate(
                    [
                        g_tower_out_ref[pl.ds(spot + half, TOWER1 // 2, stride=2), :][
                            :, task * TOWER2 : (task + 1) * TOWER2
                        ]
                        for half in range(2)
                    ],
                    axis=1,
                )
            )
            flat_ref[pl.ds(where_row["tower_in_bias"] + task, 1), :] = g_tower_small_ref[
                0:1, task * TOWER1 : (task + 1) * TOWER1
            ]
        flat_ref[pl.ds(where_row["tower_out_bias"], 1), :] = g_tower_small_ref[1:2, :LANES]
        if used_rows < count * rows:
            flat_ref[pl.ds(used_rows, count * rows - used_rows), :] = jnp.zeros(
                (count * rows - used_rows, LANES), F32
            )
        collect_pieces(me_ref[0], count, rows, flat_ref, grads_ref)


def level_one_backward(
    count,
    rows,
    me_ref,
    mixed_grad_ref,
    masked_ref,
    level_ref,
    active_ref,
    slope_ref,
    normal_ref,
    scale_ref,
    probs_ref,
    w_in_ref,
    w_out_ref,
    small_ref,
    gate_ref,
    entry_ref,
    level_grad_ref,
    sums_ref,
    grads_ref,
    flat_ref,
    g_in_ref,
    g_out_ref,
    g_small_ref,
    g_gate_ref,
    g_sum_ref,
):
    width = masked_ref.shape[1]
    lanes = width // LANES
    where_row, used_rows = first_layout(width)

    @pl.when(pl.program_id(0) == 0)
    def _():
        for ref in (g_in_ref, g_out_ref, g_small_ref, g_gate_ref, g_sum_ref):
            ref[...] = jnp.zeros(ref.shape, F32)

    level = level_ref[...]
    probs = probs_ref[...]
    mixed_grads = [mixed_grad_ref[index] for index in range(3)]
    columns = [None] * 14
    for e in range(6):
        output = normal_ref[e].astype(F32) * small_ref[2, e : e + 1, :] + small_ref[3, e : e + 1, :]
        for index, (low, _) in enumerate(GROUPS_ONE):
            if e in MEMBERS_ONE[index]:
                columns[low + MEMBERS_ONE[index].index(e)] = row_sum(mixed_grads[index] * output)
    logit_grad = group_softmax_back(probs, into_lane(columns), GROUPS_ONE).astype(BF16)
    g_gate_ref[...] += mm_tn(level, logit_grad)
    level_grad = mm_nt(logit_grad, gate_ref[...])
    for e in range(6):
        normal = normal_ref[e].astype(F32)
        out_grad = None
        for index, (low, _) in enumerate(GROUPS_ONE):
            if e in MEMBERS_ONE[index]:
                column = low + MEMBERS_ONE[index].index(e)
                term = probs[:, column : column + 1] * mixed_grads[index]
                out_grad = term if out_grad is None else out_grad + term
        g_small_ref[2, e : e + 1, :] += column_sum(out_grad * normal)
        g_small_ref[3, e : e + 1, :] += column_sum(out_grad)
        post_grad = norm_backward(
            out_grad * small_ref[2, e : e + 1, :], normal, scale_ref[:, e : e + 1]
        ).astype(BF16)
        g_out_ref[e] += mm_tn(active_ref[e], post_grad)
        g_small_ref[1, e : e + 1, :] += column_sum(post_grad.astype(F32))
        pre_grad = (mm_nt(post_grad, w_out_ref[e]) * slope_ref[e].astype(F32)).astype(BF16)
        g_in_ref[e] += mm_tn(level, pre_grad)
        g_small_ref[0, e : e + 1, :] += column_sum(pre_grad.astype(F32))
        level_grad = level_grad + mm_nt(pre_grad, w_in_ref[e])
    level_grad_ref[...] = level_grad
    normed = (masked_ref[...].astype(F32) - entry_ref[0:1, :]) * entry_ref[1:2, :]
    g_sum_ref[0:1, :] += column_sum(level_grad * normed)
    g_sum_ref[1:2, :] += column_sum(level_grad)

    @pl.when(pl.program_id(0) == pl.num_programs(0) - 1)
    def _():
        for e in range(6):
            put_wide_rows(flat_ref, where_row["expert_in"] + e * 2 * width, width, g_in_ref[e])
            put_wide_rows(flat_ref, where_row["expert_out"] + e * 2 * H, H, g_out_ref[e])
        for index, name in enumerate(
            ("expert_in_bias", "expert_out_bias", "norm_gain", "norm_bias")
        ):
            put_wide_rows(flat_ref, where_row[name], 6, g_small_ref[index, :6, :])
        gate_rows = 14 * width // LANES
        flat_ref[pl.ds(where_row["gate"], gate_rows), :] = rows_from_table(
            g_gate_ref[...].astype(BF16), gate_rows, 14
        )
        for index in range(lanes):
            part = slice(index * LANES, (index + 1) * LANES)
            sums_ref[index : index + 1, :] = g_sum_ref[0:1, part]
            sums_ref[lanes + index : lanes + index + 1, :] = g_sum_ref[1:2, part]
        flat_ref[0 : 2 * lanes, :] = jnp.zeros((2 * lanes, LANES), F32)
        if used_rows < count * rows:
            flat_ref[pl.ds(used_rows, count * rows - used_rows), :] = jnp.zeros(
                (count * rows - used_rows, LANES), F32
            )
        collect_pieces(me_ref[0], count, rows, flat_ref, grads_ref)


def input_kernel(total_rows, level_grad_ref, masked_ref, presence_ref, entry_ref, sums_ref, out_ref):
    width = masked_ref.shape[1]
    lanes = width // LANES
    mask = spread_presence(presence_ref[...], width)
    inv_scale = entry_ref[1:2, :]
    gain = entry_ref[2:3, :]
    normed = (masked_ref[...].astype(F32) - entry_ref[0:1, :]) * inv_scale
    cross = from_lanes(sums_ref[0:lanes, :]) * (1.0 / total_rows)
    plain = from_lanes(sums_ref[lanes : 2 * lanes, :]) * (1.0 / total_rows)
    out_ref[...] = mask * ((inv_scale * gain) * (level_grad_ref[...] - plain - normed * cross))


def xor_permute(value, axis, bit):
    size = lax.axis_size(axis)
    return lax.ppermute(value, axis, [(index, index ^ bit) for index in range(size)])


def is_power(value):
    return value & (value - 1) == 0


def butterfly(value, merge):
    for axis in AXES:
        bit = 1
        while bit < lax.axis_size(axis):
            value = merge(value, xor_permute(value, axis, bit), axis, bit)
            bit *= 2
    return value


def hypercube_ok():
    wide, narrow = lax.axis_size("wide"), lax.axis_size("narrow")
    return wide == 8 and narrow == 4


def gather_pieces(local, rows):
    padded = up(rows, 16)
    block = jnp.pad(local.reshape(rows, LANES), ((0, padded - rows), (0, 0)))
    near = [block] + [xor_permute(block, "narrow", k) for k in (1, 2, 3)]
    first, second = jnp.stack(near[:2]), jnp.stack(near[2:])
    first_y, second_x = xor_permute(first, "wide", 4), xor_permute(second, "wide", 2)
    first_x, second_y = xor_permute(first, "wide", 2), xor_permute(second, "wide", 4)
    first_xy, second_xy = xor_permute(first_y, "wide", 2), xor_permute(second_x, "wide", 4)
    own = [first, second, first_x, second_x, first_y, second_y, first_xy, second_xy]
    other = [xor_permute(piece, "wide", 1) for piece in own]
    pieces = []
    for index in range(4):
        pieces += [own[2 * index], own[2 * index + 1], other[2 * index], other[2 * index + 1]]
    return pieces


def scatter_pieces(value):
    split = value.reshape(2, 2, 2, 4, value.shape[1], LANES)
    keep = split[:, :, 0].astype(F32) + xor_permute(split[:, :, 1], "wide", 1).astype(F32)
    low = keep.astype(BF16)
    first = keep[0, :, :2] + xor_permute(low[1, :, :2], "wide", 4).astype(F32)
    second = keep[:, 0, 2:] + xor_permute(low[:, 1, 2:], "wide", 2).astype(F32)
    first = first[0] + xor_permute(first[1].astype(BF16), "wide", 2).astype(F32)
    second = second[0] + xor_permute(second[1].astype(BF16), "wide", 4).astype(F32)
    total = first[0]
    total = total + xor_permute(first[1].astype(BF16), "narrow", 1).astype(F32)
    total = total + xor_permute(second[0].astype(BF16), "narrow", 2).astype(F32)
    total = total + xor_permute(second[1].astype(BF16), "narrow", 3).astype(F32)
    return total


def gather_flat(local):
    whole = lax.all_gather(local, AXES, axis=0, tiled=True)
    return whole.reshape(1, whole.shape[0] // LANES, LANES)


def per_device(features, presence, first_params, second_params, cotangent):
    rows, width = features.shape
    lanes = width // LANES
    devices_all = lax.axis_size(AXES)
    total_rows = rows * devices_all
    cube = hypercube_ok()
    tile = math.gcd(rows, 256)
    steps = rows // tile
    me = lax.axis_index(AXES).astype(jnp.int32).reshape(1)
    flat_rows = [first_params.shape[0] // LANES, second_params.shape[0] // LANES]
    if cube:
        count, chunks = devices_all, flat_rows
        pieces_one = gather_pieces(first_params, flat_rows[0])
        pieces_two = gather_pieces(second_params, flat_rows[1])
    else:
        count, chunks = 1, [flat_rows[0] * devices_all, flat_rows[1] * devices_all]
        pieces_one, pieces_two = [gather_flat(first_params)], [gather_flat(second_params)]

    masked, stats = pl.pallas_call(
        stats_kernel,
        out_shape=(
            jax.ShapeDtypeStruct((rows, width), BF16),
            jax.ShapeDtypeStruct((2 * lanes, LANES), F32),
        ),
        compiler_params=pltpu.CompilerParams(vmem_limit_bytes=VMEM_LIMIT),
    )(features, presence)

    members = [rows]

    def merge(mine, theirs, axis, bit):
        delta = mine[:lanes] - theirs[:lanes]
        mean = 0.5 * (mine[:lanes] + theirs[:lanes])
        moment = mine[lanes:] + theirs[lanes:] + delta * delta * (0.5 * members[0])
        members[0] *= 2
        return jnp.concatenate([mean, moment])

    stats = butterfly(stats, merge)

    shape = jax.ShapeDtypeStruct
    saved = run_kernel(
        functools.partial(
            level_one_forward, count, chunks[0], float(total_rows), len(pieces_one)
        ),
        steps,
        [scalar_spec(), tile_spec((rows, width), tile, 0), full_spec()]
        + [full_spec()] * len(pieces_one),
        [
            tile_spec((rows, width), tile, 0),
            tile_spec((6, rows, H), tile, 1),
            tile_spec((6, rows, H), tile, 1),
            tile_spec((6, rows, H), tile, 1),
            tile_spec((rows, LANES), tile, 0),
            tile_spec((rows, LANES), tile, 0),
            tile_spec((3, rows, H), tile, 1),
            full_spec(),
            full_spec(),
            full_spec(),
            full_spec(),
            full_spec(),
        ],
        [
            shape((rows, width), BF16),
            shape((6, rows, H), BF16),
            shape((6, rows, H), BF16),
            shape((6, rows, H), BF16),
            shape((rows, LANES), F32),
            shape((rows, LANES), F32),
            shape((3, rows, H), BF16),
            shape((6, width, H), BF16),
            shape((6, H, H), BF16),
            shape((4, 8, H), F32),
            shape((width, LANES), BF16),
            shape((8, width), F32),
        ],
        [pltpu.VMEM((count * chunks[0], LANES), F32)],
        [me, masked, stats] + pieces_one,
        rows * 6 * (width + H) * H * 2,
        16 * 2**20,
    )
    level, active, slope, normal, scale, probs, mixed, w_in, w_out, small, gate, entry = saved

    towers, mixed_grad, grads_two = run_kernel(
        functools.partial(level_two, count, chunks[1], len(pieces_two)),
        steps,
        [scalar_spec(), tile_spec((3, rows, H), tile, 1), tile_spec((rows, LANES), tile, 0)]
        + [full_spec()] * len(pieces_two),
        [
            tile_spec((rows, LANES), tile, 0),
            tile_spec((3, rows, H), tile, 1),
            full_spec(),
        ],
        [
            shape((rows, LANES), F32),
            shape((3, rows, H), F32),
            shape((count, up(chunks[1], 16), LANES), BF16),
        ],
        [
            pltpu.VMEM((count * chunks[1], LANES), F32),
            pltpu.VMEM((6, H, H), BF16),
            pltpu.VMEM((6, H, H), BF16),
            pltpu.VMEM((4, 8, H), F32),
            pltpu.VMEM((H, LANES), BF16),
            pltpu.VMEM((2, H, TOWER1), BF16),
            pltpu.VMEM((2 * TOWER1, LANES), BF16),
            pltpu.VMEM((2 * TOWER1, LANES), F32),
            pltpu.VMEM((8, 2 * TOWER1), F32),
            pltpu.VMEM((6, H, H), F32),
            pltpu.VMEM((6, H, H), F32),
            pltpu.VMEM((4, 8, H), F32),
            pltpu.VMEM((H, LANES), F32),
            pltpu.VMEM((2, H, TOWER1), F32),
            pltpu.VMEM((2 * TOWER1, LANES), F32),
            pltpu.VMEM((8, 2 * TOWER1), F32),
        ],
        [me, mixed, cotangent] + pieces_two,
        rows * 6 * 2 * H * H * 2 * 3,
        8 * 2**20,
    )
    if cube:
        second_grad = scatter_pieces(grads_two)[: flat_rows[1]].reshape(-1)
    else:
        second_grad = lax.psum_scatter(
            grads_two.reshape(-1)[: flat_rows[1] * devices_all * LANES].astype(F32),
            AXES,
            scatter_dimension=0,
            tiled=True,
        )

    level_grad, sums, grads_one = run_kernel(
        functools.partial(level_one_backward, count, chunks[0]),
        steps,
        [
            scalar_spec(),
            tile_spec((3, rows, H), tile, 1),
            tile_spec((rows, width), tile, 0),
            tile_spec((rows, width), tile, 0),
            tile_spec((6, rows, H), tile, 1),
            tile_spec((6, rows, H), tile, 1),
            tile_spec((6, rows, H), tile, 1),
            tile_spec((rows, LANES), tile, 0),
            tile_spec((rows, LANES), tile, 0),
        ]
        + [full_spec()] * 5,
        [tile_spec((rows, width), tile, 0), full_spec(), full_spec()],
        [
            shape((rows, width), F32),
            shape((2 * lanes, LANES), F32),
            shape((count, up(chunks[0], 16), LANES), BF16),
        ],
        [
            pltpu.VMEM((count * chunks[0], LANES), F32),
            pltpu.VMEM((6, width, H), F32),
            pltpu.VMEM((6, H, H), F32),
            pltpu.VMEM((4, 8, H), F32),
            pltpu.VMEM((width, LANES), F32),
            pltpu.VMEM((8, width), F32),
        ],
        [
            me,
            mixed_grad,
            masked,
            level,
            active,
            slope,
            normal,
            scale,
            probs,
            w_in,
            w_out,
            small,
            gate,
            entry,
        ],
        rows * 6 * (width + H) * H * 2 * 2,
        20 * 2**20,
    )
    sums = butterfly(sums, lambda mine, theirs, axis, bit: mine + theirs)
    if cube:
        first_grad = scatter_pieces(grads_one)[: flat_rows[0]].reshape(-1)
    else:
        first_grad = lax.psum_scatter(
            grads_one.reshape(-1)[: flat_rows[0] * devices_all * LANES].astype(F32),
            AXES,
            scatter_dimension=0,
            tiled=True,
        )
    start = me[0] * first_params.shape[0]
    position = start + jnp.arange(2 * width)
    head = jnp.where(position < 2 * width, sums.reshape(-1), first_grad[: 2 * width])
    first_grad = jnp.concatenate([head, first_grad[2 * width :]])

    input_grad = run_kernel(
        functools.partial(input_kernel, float(total_rows)),
        steps,
        [
            tile_spec((rows, width), tile, 0),
            tile_spec((rows, width), tile, 0),
            tile_spec((rows, presence.shape[1]), tile, 0),
            full_spec(),
            full_spec(),
        ],
        tile_spec((rows, width), tile, 0),
        shape((rows, width), F32),
        [],
        [level_grad, masked, presence, entry, sums],
        rows * width * 10,
        6 * 2**20,
    )
    return (towers, input_grad, first_grad, second_grad)


def solution(mesh):
    placed = (
        P(AXES, None),
        P(AXES, None),
        P(AXES),
        P(AXES),
        P(AXES, None),
    )
    return jax.shard_map(
        per_device,
        mesh=mesh,
        in_specs=placed,
        out_specs=(P(AXES, None), P(AXES, None), P(AXES), P(AXES)),
        check_vma=False,
    )
```

```python
import functools
import math

import jax
import jax.numpy as jnp
from jax import lax
from jax.experimental import pallas as pl
from jax.experimental.pallas import tpu as pltpu
from jax.sharding import PartitionSpec as P

H = 256
TOWER1 = 128
TOWER2 = 64
LANES = 128
EPSILON = 1e-05
AXES = ("wide", "narrow")
F32 = jnp.float32
BF16 = jnp.bfloat16
GROUPS_ONE = ((0, 4), (4, 8), (8, 14))
MEMBERS_ONE = ((0, 1, 4, 5), (2, 3, 4, 5), (0, 1, 2, 3, 4, 5))
GROUPS_TWO = ((0, 4), (4, 8))
MEMBERS_TWO = ((0, 1, 4, 5), (2, 3, 4, 5))


def up(value, step):
    return -(-value // step) * step


def mm(left, right):
    return jnp.dot(left, right, preferred_element_type=F32)


def mm_nt(left, right):
    return lax.dot_general(left, right, (((1,), (1,)), ((), ())), preferred_element_type=F32)


def mm_tn(left, right):
    return lax.dot_general(left, right, (((0,), (0,)), ((), ())), preferred_element_type=F32)


def sigmoid(values):
    return 0.5 * jnp.tanh(0.5 * values) + 0.5


def group_softmax(logits, groups):
    lane = lax.broadcasted_iota(jnp.int32, logits.shape, 1)
    spread = jnp.zeros_like(logits)
    for low, high in groups:
        inside = (lane >= low) & (lane < high)
        peak = jnp.max(jnp.where(inside, logits, -jnp.inf), axis=1, keepdims=True)
        spread = jnp.where(inside, logits - peak, spread)
    raw = jnp.exp(spread)
    result = jnp.zeros_like(logits)
    for low, high in groups:
        inside = (lane >= low) & (lane < high)
        total = jnp.sum(jnp.where(inside, raw, 0.0), axis=1, keepdims=True)
        result = jnp.where(inside, raw / total, result)
    return result


def group_softmax_back(probs, grads, groups):
    lane = lax.broadcasted_iota(jnp.int32, probs.shape, 1)
    product = probs * grads
    result = jnp.zeros_like(probs)
    for low, high in groups:
        inside = (lane >= low) & (lane < high)
        total = jnp.sum(jnp.where(inside, product, 0.0), axis=1, keepdims=True)
        result = jnp.where(inside, product - probs * total, result)
    return result


def into_lane(columns):
    rows = columns[0].shape[0]
    lane = lax.broadcasted_iota(jnp.int32, (rows, LANES), 1)
    result = jnp.zeros((rows, LANES), F32)
    for position, column in enumerate(columns):
        result = jnp.where(lane == position, column, result)
    return result


def mix_parts(weights, low, members, outputs):
    running = None
    for position, member in enumerate(members):
        term = column_block(weights, low + position) * outputs[member]
        running = term if running is None else running + term
    return running


def row_sum(values):
    return jnp.sum(values, axis=1, keepdims=True)


def column_sum(values):
    return jnp.sum(values, axis=0, keepdims=True)


def norm_forward(post):
    centred = post - row_sum(post) * (1.0 / H)
    scale = lax.rsqrt(row_sum(centred * centred) * (1.0 / H) + EPSILON)
    return centred * scale, scale


def twice(values):
    return jnp.concatenate([values, values], axis=1)


def norm_backward(scaled, normal, scale, means):
    both = jnp.concatenate([scaled.astype(BF16), (scaled * normal).astype(BF16)], axis=1)
    mean = mm(both, means)
    return twice(scale) * (
        scaled - twice(mean[:, :LANES]) - normal * twice(mean[:, LANES:])
    )


def make_means():
    row = lax.broadcasted_iota(jnp.int32, (2 * H, 2 * LANES), 0)
    lane = lax.broadcasted_iota(jnp.int32, (2 * H, 2 * LANES), 1)
    return jnp.where((row < H) == (lane < LANES), 1.0 / H, 0.0).astype(BF16)


def make_spread(columns):
    row = lax.broadcasted_iota(jnp.int32, (2 * LANES, columns * LANES), 0)
    lane = lax.broadcasted_iota(jnp.int32, (2 * LANES, columns * LANES), 1)
    return jnp.where((row & (LANES - 1)) == (lane >> 7), 1.0, 0.0).astype(BF16)


def spread_columns(values, spread):
    high = values.astype(BF16)
    low = (values - high.astype(F32)).astype(BF16)
    return mm(jnp.concatenate([high, low], axis=1), spread)


def column_block(spread, column):
    return twice(spread[:, column * LANES : (column + 1) * LANES])


def first_layout(width):
    names = (
        ("in_gain", width),
        ("in_bias", width),
        ("expert_in", 6 * width * H),
        ("expert_in_bias", 6 * H),
        ("expert_out", 6 * H * H),
        ("expert_out_bias", 6 * H),
        ("norm_gain", 6 * H),
        ("norm_bias", 6 * H),
        ("gate", 14 * width),
    )
    return place_names(names)


def second_layout():
    names = (
        ("expert_in", 6 * H * H),
        ("expert_in_bias", 6 * H),
        ("expert_out", 6 * H * H),
        ("expert_out_bias", 6 * H),
        ("norm_gain", 6 * H),
        ("norm_bias", 6 * H),
        ("gate", 2 * H * 4),
        ("tower_in", 2 * H * TOWER1),
        ("tower_in_bias", 2 * TOWER1),
        ("tower_out", 2 * TOWER1 * TOWER2),
        ("tower_out_bias", 2 * TOWER2),
    )
    return place_names(names)


def place_names(names):
    rows = {}
    offset = 0
    for name, amount in names:
        rows[name] = offset // LANES
        offset += amount
    return rows, offset // LANES


def spread_pieces(me, rows, piece_refs, flat_ref, extra_ref=None):
    slot = 0
    for ref in piece_refs:
        for index in range(ref.shape[0]):
            owner = lax.bitwise_xor(me, jnp.int32(slot))
            block = ref[index].astype(F32)
            flat_ref[pl.ds(owner * rows, rows), :] = block[:rows]
            if extra_ref is not None:
                extra_ref[slot] = block[rows : rows + extra_ref.shape[1]]
            slot += 1


def wide_rows(flat_ref, row, amount):
    return jnp.concatenate(
        [flat_ref[pl.ds(row, amount, stride=2), :], flat_ref[pl.ds(row + 1, amount, stride=2), :]],
        axis=1,
    )


def put_wide_rows(flat_ref, row, amount, value):
    flat_ref[pl.ds(row, amount, stride=2), :] = value[:, :LANES]
    flat_ref[pl.ds(row + 1, amount, stride=2), :] = value[:, LANES:]


def collect_pieces(me, count, rows, flat_ref, out_refs):
    for slot in range(count):
        owner = lax.bitwise_xor(me, jnp.int32(slot))
        value = flat_ref[pl.ds(owner * rows, rows), :].astype(BF16)
        if len(out_refs) == 1:
            out_refs[0][slot, :rows, :] = value
        else:
            part, place = slot // 4 % 2, slot // 8 * 4 + slot % 4
            out_refs[part][place, :rows, :] = value


def roll_rows(value, columns, sign):
    item = lax.broadcasted_iota(jnp.int32, value.shape, 0)
    bit = 1
    while columns * bit % LANES:
        moved = pltpu.roll(value, sign * columns * bit % LANES, 1)
        value = jnp.where((item & bit) != 0, moved, value)
        bit *= 2
    return value


def table_places(width, columns, rows):
    item = lax.broadcasted_iota(jnp.int32, (width, rows), 0)
    index = lax.broadcasted_iota(jnp.int32, (width, rows), 1)
    first = (index == ((item * columns) >> 7)).astype(F32).astype(BF16)
    last = (index == ((item * columns + columns - 1) >> 7)).astype(F32).astype(BF16)
    item = lax.broadcasted_iota(jnp.int32, (width, LANES), 0)
    lane = lax.broadcasted_iota(jnp.int32, (width, LANES), 1)
    return first, last, lane >= ((item * columns) & (LANES - 1)), lane < columns


def table_from_rows(flat, width, columns):
    first, last, late, used = table_places(width, columns, flat.shape[0])
    chosen = jnp.where(late, mm(first, flat), mm(last, flat))
    return jnp.where(used, roll_rows(chosen, columns, -1), 0.0)


def rows_from_table(table, rows, columns):
    first, last, late, _ = table_places(table.shape[0], columns, rows)
    moved = roll_rows(table, columns, 1)
    return mm_tn(first, jnp.where(late, moved, 0.0).astype(BF16)) + mm_tn(
        last, jnp.where(late, 0.0, moved).astype(BF16)
    )


def full_spec():
    return pl.BlockSpec(memory_space=pltpu.VMEM)


def scalar_spec():
    return pl.BlockSpec(memory_space=pltpu.SMEM)


def run_kernel(kernel, inputs, out_shape, scratch, limit, flops, scalar=True):
    specs = [full_spec()] * len(inputs)
    if scalar:
        specs[0] = scalar_spec()
    out_specs = jax.tree.map(lambda _: full_spec(), out_shape)
    return pl.pallas_call(
        kernel,
        in_specs=specs,
        out_specs=out_specs,
        out_shape=out_shape,
        scratch_shapes=scratch,
        compiler_params=pltpu.CompilerParams(vmem_limit_bytes=limit * 2**20),
        cost_estimate=pl.CostEstimate(flops=2**20, bytes_accessed=2**10, transcendentals=0),
    )(*inputs)


def spread_presence(presence, width):
    fields = presence.shape[0]
    field = lax.broadcasted_iota(jnp.int32, (fields, width), 0)
    column = lax.broadcasted_iota(jnp.int32, (fields, width), 1)
    pick = (column // (width // fields) == field).astype(F32).astype(BF16)
    return mm_tn(presence.astype(F32).astype(BF16), pick)


def split_three(values):
    parts = []
    for _ in range(3):
        part = values.astype(BF16).astype(F32)
        parts.append(part)
        values = values - part
    return parts


def stats_kernel(
    me_ref, features_ref, presence_ref, params_ref, second_ref, masked_ref, block_ref, block_two_ref
):
    del me_ref
    rows, width = features_ref.shape
    mask = spread_presence(presence_ref[...], width)
    masked = features_ref[...].astype(F32) * mask
    masked_ref[...] = masked.astype(BF16)
    mean = column_sum(masked) * (1.0 / rows)
    spread = masked - mean
    moment = column_sum(spread * spread)
    lines = [params_ref[...].astype(F32)]
    for value in (mean, moment):
        for part in split_three(value):
            for index in range(width // LANES):
                lines.append(part[:, index * LANES : (index + 1) * LANES])
    used = params_ref.shape[0] + 6 * (width // LANES)
    lines.append(jnp.zeros((block_ref.shape[0] - used, LANES), F32))
    block_ref[...] = jnp.concatenate(lines, axis=0).astype(BF16)
    second = second_ref[...].astype(F32)
    rest = jnp.zeros((block_two_ref.shape[0] - second.shape[0], LANES), F32)
    block_two_ref[...] = jnp.concatenate([second, rest], axis=0).astype(BF16)


def from_lanes(block):
    return jnp.concatenate([block[index : index + 1, :] for index in range(block.shape[0])], axis=1)


def tiles(tile):
    return lambda ref_rows, body: lax.fori_loop(
        0, ref_rows // tile, lambda step, carry: body(pl.multiple_of(step * tile, tile), carry), 0
    )


def spot(e):
    return slice(e * H, (e + 1) * H)


def level_one_forward(
    rows,
    tile,
    n_pieces,
    me_ref,
    masked_ref,
    *rest,
):
    piece_refs = rest[:n_pieces]
    (
        level_ref,
        active_ref,
        slope_ref,
        normal_ref,
        scale_ref,
        probs_ref,
        mixed_ref,
        w_in_ref,
        w_out_ref,
        small_ref,
        gate_ref,
        entry_ref,
        flat_ref,
        extra_ref,
        output_ref,
        wide_ref,
        spread_ref,
    ) = rest[n_pieces:]
    width = masked_ref.shape[1]
    where_row, _ = first_layout(width)

    spread_pieces(me_ref[0], rows, piece_refs, flat_ref, extra_ref)
    spread_ref[...] = make_spread(14)
    for e in range(6):
        w_in_ref[:, spot(e)] = wide_rows(
            flat_ref, where_row["expert_in"] + e * 2 * width, width
        ).astype(BF16)
        w_out_ref[e] = wide_rows(flat_ref, where_row["expert_out"] + e * 2 * H, H).astype(BF16)
    for index, name in enumerate(("expert_in_bias", "expert_out_bias", "norm_gain", "norm_bias")):
        small_ref[index, :6, :] = wide_rows(flat_ref, where_row[name], 6)
    gate_flat = flat_ref[pl.ds(where_row["gate"], 14 * width // LANES), :].astype(BF16)
    gate_ref[...] = table_from_rows(gate_flat, width, 14).astype(BF16)
    lanes = width // LANES
    events = masked_ref.shape[0]
    count = extra_ref.shape[0]
    means = extra_ref[:, 0:lanes, :]
    for part in (1, 2):
        means = means + extra_ref[:, part * lanes : (part + 1) * lanes, :]
    mean = jnp.sum(means, axis=0) * (1.0 / count)
    away = jnp.sum(jnp.square(means - mean[None]), axis=0) * events
    for part in (3, 4, 5):
        away = away + jnp.sum(extra_ref[:, part * lanes : (part + 1) * lanes, :], axis=0)
    entry_ref[0:1, :] = from_lanes(mean)
    entry_ref[1:2, :] = from_lanes(lax.rsqrt(away * (1.0 / (events * count)) + EPSILON))
    entry_ref[2:3, :] = from_lanes(flat_ref[0:lanes, :])
    entry_ref[3:4, :] = from_lanes(flat_ref[lanes : 2 * lanes, :])

    def body(start, carry):
        now = pl.ds(start, tile)
        normed = (masked_ref[now, :].astype(F32) - entry_ref[0:1, :]) * entry_ref[1:2, :]
        level_ref[now, :] = (normed * entry_ref[2:3, :] + entry_ref[3:4, :]).astype(BF16)
        probs_ref[now, :] = group_softmax(mm(level_ref[now, :], gate_ref[...]), GROUPS_ONE)
        for e in range(6):
            pre = mm(level_ref[now, :], w_in_ref[:, spot(e)]) + small_ref[0, e : e + 1, :]
            gate = sigmoid(pre)
            silu = pre * gate
            active_ref[e, now, :] = silu.astype(BF16)
            slope_ref[e, now, :] = (gate + silu * (1.0 - gate)).astype(BF16)
        for e in range(6):
            post = mm(active_ref[e, now, :], w_out_ref[e]) + small_ref[1, e : e + 1, :]
            normal, scale = norm_forward(post)
            normal_ref[e, now, :] = normal.astype(BF16)
            scale_ref[e, now, :] = jnp.broadcast_to(scale, (tile, LANES))
            output_ref[e] = normal * small_ref[2, e : e + 1, :] + small_ref[3, e : e + 1, :]
        wide_ref[...] = spread_columns(probs_ref[now, :], spread_ref[...])
        for index, (low, _) in enumerate(GROUPS_ONE):
            mixed_ref[index, now, :] = mix_parts(
                wide_ref, low, MEMBERS_ONE[index], output_ref
            ).astype(BF16)
        return carry

    tiles(tile)(masked_ref.shape[0], body)


def level_two(count, rows, tile, n_pieces, n_outs, me_ref, mixed_ref, cotangent_ref, *rest):
    piece_refs = rest[:n_pieces]
    grads_refs = rest[n_pieces + 2 : n_pieces + 2 + n_outs]
    towers_ref, mixed_grad_ref = rest[n_pieces : n_pieces + 2]
    (
        flat_ref,
        w_in_ref,
        w_out_ref,
        small_ref,
        gate_ref,
        tower_in_ref,
        tower_out_ref,
        tower_tmp_ref,
        tower_small_ref,
        g_small_ref,
        g_tower_out_ref,
        g_tower_small_ref,
        active_ref,
        slope_ref,
        normal_ref,
        scale_ref,
        output_ref,
        combined_ref,
        combined_grad_ref,
        tower_active_ref,
        tower_grad_ref,
        logit_ref,
        post_grad_ref,
        pre_grad_ref,
        wide_ref,
        spread_ref,
        means_ref,
    ) = rest[n_pieces + 2 + n_outs :]
    where_row, used_rows = second_layout()
    all_rows = mixed_ref.shape[1]

    spread_pieces(me_ref[0], rows, piece_refs, flat_ref)
    spread_ref[...] = make_spread(8)
    means_ref[...] = make_means()
    for e in range(6):
        w_in_ref[:, spot(e)] = wide_rows(flat_ref, where_row["expert_in"] + e * 2 * H, H).astype(
            BF16
        )
        w_out_ref[e] = wide_rows(flat_ref, where_row["expert_out"] + e * 2 * H, H).astype(BF16)
    for index, name in enumerate(("expert_in_bias", "expert_out_bias", "norm_gain", "norm_bias")):
        small_ref[index, :6, :] = wide_rows(flat_ref, where_row[name], 6)
    gate_rows = H * 4 // LANES
    shift_a = lax.broadcasted_iota(jnp.int32, (LANES, LANES), 0)
    shift_b = lax.broadcasted_iota(jnp.int32, (LANES, LANES), 1)
    shift = ((shift_a + 4 == shift_b) & (shift_a < 4)).astype(F32).astype(BF16)
    tables = []
    for task in range(2):
        piece = flat_ref[pl.ds(where_row["gate"] + task * gate_rows, gate_rows), :].astype(BF16)
        tables.append(table_from_rows(piece, H, 4).astype(BF16))
    gate_ref[...] = (tables[0].astype(F32) + mm(tables[1], shift)).astype(BF16)
    zero = jnp.zeros((TOWER1 // 2, TOWER2), F32)
    for task in range(2):
        tower_in_ref[task] = flat_ref[pl.ds(where_row["tower_in"] + task * H, H), :].astype(BF16)
        packed = flat_ref[pl.ds(where_row["tower_out"] + task * TOWER1 // 2, TOWER1 // 2), :]
        for half in range(2):
            pair = [packed[:, half * TOWER2 : (half + 1) * TOWER2], zero]
            if task == 1:
                pair.reverse()
            tower_tmp_ref[pl.ds(task * TOWER1 + half, TOWER1 // 2, stride=2), :] = jnp.concatenate(
                pair, axis=1
            )
    tower_out_ref[...] = tower_tmp_ref[...].astype(BF16)
    tower_small_ref[0:1, :] = from_lanes(flat_ref[pl.ds(where_row["tower_in_bias"], 2), :])
    tower_small_ref[1:2, :LANES] = flat_ref[pl.ds(where_row["tower_out_bias"], 1), :]
    g_small_ref[...] = jnp.zeros(g_small_ref.shape, F32)
    g_tower_small_ref[...] = jnp.zeros(g_tower_small_ref.shape, F32)

    def body(start, carry):
        now = pl.ds(start, tile)
        lane = lax.broadcasted_iota(jnp.int32, (tile, LANES), 1)
        for e in range(6):
            pre = mm(mixed_ref[e // 2, now, :], w_in_ref[:, spot(e)]) + small_ref[0, e : e + 1, :]
            gate = sigmoid(pre)
            silu = pre * gate
            active_ref[e, now, :] = silu.astype(BF16)
            slope_ref[:, spot(e)] = gate + silu * (1.0 - gate)
        for e in range(6):
            post = mm(active_ref[e, now, :], w_out_ref[e]) + small_ref[1, e : e + 1, :]
            normal, scale = norm_forward(post)
            normal_ref[e] = normal
            scale_ref[e] = jnp.broadcast_to(scale, (tile, LANES))
            output_ref[e] = normal * small_ref[2, e : e + 1, :] + small_ref[3, e : e + 1, :]
        logits = jnp.where(
            lane < 4, mm(mixed_ref[0, now, :], gate_ref[...]), mm(mixed_ref[1, now, :], gate_ref[...])
        )
        probs = group_softmax(logits, GROUPS_TWO)
        wide_ref[...] = spread_columns(probs, spread_ref[...])
        for task in range(2):
            combined_ref[task, now, :] = mix_parts(
                wide_ref, 4 * task, MEMBERS_TWO[task], output_ref
            ).astype(BF16)
        tower_pre = (
            jnp.concatenate(
                [mm(combined_ref[task, now, :], tower_in_ref[task]) for task in range(2)], axis=1
            )
            + tower_small_ref[0:1, :]
        )
        tower_gate = sigmoid(tower_pre)
        tower_silu = tower_pre * tower_gate
        tower_active_ref[now, :] = tower_silu.astype(BF16)
        towers_ref[now, :] = (
            mm(tower_active_ref[now, :], tower_out_ref[...]) + tower_small_ref[1:2, :LANES]
        )
        cotangent = cotangent_ref[now, :]
        g_tower_small_ref[1:2, :LANES] += column_sum(cotangent.astype(F32))
        tower_slope = tower_gate + tower_silu * (1.0 - tower_gate)
        tower_grad = (mm_nt(cotangent, tower_out_ref[...]) * tower_slope).astype(BF16)
        tower_grad_ref[now, :] = tower_grad
        g_tower_small_ref[0:1, :] += column_sum(tower_grad.astype(F32))
        for task in range(2):
            combined_grad_ref[task] = mm_nt(
                tower_grad_ref[now, task * TOWER1 : (task + 1) * TOWER1], tower_in_ref[task]
            )
        prob_grads = into_lane(
            [
                row_sum(combined_grad_ref[task] * output_ref[member])
                for task in range(2)
                for member in MEMBERS_TWO[task]
            ]
        )
        logit_grad = group_softmax_back(probs, prob_grads, GROUPS_TWO)
        logit_ref[0, now, :] = jnp.where(lane < 4, logit_grad, 0.0).astype(BF16)
        logit_ref[1, now, :] = jnp.where((lane >= 4) & (lane < 8), logit_grad, 0.0).astype(BF16)
        for e in range(6):
            out_grad = None
            for task in range(2):
                if e in MEMBERS_TWO[task]:
                    column = 4 * task + MEMBERS_TWO[task].index(e)
                    term = column_block(wide_ref, column) * combined_grad_ref[task]
                    out_grad = term if out_grad is None else out_grad + term
            normal = normal_ref[e]
            g_small_ref[2, e : e + 1, :] += column_sum(out_grad * normal)
            g_small_ref[3, e : e + 1, :] += column_sum(out_grad)
            post_grad = norm_backward(
                out_grad * small_ref[2, e : e + 1, :], normal, scale_ref[e], means_ref[...]
            )
            post_grad = post_grad.astype(BF16)
            post_grad_ref[e, now, :] = post_grad
            g_small_ref[1, e : e + 1, :] += column_sum(post_grad.astype(F32))
        for e in range(6):
            act_grad = mm_nt(post_grad_ref[e, now, :], w_out_ref[e])
            pre_grad = (act_grad * slope_ref[:, spot(e)]).astype(BF16)
            pre_grad_ref[now, spot(e)] = pre_grad
            g_small_ref[0, e : e + 1, :] += column_sum(pre_grad.astype(F32))
        for index in range(3):
            pair = slice(2 * index * H, 2 * (index + 1) * H)
            grad = mm_nt(pre_grad_ref[now, pair], w_in_ref[:, pair])
            if index < 2:
                grad = grad + mm_nt(logit_ref[index, now, :], gate_ref[...])
            mixed_grad_ref[index, now, :] = grad
        return carry

    tiles(tile)(all_rows, body)

    for e in range(6):
        put_wide_rows(
            flat_ref,
            where_row["expert_in"] + e * 2 * H,
            H,
            mm_tn(mixed_ref[e // 2], pre_grad_ref[:, spot(e)]),
        )
        put_wide_rows(
            flat_ref,
            where_row["expert_out"] + e * 2 * H,
            H,
            mm_tn(active_ref[e], post_grad_ref[e]),
        )
    for index, name in enumerate(("expert_in_bias", "expert_out_bias", "norm_gain", "norm_bias")):
        put_wide_rows(flat_ref, where_row[name], 6, g_small_ref[index, :6, :])
    back = ((shift_a == shift_b + 4) & (shift_b < 4)).astype(F32).astype(BF16)
    tables = [mm_tn(mixed_ref[task], logit_ref[task]) for task in range(2)]
    tables[1] = mm(tables[1].astype(BF16), back)
    g_tower_out_ref[...] = mm_tn(tower_active_ref[...], cotangent_ref[...])
    for task in range(2):
        flat_ref[pl.ds(where_row["gate"] + task * gate_rows, gate_rows), :] = rows_from_table(
            tables[task], gate_rows, 4
        )
        flat_ref[pl.ds(where_row["tower_in"] + task * H, H), :] = mm_tn(
            combined_ref[task], tower_grad_ref[:, task * TOWER1 : (task + 1) * TOWER1]
        )
        flat_ref[pl.ds(where_row["tower_out"] + task * TOWER1 // 2, TOWER1 // 2), :] = (
            jnp.concatenate(
                [
                    g_tower_out_ref[pl.ds(task * TOWER1 + half, TOWER1 // 2, stride=2), :][
                        :, task * TOWER2 : (task + 1) * TOWER2
                    ]
                    for half in range(2)
                ],
                axis=1,
            )
        )
        flat_ref[pl.ds(where_row["tower_in_bias"] + task, 1), :] = g_tower_small_ref[
            0:1, task * TOWER1 : (task + 1) * TOWER1
        ]
    flat_ref[pl.ds(where_row["tower_out_bias"], 1), :] = g_tower_small_ref[1:2, :LANES]
    if used_rows < count * rows:
        flat_ref[pl.ds(used_rows, count * rows - used_rows), :] = jnp.zeros(
            (count * rows - used_rows, LANES), F32
        )
    collect_pieces(me_ref[0], count, rows, flat_ref, grads_refs)


def level_one_backward(
    tile,
    begin,
    mixed_grad_ref,
    masked_ref,
    slope_ref,
    normal_ref,
    scale_ref,
    probs_ref,
    w_in_ref,
    w_out_ref,
    small_ref,
    gate_ref,
    entry_ref,
    *rest,
):
    if begin:
        before_sum_ref, before_small_ref, *rest = rest
    (
        level_grad_ref,
        g_sum_ref,
        g_small_ref,
        logit_ref,
        post_grad_ref,
        pre_grad_ref,
        wide_ref,
        spread_ref,
        means_ref,
    ) = rest
    spread_ref[...] = make_spread(14)
    means_ref[...] = make_means()
    if begin:
        g_small_ref[...] = before_small_ref[...]
        g_sum_ref[...] = before_sum_ref[...]
    else:
        g_small_ref[...] = jnp.zeros(g_small_ref.shape, F32)
        g_sum_ref[...] = jnp.zeros(g_sum_ref.shape, F32)

    def body(start, carry):
        here = pl.ds(start, tile)
        now = pl.ds(begin + start, tile)
        probs = probs_ref[now, :]
        wide_ref[...] = spread_columns(probs, spread_ref[...])
        columns = [None] * 14
        for e in range(6):
            output = (
                normal_ref[e, now, :].astype(F32) * small_ref[2, e : e + 1, :]
                + small_ref[3, e : e + 1, :]
            )
            for index, (low, _) in enumerate(GROUPS_ONE):
                if e in MEMBERS_ONE[index]:
                    columns[low + MEMBERS_ONE[index].index(e)] = row_sum(
                        mixed_grad_ref[index, now, :] * output
                    )
        logit_ref[here, :] = group_softmax_back(probs, into_lane(columns), GROUPS_ONE).astype(BF16)
        for e in range(6):
            normal = normal_ref[e, now, :].astype(F32)
            out_grad = None
            for index, (low, _) in enumerate(GROUPS_ONE):
                if e in MEMBERS_ONE[index]:
                    column = low + MEMBERS_ONE[index].index(e)
                    term = column_block(wide_ref, column) * mixed_grad_ref[index, now, :]
                    out_grad = term if out_grad is None else out_grad + term
            g_small_ref[2, e : e + 1, :] += column_sum(out_grad * normal)
            g_small_ref[3, e : e + 1, :] += column_sum(out_grad)
            post_grad = norm_backward(
                out_grad * small_ref[2, e : e + 1, :],
                normal,
                scale_ref[e, now, :],
                means_ref[...],
            ).astype(BF16)
            post_grad_ref[e, here, :] = post_grad
            g_small_ref[1, e : e + 1, :] += column_sum(post_grad.astype(F32))
        for e in range(6):
            act_grad = mm_nt(post_grad_ref[e, here, :], w_out_ref[e])
            pre_grad = (act_grad * slope_ref[e, now, :].astype(F32)).astype(BF16)
            pre_grad_ref[here, spot(e)] = pre_grad
            g_small_ref[0, e : e + 1, :] += column_sum(pre_grad.astype(F32))
        level_grad = mm_nt(pre_grad_ref[here, :], w_in_ref[...]) + mm_nt(
            logit_ref[here, :], gate_ref[...]
        )
        level_grad_ref[here, :] = level_grad
        normed = (masked_ref[now, :].astype(F32) - entry_ref[0:1, :]) * entry_ref[1:2, :]
        g_sum_ref[0:1, :] += column_sum(level_grad * normed)
        g_sum_ref[1:2, :] += column_sum(level_grad)
        return carry

    tiles(tile)(logit_ref.shape[0], body)


def level_one_weights(
    count,
    rows,
    me_ref,
    level_ref,
    active_ref,
    small_ref,
    logit_a_ref,
    logit_b_ref,
    post_a_ref,
    post_b_ref,
    pre_a_ref,
    pre_b_ref,
    *rest,
):
    *grads_refs, flat_ref = rest
    width = level_ref.shape[1]
    lanes = width // LANES
    where_row, used_rows = first_layout(width)
    half = logit_a_ref.shape[0]
    one, two = slice(0, half), slice(half, level_ref.shape[0])
    for e in range(6):
        put_wide_rows(
            flat_ref,
            where_row["expert_in"] + e * 2 * width,
            width,
            mm_tn(level_ref[one, :], pre_a_ref[:, spot(e)])
            + mm_tn(level_ref[two, :], pre_b_ref[:, spot(e)]),
        )
        put_wide_rows(
            flat_ref,
            where_row["expert_out"] + e * 2 * H,
            H,
            mm_tn(active_ref[e, one, :], post_a_ref[e])
            + mm_tn(active_ref[e, two, :], post_b_ref[e]),
        )
    for index, name in enumerate(("expert_in_bias", "expert_out_bias", "norm_gain", "norm_bias")):
        put_wide_rows(flat_ref, where_row[name], 6, small_ref[index, :6, :])
    gate_rows = 14 * width // LANES
    gate = mm_tn(level_ref[one, :], logit_a_ref[...]) + mm_tn(level_ref[two, :], logit_b_ref[...])
    flat_ref[pl.ds(where_row["gate"], gate_rows), :] = rows_from_table(gate, gate_rows, 14)
    flat_ref[0 : 2 * lanes, :] = jnp.zeros((2 * lanes, LANES), F32)
    if used_rows < count * rows:
        flat_ref[pl.ds(used_rows, count * rows - used_rows), :] = jnp.zeros(
            (count * rows - used_rows, LANES), F32
        )
    collect_pieces(me_ref[0], count, rows, flat_ref, grads_refs)


def input_kernel(
    total_rows, grad_a_ref, grad_b_ref, masked_ref, presence_ref, entry_ref, sums_ref, out_ref
):
    width = masked_ref.shape[1]
    mask = spread_presence(presence_ref[...], width)
    inv_scale = entry_ref[1:2, :]
    gain = entry_ref[2:3, :]
    cross = sums_ref[0:1, :] * (1.0 / total_rows)
    plain = sums_ref[1:2, :] * (1.0 / total_rows)
    half = grad_a_ref.shape[0]
    for part, ref in enumerate((grad_a_ref, grad_b_ref)):
        now = slice(part * half, (part + 1) * half)
        normed = (masked_ref[now, :].astype(F32) - entry_ref[0:1, :]) * inv_scale
        out_ref[now, :] = mask[now] * ((inv_scale * gain) * (ref[...] - plain - normed * cross))


def xor_permute(value, axis, bit):
    size = lax.axis_size(axis)
    return lax.ppermute(value, axis, [(index, index ^ bit) for index in range(size)])


def hypercube_ok():
    wide, narrow = lax.axis_size("wide"), lax.axis_size("narrow")
    return wide == 8 and narrow == 4


def after(value, *others):
    return lax.optimization_barrier((value, *others))[0]


def small_kernel(kernel, inputs, out_shape, scalar=False):
    return run_kernel(kernel, inputs, out_shape, [], 8, 2**20, scalar=scalar)


def stack_kernel(*refs):
    sources, targets = refs[:4], refs[4:]
    each = 4 // len(targets)
    for index, ref in enumerate(sources):
        targets[index // each][index % each] = ref[...]


def gather_near(block):
    return [block] + [xor_permute(block, "narrow", k) for k in (1, 2, 3)]


def stack_near(near, parts):
    rows = near[0].shape[0]
    shapes = [jax.ShapeDtypeStruct((4 // parts, rows, LANES), BF16)] * parts
    return small_kernel(stack_kernel, near, shapes)


def gather_halves(first, second):
    first_y, second_x = xor_permute(first, "wide", 4), xor_permute(second, "wide", 2)
    first_x, second_y = xor_permute(first, "wide", 2), xor_permute(second, "wide", 4)
    first_xy, second_xy = xor_permute(first_y, "wide", 2), xor_permute(second_x, "wide", 4)
    own = [first, second, first_x, second_x, first_y, second_y, first_xy, second_xy]
    other = [xor_permute(piece, "wide", 1) for piece in own]
    pieces = []
    for index in range(4):
        pieces += [own[2 * index], own[2 * index + 1], other[2 * index], other[2 * index + 1]]
    return pieces


def gather_plane(stack):
    return [stack] + [xor_permute(stack, "wide", bit) for bit in (2, 4, 6)]


def gather_core(own):
    pieces = []
    for piece in own:
        pieces += [piece, xor_permute(piece, "wide", 1)]
    return pieces


def core_direct_kernel(keep_ref, got_ref, own_ref, *send_refs):
    total = keep_ref[...].astype(F32) + got_ref[...].astype(F32)
    own_ref[...] = total[0:4]
    for part, ref in enumerate(send_refs):
        ref[...] = total[4 * (part + 1) : 4 * (part + 2)].astype(BF16)


def plane_direct_kernel(own_ref, one_ref, two_ref, three_ref, keep_ref, *send_refs):
    total = own_ref[...]
    for ref in (one_ref, two_ref, three_ref):
        total = total + ref[...].astype(F32)
    keep_ref[...] = total[0]
    for part, ref in enumerate(send_refs):
        ref[...] = total[part + 1].astype(BF16)


def last_kernel(own_ref, one_ref, two_ref, three_ref, out_ref):
    total = own_ref[...]
    for ref in (one_ref, two_ref, three_ref):
        total = total + ref[...].astype(F32)
    out_ref[...] = total[: out_ref.shape[0]]


def last_head_kernel(me_ref, sums_ref, own_ref, one_ref, two_ref, three_ref, out_ref):
    last_kernel(own_ref, one_ref, two_ref, three_ref, out_ref)
    put_head(me_ref, sums_ref, out_ref)


def put_head(me_ref, sums_ref, out_ref):
    @pl.when(me_ref[0] == 0)
    def _():
        lanes = sums_ref.shape[1] // LANES
        for index in range(2 * lanes):
            part = slice(index % lanes * LANES, (index % lanes + 1) * LANES)
            row = index // lanes
            out_ref[index : index + 1, :] = sums_ref[row : row + 1, part]


def head_kernel(me_ref, sums_ref, block_ref, out_ref):
    out_ref[...] = block_ref[...]
    put_head(me_ref, sums_ref, out_ref)


def add_kernel(one_ref, two_ref, out_ref):
    out_ref[...] = one_ref[...] + two_ref[...]


def core_halves_kernel(
    keep_ref, got_ref, sums_ref, sums_got_ref, one_ref, two_ref, out_ref, send_one_ref, send_two_ref
):
    total = keep_ref[...].astype(F32) + got_ref[...].astype(F32)
    for x in range(2):
        for z in range(2):
            one_ref[2 * x + z] = total[4 * x + z]
            send_one_ref[2 * x + z] = total[8 + 4 * x + z].astype(BF16)
    for y in range(2):
        for z in range(2):
            two_ref[2 * y + z] = total[8 * y + 2 + z]
            send_two_ref[2 * y + z] = total[8 * y + 4 + 2 + z].astype(BF16)
    out_ref[...] = sums_ref[...] + sums_got_ref[...]


def plane_halves_kernel(
    one_ref,
    two_ref,
    got_one_ref,
    got_two_ref,
    sums_ref,
    sums_got_ref,
    keep_one_ref,
    keep_two_ref,
    out_ref,
    send_one_ref,
    send_two_ref,
):
    for ref, got, keep, send in (
        (one_ref, got_one_ref, keep_one_ref, send_one_ref),
        (two_ref, got_two_ref, keep_two_ref, send_two_ref),
    ):
        total = ref[...] + got[...].astype(F32)
        keep[...] = total[0:2]
        send[...] = total[2:4].astype(BF16)
    out_ref[...] = sums_ref[...] + sums_got_ref[...]


def near_halves_kernel(
    one_ref, two_ref, got_one_ref, got_two_ref, keep_ref, send_one_ref, send_two_ref, send_three_ref
):
    one = one_ref[...] + got_one_ref[...].astype(F32)
    two = two_ref[...] + got_two_ref[...].astype(F32)
    keep_ref[...] = one[0]
    send_one_ref[...] = one[1].astype(BF16)
    send_two_ref[...] = two[0].astype(BF16)
    send_three_ref[...] = two[1].astype(BF16)


def add_four_kernel(one_ref, two_ref, three_ref, four_ref, out_ref):
    out_ref[...] = (one_ref[...] + two_ref[...]) + (three_ref[...] + four_ref[...])


def scatter_plain(value):
    return lax.psum_scatter(value.astype(F32), AXES, scatter_dimension=0, tiled=True)[0]


def per_device(features, presence, first_params, second_params, cotangent):
    rows, width = features.shape
    lanes = width // LANES
    devices_all = count = lax.axis_size(AXES)
    total_rows = rows * devices_all
    cube = hypercube_ok()
    tile = math.gcd(rows, 256)
    half = rows // 2
    me = lax.axis_index(AXES).astype(jnp.int32).reshape(1)
    chunks = [first_params.shape[0] // LANES, second_params.shape[0] // LANES]
    extra = 6 * lanes
    shape = jax.ShapeDtypeStruct
    fields = presence.T
    blocks = [up(chunks[0], 16), up(chunks[1], 16)]

    masked, block_one, block_two = run_kernel(
        stats_kernel,
        [
            me,
            features,
            fields,
            first_params.reshape(chunks[0], LANES),
            second_params.reshape(chunks[1], LANES),
        ],
        (
            shape((rows, width), BF16),
            shape((up(chunks[0] + extra, 16), LANES), BF16),
            shape((blocks[1], LANES), BF16),
        ),
        [],
        8,
        rows * width * 10,
    )
    if cube:
        origin = me
        near_one = gather_near(block_one)
        first, second = stack_near(near_one, 2)
        near_two = gather_near(after(block_two, first))
        pieces_one = gather_halves(first, second)
        (stack_two,) = stack_near(near_two, 1)
        plane_two = gather_plane(after(stack_two, pieces_one[12], pieces_one[13]))
        masked = after(masked, stack_two)
    else:
        origin = jnp.zeros((1,), jnp.int32)
        pieces_one = [lax.all_gather(block_one, AXES)]
        plane_two = [lax.all_gather(block_two, AXES)]

    saved = run_kernel(
        functools.partial(level_one_forward, chunks[0], tile, len(pieces_one)),
        [origin, masked] + pieces_one,
        [
            shape((rows, width), BF16),
            shape((6, rows, H), BF16),
            shape((6, rows, H), BF16),
            shape((6, rows, H), BF16),
            shape((6, rows, LANES), F32),
            shape((rows, LANES), F32),
            shape((3, rows, H), BF16),
            shape((width, 6 * H), BF16),
            shape((6, H, H), BF16),
            shape((4, 8, H), F32),
            shape((width, LANES), BF16),
            shape((8, width), F32),
        ],
        [
            pltpu.VMEM((count * chunks[0], LANES), F32),
            pltpu.VMEM((count, extra, LANES), F32),
            pltpu.VMEM((6, tile, H), F32),
            pltpu.VMEM((tile, 14 * LANES), F32),
            pltpu.VMEM((2 * LANES, 14 * LANES), BF16),
        ],
        20,
        rows * 6 * (width + H) * H * 2,
    )
    level, active, slope, normal, scale, probs, mixed, w_in, w_out, small, gate, entry = saved
    pieces_two = gather_core([after(piece, entry) for piece in plane_two]) if cube else plane_two

    outs = 2 if cube else 1
    towers, mixed_grad, *grads_two = run_kernel(
        functools.partial(level_two, count, chunks[1], tile, len(pieces_two), outs),
        [origin, mixed, cotangent] + pieces_two,
        [
            shape((rows, LANES), F32),
            shape((3, rows, H), F32),
        ]
        + [shape((count // outs, blocks[1], LANES), BF16)] * outs,
        [
            pltpu.VMEM((count * chunks[1], LANES), F32),
            pltpu.VMEM((H, 6 * H), BF16),
            pltpu.VMEM((6, H, H), BF16),
            pltpu.VMEM((4, 8, H), F32),
            pltpu.VMEM((H, LANES), BF16),
            pltpu.VMEM((2, H, TOWER1), BF16),
            pltpu.VMEM((2 * TOWER1, LANES), BF16),
            pltpu.VMEM((2 * TOWER1, LANES), F32),
            pltpu.VMEM((8, 2 * TOWER1), F32),
            pltpu.VMEM((4, 8, H), F32),
            pltpu.VMEM((2 * TOWER1, LANES), F32),
            pltpu.VMEM((8, 2 * TOWER1), F32),
            pltpu.VMEM((6, rows, H), BF16),
            pltpu.VMEM((tile, 6 * H), F32),
            pltpu.VMEM((6, tile, H), F32),
            pltpu.VMEM((6, tile, LANES), F32),
            pltpu.VMEM((6, tile, H), F32),
            pltpu.VMEM((2, rows, H), BF16),
            pltpu.VMEM((2, tile, H), F32),
            pltpu.VMEM((rows, 2 * TOWER1), BF16),
            pltpu.VMEM((rows, 2 * TOWER1), BF16),
            pltpu.VMEM((2, rows, LANES), BF16),
            pltpu.VMEM((6, rows, H), BF16),
            pltpu.VMEM((rows, 6 * H), BF16),
            pltpu.VMEM((tile, 8 * LANES), F32),
            pltpu.VMEM((2 * LANES, 8 * LANES), BF16),
            pltpu.VMEM((2 * H, 2 * LANES), BF16),
        ],
        32,
        rows * 6 * 2 * H * H * 2 * 3,
    )
    if cube:
        keep_two, send_two = grads_two
        own_two, *sends_two = small_kernel(
            core_direct_kernel,
            [keep_two, xor_permute(send_two, "wide", 1)],
            [shape((4, blocks[1], LANES), F32)] + [shape((4, blocks[1], LANES), BF16)] * 3,
        )

    def backward(part, *before):
        return run_kernel(
            functools.partial(level_one_backward, min(tile, half), part * half),
            [
                mixed_grad,
                masked,
                slope,
                normal,
                scale,
                probs,
                w_in,
                w_out,
                small,
                gate,
                entry if part == 0 or not cube else after(entry, own_two),
                *before,
            ],
            [
                shape((half, width), F32),
                shape((8, width), F32),
                shape((4, 8, H), F32),
                shape((half, LANES), BF16),
                shape((6, half, H), BF16),
                shape((half, 6 * H), BF16),
            ],
            [
                pltpu.VMEM((min(tile, half), 14 * LANES), F32),
                pltpu.VMEM((2 * LANES, 14 * LANES), BF16),
                pltpu.VMEM((2 * H, 2 * LANES), BF16),
            ],
            12,
            rows * 6 * (width + H) * H * 2,
            scalar=False,
        )

    grad_a, sums, g_small, logit_a, post_a, pre_a = backward(0)
    grad_b, sums, g_small, logit_b, post_b, pre_b = backward(1, sums, g_small)
    grads_one = run_kernel(
        functools.partial(level_one_weights, count, chunks[0]),
        [
            origin,
            level,
            active,
            g_small,
            logit_a,
            logit_b,
            post_a,
            post_b,
            pre_a,
            pre_b,
        ],
        [shape((count // outs, blocks[0], LANES), BF16)] * outs,
        [pltpu.VMEM((count * chunks[0], LANES), F32)],
        12,
        rows * 6 * (width + H) * H * 2,
    )
    if cube:
        low, high = shape((4, blocks[0], LANES), BF16), shape((4, blocks[0], LANES), F32)
        summed = shape((8, width), F32)
        keep, send = grads_one
        sums = small_kernel(
            add_kernel, [sums, after(xor_permute(sums, "wide", 1), send)], summed
        )
        keep_two, *sends_two = small_kernel(
            plane_direct_kernel,
            [own_two]
            + [xor_permute(part, "wide", bit) for part, bit in zip(sends_two, (2, 4, 6))],
            [shape((blocks[1], LANES), F32)] + [shape((blocks[1], LANES), BF16)] * 3,
        )
        one, two, sums, send_one, send_two = small_kernel(
            core_halves_kernel,
            [after(keep, keep_two), xor_permute(send, "wide", 1), sums, xor_permute(sums, "wide", 4)],
            [high, high, summed, low, low],
        )
        low, high = shape((2, blocks[0], LANES), BF16), shape((2, blocks[0], LANES), F32)
        one, two, sums, send_one, send_two = small_kernel(
            plane_halves_kernel,
            [
                one,
                two,
                xor_permute(send_one, "wide", 4),
                xor_permute(send_two, "wide", 2),
                sums,
                xor_permute(sums, "wide", 2),
            ],
            [high, high, summed, low, low],
        )
        low, high = shape((blocks[0], LANES), BF16), shape((blocks[0], LANES), F32)
        keep, *sends = small_kernel(
            near_halves_kernel,
            [one, two, xor_permute(send_one, "wide", 2), xor_permute(send_two, "wide", 4)],
            [high, low, low, low],
        )
        sums = small_kernel(
            add_four_kernel,
            [sums] + [xor_permute(sums, "narrow", k) for k in (1, 2, 3)],
            summed,
        )
        second_grad = small_kernel(
            last_kernel,
            [keep_two]
            + [xor_permute(part, "narrow", k) for part, k in zip(sends_two, (1, 2, 3))],
            shape((chunks[1], LANES), F32),
        )
        first_grad = small_kernel(
            last_head_kernel,
            [me, sums, keep]
            + [xor_permute(part, "narrow", k) for part, k in zip(sends, (1, 2, 3))],
            shape((chunks[0], LANES), F32),
            scalar=True,
        )
    else:
        sums = lax.psum(sums, AXES)
        second_grad = scatter_plain(grads_two[0])[: chunks[1]]
        first_grad = small_kernel(
            head_kernel,
            [me, sums, scatter_plain(grads_one[0])[: chunks[0]]],
            shape((chunks[0], LANES), F32),
            scalar=True,
        )

    input_grad = run_kernel(
        functools.partial(input_kernel, float(total_rows)),
        [grad_a, grad_b, masked, fields, entry, sums],
        shape((rows, width), F32),
        [],
        8,
        rows * width * 10,
        scalar=False,
    )
    return (towers, input_grad, first_grad.reshape(-1), second_grad.reshape(-1))


def solution(mesh):
    placed = (
        P(AXES, None),
        P(AXES, None),
        P(AXES),
        P(AXES),
        P(AXES, None),
    )
    return jax.shard_map(
        per_device,
        mesh=mesh,
        in_specs=placed,
        out_specs=(P(AXES, None), P(AXES, None), P(AXES), P(AXES)),
        check_vma=False,
    )
```

```python
import functools
import math

import jax
import jax.numpy as jnp
from jax import lax
from jax.experimental import pallas as pl
from jax.experimental.pallas import tpu as pltpu
from jax.sharding import PartitionSpec as P

H = 256
TOWER1 = 128
TOWER2 = 64
LANES = 128
EPSILON = 1e-05
AXES = ("wide", "narrow")
F32 = jnp.float32
BF16 = jnp.bfloat16
GROUPS_ONE = ((0, 4), (4, 8), (8, 14))
MEMBERS_ONE = ((0, 1, 4, 5), (2, 3, 4, 5), (0, 1, 2, 3, 4, 5))
GROUPS_TWO = ((0, 4), (4, 8))
MEMBERS_TWO = ((0, 1, 4, 5), (2, 3, 4, 5))


def up(value, step):
    return -(-value // step) * step


def mm(left, right):
    return jnp.dot(left, right, preferred_element_type=F32)


def mm_nt(left, right):
    return lax.dot_general(left, right, (((1,), (1,)), ((), ())), preferred_element_type=F32)


def mm_tn(left, right):
    return lax.dot_general(left, right, (((0,), (0,)), ((), ())), preferred_element_type=F32)


def sigmoid(values):
    return 0.5 * jnp.tanh(0.5 * values) + 0.5


def group_softmax(logits, groups):
    lane = lax.broadcasted_iota(jnp.int32, logits.shape, 1)
    spread = jnp.zeros_like(logits)
    for low, high in groups:
        inside = (lane >= low) & (lane < high)
        peak = jnp.max(jnp.where(inside, logits, -jnp.inf), axis=1, keepdims=True)
        spread = jnp.where(inside, logits - peak, spread)
    raw = jnp.exp(spread)
    result = jnp.zeros_like(logits)
    for low, high in groups:
        inside = (lane >= low) & (lane < high)
        total = jnp.sum(jnp.where(inside, raw, 0.0), axis=1, keepdims=True)
        result = jnp.where(inside, raw / total, result)
    return result


def group_softmax_back(probs, grads, groups):
    lane = lax.broadcasted_iota(jnp.int32, probs.shape, 1)
    product = probs * grads
    result = jnp.zeros_like(probs)
    for low, high in groups:
        inside = (lane >= low) & (lane < high)
        total = jnp.sum(jnp.where(inside, product, 0.0), axis=1, keepdims=True)
        result = jnp.where(inside, product - probs * total, result)
    return result


def into_lane(columns):
    rows = columns[0].shape[0]
    lane = lax.broadcasted_iota(jnp.int32, (rows, LANES), 1)
    result = jnp.zeros((rows, LANES), F32)
    for position, column in enumerate(columns):
        result = jnp.where(lane == position, column, result)
    return result


def mix_parts(weights, low, members, outputs):
    running = None
    for position, member in enumerate(members):
        term = column_block(weights, low + position) * outputs[member]
        running = term if running is None else running + term
    return running


def row_sum(values):
    return jnp.sum(values, axis=1, keepdims=True)


def column_sum(values):
    return jnp.sum(values, axis=0, keepdims=True)


def norm_forward(post):
    centred = post - row_sum(post) * (1.0 / H)
    scale = lax.rsqrt(row_sum(centred * centred) * (1.0 / H) + EPSILON)
    return centred * scale, scale


def twice(values):
    return jnp.concatenate([values, values], axis=1)


def norm_backward(scaled, normal, scale, means):
    both = jnp.concatenate([scaled.astype(BF16), (scaled * normal).astype(BF16)], axis=1)
    mean = mm(both, means)
    return twice(scale) * (
        scaled - twice(mean[:, :LANES]) - normal * twice(mean[:, LANES:])
    )


def make_means():
    row = lax.broadcasted_iota(jnp.int32, (2 * H, 2 * LANES), 0)
    lane = lax.broadcasted_iota(jnp.int32, (2 * H, 2 * LANES), 1)
    return jnp.where((row < H) == (lane < LANES), 1.0 / H, 0.0).astype(BF16)


def make_spread(columns):
    row = lax.broadcasted_iota(jnp.int32, (2 * LANES, columns * LANES), 0)
    lane = lax.broadcasted_iota(jnp.int32, (2 * LANES, columns * LANES), 1)
    return jnp.where((row & (LANES - 1)) == (lane >> 7), 1.0, 0.0).astype(BF16)


def spread_columns(values, spread):
    high = values.astype(BF16)
    low = (values - high.astype(F32)).astype(BF16)
    return mm(jnp.concatenate([high, low], axis=1), spread)


def column_block(spread, column):
    return twice(spread[:, column * LANES : (column + 1) * LANES])


def first_layout(width):
    names = (
        ("in_gain", width),
        ("in_bias", width),
        ("expert_in", 6 * width * H),
        ("expert_in_bias", 6 * H),
        ("expert_out", 6 * H * H),
        ("expert_out_bias", 6 * H),
        ("norm_gain", 6 * H),
        ("norm_bias", 6 * H),
        ("gate", 14 * width),
    )
    return place_names(names)


def second_layout():
    names = (
        ("expert_in", 6 * H * H),
        ("expert_in_bias", 6 * H),
        ("expert_out", 6 * H * H),
        ("expert_out_bias", 6 * H),
        ("norm_gain", 6 * H),
        ("norm_bias", 6 * H),
        ("gate", 2 * H * 4),
        ("tower_in", 2 * H * TOWER1),
        ("tower_in_bias", 2 * TOWER1),
        ("tower_out", 2 * TOWER1 * TOWER2),
        ("tower_out_bias", 2 * TOWER2),
    )
    return place_names(names)


def place_names(names):
    rows = {}
    offset = 0
    for name, amount in names:
        rows[name] = offset // LANES
        offset += amount
    return rows, offset // LANES


def spread_pieces(me, rows, piece_refs, flat_ref, extra_ref=None):
    slot = 0
    for ref in piece_refs:
        for index in range(ref.shape[0]):
            owner = lax.bitwise_xor(me, jnp.int32(slot))
            block = ref[index].astype(F32)
            flat_ref[pl.ds(owner * rows, rows), :] = block[:rows]
            if extra_ref is not None:
                extra_ref[slot] = block[rows : rows + extra_ref.shape[1]]
            slot += 1


def wide_rows(flat_ref, row, amount):
    return jnp.concatenate(
        [flat_ref[pl.ds(row, amount, stride=2), :], flat_ref[pl.ds(row + 1, amount, stride=2), :]],
        axis=1,
    )


def put_wide_rows(flat_ref, row, amount, value):
    flat_ref[pl.ds(row, amount, stride=2), :] = value[:, :LANES]
    flat_ref[pl.ds(row + 1, amount, stride=2), :] = value[:, LANES:]


def collect_pieces(me, count, rows, flat_ref, out_refs):
    for slot in range(count):
        owner = lax.bitwise_xor(me, jnp.int32(slot))
        value = flat_ref[pl.ds(owner * rows, rows), :].astype(BF16)
        if len(out_refs) == 1:
            out_refs[0][slot, :rows, :] = value
        else:
            part, place = slot // 4 % 2, slot // 8 * 4 + slot % 4
            out_refs[part][place, :rows, :] = value


def roll_rows(value, columns, sign):
    item = lax.broadcasted_iota(jnp.int32, value.shape, 0)
    bit = 1
    while columns * bit % LANES:
        moved = pltpu.roll(value, sign * columns * bit % LANES, 1)
        value = jnp.where((item & bit) != 0, moved, value)
        bit *= 2
    return value


def table_places(width, columns, rows):
    item = lax.broadcasted_iota(jnp.int32, (width, rows), 0)
    index = lax.broadcasted_iota(jnp.int32, (width, rows), 1)
    first = (index == ((item * columns) >> 7)).astype(F32).astype(BF16)
    last = (index == ((item * columns + columns - 1) >> 7)).astype(F32).astype(BF16)
    item = lax.broadcasted_iota(jnp.int32, (width, LANES), 0)
    lane = lax.broadcasted_iota(jnp.int32, (width, LANES), 1)
    return first, last, lane >= ((item * columns) & (LANES - 1)), lane < columns


def table_from_rows(flat, width, columns):
    first, last, late, used = table_places(width, columns, flat.shape[0])
    chosen = jnp.where(late, mm(first, flat), mm(last, flat))
    return jnp.where(used, roll_rows(chosen, columns, -1), 0.0)


def rows_from_table(table, rows, columns):
    first, last, late, _ = table_places(table.shape[0], columns, rows)
    moved = roll_rows(table, columns, 1)
    return mm_tn(first, jnp.where(late, moved, 0.0).astype(BF16)) + mm_tn(
        last, jnp.where(late, 0.0, moved).astype(BF16)
    )


def full_spec():
    return pl.BlockSpec(memory_space=pltpu.VMEM)


def scalar_spec():
    return pl.BlockSpec(memory_space=pltpu.SMEM)


def run_kernel(kernel, inputs, out_shape, scratch, limit, flops, scalar=True, spec=None):
    specs = [spec or full_spec()] * len(inputs)
    if scalar:
        specs[0] = scalar_spec()
    several = isinstance(out_shape, (list, tuple))
    out_specs = [full_spec()] * len(out_shape) if several else full_spec()
    return pl.pallas_call(
        kernel,
        in_specs=specs,
        out_specs=out_specs,
        out_shape=out_shape,
        scratch_shapes=scratch,
        compiler_params=pltpu.CompilerParams(vmem_limit_bytes=limit * 2**20),
        cost_estimate=pl.CostEstimate(flops=2**20, bytes_accessed=2**10, transcendentals=0),
    )(*inputs)


def spread_presence(presence, width):
    fields = presence.shape[0]
    field = lax.broadcasted_iota(jnp.int32, (fields, width), 0)
    column = lax.broadcasted_iota(jnp.int32, (fields, width), 1)
    pick = (column // (width // fields) == field).astype(F32).astype(BF16)
    return mm_tn(presence.astype(F32).astype(BF16), pick)


def split_three(values):
    parts = []
    for _ in range(3):
        part = values.astype(BF16).astype(F32)
        parts.append(part)
        values = values - part
    return parts


def stats_kernel(
    me_ref,
    features_hbm,
    presence_hbm,
    params_hbm,
    second_hbm,
    masked_ref,
    block_ref,
    block_two_ref,
    features_ref,
    presence_ref,
    params_ref,
    second_ref,
    sems,
):
    del me_ref
    copies = [
        pltpu.make_async_copy(source, target, sems.at[index])
        for index, (source, target) in enumerate(
            (
                (presence_hbm, presence_ref),
                (features_hbm, features_ref),
                (params_hbm, params_ref),
                (second_hbm, second_ref),
            )
        )
    ]
    for copy in copies:
        copy.start()
    for copy in copies:
        copy.wait()
    rows, width = features_ref.shape
    mask = spread_presence(presence_ref[...], width)
    masked = features_ref[...].astype(F32) * mask
    masked_ref[...] = masked.astype(BF16)
    mean = column_sum(masked) * (1.0 / rows)
    spread = masked - mean
    moment = column_sum(spread * spread)
    lines = [params_ref[...].astype(F32)]
    for value in (mean, moment):
        for part in split_three(value):
            for index in range(width // LANES):
                lines.append(part[:, index * LANES : (index + 1) * LANES])
    used = params_ref.shape[0] + 6 * (width // LANES)
    lines.append(jnp.zeros((block_ref.shape[0] - used, LANES), F32))
    block_ref[...] = jnp.concatenate(lines, axis=0).astype(BF16)
    second = second_ref[...].astype(F32)
    rest = jnp.zeros((block_two_ref.shape[0] - second.shape[0], LANES), F32)
    block_two_ref[...] = jnp.concatenate([second, rest], axis=0).astype(BF16)


def from_lanes(block):
    return jnp.concatenate([block[index : index + 1, :] for index in range(block.shape[0])], axis=1)


def tiles(tile):
    return lambda ref_rows, body: lax.fori_loop(
        0, ref_rows // tile, lambda step, carry: body(pl.multiple_of(step * tile, tile), carry), 0
    )


def in_turn(first, second):
    for e in range(7):
        if e < 6:
            first(e)
        if e > 0:
            second(e - 1)


def spot(e):
    return slice(e * H, (e + 1) * H)


def level_one_forward(
    rows,
    tile,
    n_pieces,
    me_ref,
    masked_ref,
    *rest,
):
    piece_refs = rest[:n_pieces]
    (
        level_ref,
        active_ref,
        slope_ref,
        normal_ref,
        scale_ref,
        probs_ref,
        mixed_ref,
        w_in_ref,
        w_out_ref,
        small_ref,
        gate_ref,
        entry_ref,
        flat_ref,
        extra_ref,
        output_ref,
        wide_ref,
        spread_ref,
    ) = rest[n_pieces:]
    width = masked_ref.shape[1]
    where_row, _ = first_layout(width)

    spread_pieces(me_ref[0], rows, piece_refs, flat_ref, extra_ref)
    spread_ref[...] = make_spread(14)
    for e in range(6):
        w_in_ref[:, spot(e)] = wide_rows(
            flat_ref, where_row["expert_in"] + e * 2 * width, width
        ).astype(BF16)
        w_out_ref[e] = wide_rows(flat_ref, where_row["expert_out"] + e * 2 * H, H).astype(BF16)
    for index, name in enumerate(("expert_in_bias", "expert_out_bias", "norm_gain", "norm_bias")):
        small_ref[index, :6, :] = wide_rows(flat_ref, where_row[name], 6)
    gate_flat = flat_ref[pl.ds(where_row["gate"], 14 * width // LANES), :].astype(BF16)
    gate_ref[...] = table_from_rows(gate_flat, width, 14).astype(BF16)
    lanes = width // LANES
    events = masked_ref.shape[0]
    count = extra_ref.shape[0]
    means = extra_ref[:, 0:lanes, :]
    for part in (1, 2):
        means = means + extra_ref[:, part * lanes : (part + 1) * lanes, :]
    mean = jnp.sum(means, axis=0) * (1.0 / count)
    away = jnp.sum(jnp.square(means - mean[None]), axis=0) * events
    for part in (3, 4, 5):
        away = away + jnp.sum(extra_ref[:, part * lanes : (part + 1) * lanes, :], axis=0)
    entry_ref[0:1, :] = from_lanes(mean)
    entry_ref[1:2, :] = from_lanes(lax.rsqrt(away * (1.0 / (events * count)) + EPSILON))
    entry_ref[2:3, :] = from_lanes(flat_ref[0:lanes, :])
    entry_ref[3:4, :] = from_lanes(flat_ref[lanes : 2 * lanes, :])

    def body(start, carry):
        now = pl.ds(start, tile)
        normed = (masked_ref[now, :].astype(F32) - entry_ref[0:1, :]) * entry_ref[1:2, :]
        level_ref[now, :] = (normed * entry_ref[2:3, :] + entry_ref[3:4, :]).astype(BF16)
        probs_ref[now, :] = group_softmax(mm(level_ref[now, :], gate_ref[...]), GROUPS_ONE)
        def first_half(e):
            pre = mm(level_ref[now, :], w_in_ref[:, spot(e)]) + small_ref[0, e : e + 1, :]
            gate = sigmoid(pre)
            silu = pre * gate
            active_ref[e, now, :] = silu.astype(BF16)
            slope_ref[e, now, :] = (gate + silu * (1.0 - gate)).astype(BF16)

        def second_half(e):
            post = mm(active_ref[e, now, :], w_out_ref[e]) + small_ref[1, e : e + 1, :]
            normal, scale = norm_forward(post)
            normal_ref[e, now, :] = normal.astype(BF16)
            scale_ref[e, now, :] = jnp.broadcast_to(scale, (tile, LANES))
            output_ref[e] = normal * small_ref[2, e : e + 1, :] + small_ref[3, e : e + 1, :]

        in_turn(first_half, second_half)
        wide_ref[...] = spread_columns(probs_ref[now, :], spread_ref[...])
        for index, (low, _) in enumerate(GROUPS_ONE):
            mixed_ref[index, now, :] = mix_parts(
                wide_ref, low, MEMBERS_ONE[index], output_ref
            ).astype(BF16)
        return carry

    tiles(tile)(masked_ref.shape[0], body)


def level_two(count, rows, tile, n_pieces, n_outs, me_ref, mixed_ref, cotangent_ref, *rest):
    piece_refs = rest[:n_pieces]
    grads_refs = rest[n_pieces + 2 : n_pieces + 2 + n_outs]
    towers_ref, mixed_grad_ref = rest[n_pieces : n_pieces + 2]
    (
        flat_ref,
        w_in_ref,
        w_out_ref,
        small_ref,
        gate_ref,
        tower_in_ref,
        tower_out_ref,
        tower_tmp_ref,
        tower_small_ref,
        g_small_ref,
        g_tower_out_ref,
        g_tower_small_ref,
        active_ref,
        slope_ref,
        normal_ref,
        scale_ref,
        output_ref,
        combined_ref,
        combined_grad_ref,
        tower_active_ref,
        tower_grad_ref,
        logit_ref,
        post_grad_ref,
        pre_grad_ref,
        wide_ref,
        spread_ref,
        means_ref,
    ) = rest[n_pieces + 2 + n_outs :]
    where_row, used_rows = second_layout()
    all_rows = mixed_ref.shape[1]

    spread_pieces(me_ref[0], rows, piece_refs, flat_ref)
    spread_ref[...] = make_spread(8)
    means_ref[...] = make_means()
    for e in range(6):
        w_in_ref[:, spot(e)] = wide_rows(flat_ref, where_row["expert_in"] + e * 2 * H, H).astype(
            BF16
        )
        w_out_ref[e] = wide_rows(flat_ref, where_row["expert_out"] + e * 2 * H, H).astype(BF16)
    for index, name in enumerate(("expert_in_bias", "expert_out_bias", "norm_gain", "norm_bias")):
        small_ref[index, :6, :] = wide_rows(flat_ref, where_row[name], 6)
    gate_rows = H * 4 // LANES
    shift_a = lax.broadcasted_iota(jnp.int32, (LANES, LANES), 0)
    shift_b = lax.broadcasted_iota(jnp.int32, (LANES, LANES), 1)
    shift = ((shift_a + 4 == shift_b) & (shift_a < 4)).astype(F32).astype(BF16)
    tables = []
    for task in range(2):
        piece = flat_ref[pl.ds(where_row["gate"] + task * gate_rows, gate_rows), :].astype(BF16)
        tables.append(table_from_rows(piece, H, 4).astype(BF16))
    gate_ref[...] = (tables[0].astype(F32) + mm(tables[1], shift)).astype(BF16)
    zero = jnp.zeros((TOWER1 // 2, TOWER2), F32)
    for task in range(2):
        tower_in_ref[task] = flat_ref[pl.ds(where_row["tower_in"] + task * H, H), :].astype(BF16)
        packed = flat_ref[pl.ds(where_row["tower_out"] + task * TOWER1 // 2, TOWER1 // 2), :]
        for half in range(2):
            pair = [packed[:, half * TOWER2 : (half + 1) * TOWER2], zero]
            if task == 1:
                pair.reverse()
            tower_tmp_ref[pl.ds(task * TOWER1 + half, TOWER1 // 2, stride=2), :] = jnp.concatenate(
                pair, axis=1
            )
    tower_out_ref[...] = tower_tmp_ref[...].astype(BF16)
    tower_small_ref[0:1, :] = from_lanes(flat_ref[pl.ds(where_row["tower_in_bias"], 2), :])
    tower_small_ref[1:2, :LANES] = flat_ref[pl.ds(where_row["tower_out_bias"], 1), :]
    g_small_ref[...] = jnp.zeros(g_small_ref.shape, F32)
    g_tower_small_ref[...] = jnp.zeros(g_tower_small_ref.shape, F32)

    def body(start, carry):
        now = pl.ds(start, tile)
        lane = lax.broadcasted_iota(jnp.int32, (tile, LANES), 1)
        def first_half(e):
            pre = mm(mixed_ref[e // 2, now, :], w_in_ref[:, spot(e)]) + small_ref[0, e : e + 1, :]
            gate = sigmoid(pre)
            silu = pre * gate
            active_ref[e, now, :] = silu.astype(BF16)
            slope_ref[:, spot(e)] = gate + silu * (1.0 - gate)

        def second_half(e):
            post = mm(active_ref[e, now, :], w_out_ref[e]) + small_ref[1, e : e + 1, :]
            normal, scale = norm_forward(post)
            normal_ref[e] = normal
            scale_ref[e] = jnp.broadcast_to(scale, (tile, LANES))
            output_ref[e] = normal * small_ref[2, e : e + 1, :] + small_ref[3, e : e + 1, :]

        in_turn(first_half, second_half)
        logits = jnp.where(
            lane < 4, mm(mixed_ref[0, now, :], gate_ref[...]), mm(mixed_ref[1, now, :], gate_ref[...])
        )
        probs = group_softmax(logits, GROUPS_TWO)
        wide_ref[...] = spread_columns(probs, spread_ref[...])
        for task in range(2):
            combined_ref[task, now, :] = mix_parts(
                wide_ref, 4 * task, MEMBERS_TWO[task], output_ref
            ).astype(BF16)
        tower_pre = (
            jnp.concatenate(
                [mm(combined_ref[task, now, :], tower_in_ref[task]) for task in range(2)], axis=1
            )
            + tower_small_ref[0:1, :]
        )
        tower_gate = sigmoid(tower_pre)
        tower_silu = tower_pre * tower_gate
        tower_active_ref[now, :] = tower_silu.astype(BF16)
        towers_ref[now, :] = (
            mm(tower_active_ref[now, :], tower_out_ref[...]) + tower_small_ref[1:2, :LANES]
        )
        cotangent = cotangent_ref[now, :]
        g_tower_small_ref[1:2, :LANES] += column_sum(cotangent.astype(F32))
        tower_slope = tower_gate + tower_silu * (1.0 - tower_gate)
        tower_grad = (mm_nt(cotangent, tower_out_ref[...]) * tower_slope).astype(BF16)
        tower_grad_ref[now, :] = tower_grad
        g_tower_small_ref[0:1, :] += column_sum(tower_grad.astype(F32))
        for task in range(2):
            combined_grad_ref[task] = mm_nt(
                tower_grad_ref[now, task * TOWER1 : (task + 1) * TOWER1], tower_in_ref[task]
            )
        prob_grads = into_lane(
            [
                row_sum(combined_grad_ref[task] * output_ref[member])
                for task in range(2)
                for member in MEMBERS_TWO[task]
            ]
        )
        logit_grad = group_softmax_back(probs, prob_grads, GROUPS_TWO)
        logit_ref[0, now, :] = jnp.where(lane < 4, logit_grad, 0.0).astype(BF16)
        logit_ref[1, now, :] = jnp.where((lane >= 4) & (lane < 8), logit_grad, 0.0).astype(BF16)
        def norm_half(e):
            out_grad = None
            for task in range(2):
                if e in MEMBERS_TWO[task]:
                    column = 4 * task + MEMBERS_TWO[task].index(e)
                    term = column_block(wide_ref, column) * combined_grad_ref[task]
                    out_grad = term if out_grad is None else out_grad + term
            normal = normal_ref[e]
            g_small_ref[2, e : e + 1, :] += column_sum(out_grad * normal)
            g_small_ref[3, e : e + 1, :] += column_sum(out_grad)
            post_grad = norm_backward(
                out_grad * small_ref[2, e : e + 1, :], normal, scale_ref[e], means_ref[...]
            )
            post_grad = post_grad.astype(BF16)
            post_grad_ref[e, now, :] = post_grad
            g_small_ref[1, e : e + 1, :] += column_sum(post_grad.astype(F32))

        def active_half(e):
            act_grad = mm_nt(post_grad_ref[e, now, :], w_out_ref[e])
            pre_grad = (act_grad * slope_ref[:, spot(e)]).astype(BF16)
            pre_grad_ref[now, spot(e)] = pre_grad
            g_small_ref[0, e : e + 1, :] += column_sum(pre_grad.astype(F32))

        in_turn(norm_half, active_half)
        for index in range(3):
            pair = slice(2 * index * H, 2 * (index + 1) * H)
            grad = mm_nt(pre_grad_ref[now, pair], w_in_ref[:, pair])
            if index < 2:
                grad = grad + mm_nt(logit_ref[index, now, :], gate_ref[...])
            mixed_grad_ref[index, now, :] = grad
        return carry

    tiles(tile)(all_rows, body)

    for e in range(6):
        put_wide_rows(
            flat_ref,
            where_row["expert_in"] + e * 2 * H,
            H,
            mm_tn(mixed_ref[e // 2], pre_grad_ref[:, spot(e)]),
        )
        put_wide_rows(
            flat_ref,
            where_row["expert_out"] + e * 2 * H,
            H,
            mm_tn(active_ref[e], post_grad_ref[e]),
        )
    for index, name in enumerate(("expert_in_bias", "expert_out_bias", "norm_gain", "norm_bias")):
        put_wide_rows(flat_ref, where_row[name], 6, g_small_ref[index, :6, :])
    back = ((shift_a == shift_b + 4) & (shift_b < 4)).astype(F32).astype(BF16)
    tables = [mm_tn(mixed_ref[task], logit_ref[task]) for task in range(2)]
    tables[1] = mm(tables[1].astype(BF16), back)
    g_tower_out_ref[...] = mm_tn(tower_active_ref[...], cotangent_ref[...])
    for task in range(2):
        flat_ref[pl.ds(where_row["gate"] + task * gate_rows, gate_rows), :] = rows_from_table(
            tables[task], gate_rows, 4
        )
        flat_ref[pl.ds(where_row["tower_in"] + task * H, H), :] = mm_tn(
            combined_ref[task], tower_grad_ref[:, task * TOWER1 : (task + 1) * TOWER1]
        )
        flat_ref[pl.ds(where_row["tower_out"] + task * TOWER1 // 2, TOWER1 // 2), :] = (
            jnp.concatenate(
                [
                    g_tower_out_ref[pl.ds(task * TOWER1 + half, TOWER1 // 2, stride=2), :][
                        :, task * TOWER2 : (task + 1) * TOWER2
                    ]
                    for half in range(2)
                ],
                axis=1,
            )
        )
        flat_ref[pl.ds(where_row["tower_in_bias"] + task, 1), :] = g_tower_small_ref[
            0:1, task * TOWER1 : (task + 1) * TOWER1
        ]
    flat_ref[pl.ds(where_row["tower_out_bias"], 1), :] = g_tower_small_ref[1:2, :LANES]
    if used_rows < count * rows:
        flat_ref[pl.ds(used_rows, count * rows - used_rows), :] = jnp.zeros(
            (count * rows - used_rows, LANES), F32
        )
    collect_pieces(me_ref[0], count, rows, flat_ref, grads_refs)


def level_one_backward(
    tile,
    begin,
    mixed_grad_ref,
    masked_ref,
    slope_ref,
    normal_ref,
    scale_ref,
    probs_ref,
    w_in_ref,
    w_out_ref,
    small_ref,
    gate_ref,
    entry_ref,
    *rest,
):
    if begin:
        before_sum_ref, before_small_ref, *rest = rest
    (
        level_grad_ref,
        g_sum_ref,
        g_small_ref,
        logit_ref,
        post_grad_ref,
        pre_grad_ref,
        wide_ref,
        spread_ref,
        means_ref,
    ) = rest
    spread_ref[...] = make_spread(14)
    means_ref[...] = make_means()
    if begin:
        g_small_ref[...] = before_small_ref[...]
        g_sum_ref[...] = before_sum_ref[...]
    else:
        g_small_ref[...] = jnp.zeros(g_small_ref.shape, F32)
        g_sum_ref[...] = jnp.zeros(g_sum_ref.shape, F32)

    def body(start, carry):
        here = pl.ds(start, tile)
        now = pl.ds(begin + start, tile)
        probs = probs_ref[now, :]
        wide_ref[...] = spread_columns(probs, spread_ref[...])
        columns = [None] * 14
        for e in range(6):
            output = (
                normal_ref[e, now, :].astype(F32) * small_ref[2, e : e + 1, :]
                + small_ref[3, e : e + 1, :]
            )
            for index, (low, _) in enumerate(GROUPS_ONE):
                if e in MEMBERS_ONE[index]:
                    columns[low + MEMBERS_ONE[index].index(e)] = row_sum(
                        mixed_grad_ref[index, now, :] * output
                    )
        logit_ref[here, :] = group_softmax_back(probs, into_lane(columns), GROUPS_ONE).astype(BF16)
        def norm_half(e):
            normal = normal_ref[e, now, :].astype(F32)
            out_grad = None
            for index, (low, _) in enumerate(GROUPS_ONE):
                if e in MEMBERS_ONE[index]:
                    column = low + MEMBERS_ONE[index].index(e)
                    term = column_block(wide_ref, column) * mixed_grad_ref[index, now, :]
                    out_grad = term if out_grad is None else out_grad + term
            g_small_ref[2, e : e + 1, :] += column_sum(out_grad * normal)
            g_small_ref[3, e : e + 1, :] += column_sum(out_grad)
            post_grad = norm_backward(
                out_grad * small_ref[2, e : e + 1, :],
                normal,
                scale_ref[e, now, :],
                means_ref[...],
            ).astype(BF16)
            post_grad_ref[e, here, :] = post_grad
            g_small_ref[1, e : e + 1, :] += column_sum(post_grad.astype(F32))

        def active_half(e):
            act_grad = mm_nt(post_grad_ref[e, here, :], w_out_ref[e])
            pre_grad = (act_grad * slope_ref[e, now, :].astype(F32)).astype(BF16)
            pre_grad_ref[here, spot(e)] = pre_grad
            g_small_ref[0, e : e + 1, :] += column_sum(pre_grad.astype(F32))

        in_turn(norm_half, active_half)
        level_grad = mm_nt(pre_grad_ref[here, :], w_in_ref[...]) + mm_nt(
            logit_ref[here, :], gate_ref[...]
        )
        level_grad_ref[here, :] = level_grad
        normed = (masked_ref[now, :].astype(F32) - entry_ref[0:1, :]) * entry_ref[1:2, :]
        g_sum_ref[0:1, :] += column_sum(level_grad * normed)
        g_sum_ref[1:2, :] += column_sum(level_grad)
        return carry

    tiles(tile)(logit_ref.shape[0], body)


def send_sums(sums, block_refs):
    high = sums.astype(BF16).astype(F32)
    lines = []
    for value in (high, sums - high):
        for row in range(2):
            for index in range(value.shape[1] // LANES):
                lines.append(value[row : row + 1, index * LANES : (index + 1) * LANES])
    block = jnp.concatenate(lines, axis=0).astype(BF16)
    for ref in block_refs:
        ref[ref.shape[0] - 16 :, :] = block


def got_sums(block_ref, shape):
    rows = block_ref.shape[0]
    block = block_ref[rows - 16 :, :].astype(F32)
    block = block[:8] + block[8:]
    lanes = shape[1] // LANES
    lines = [from_lanes(block[row * lanes : (row + 1) * lanes]) for row in range(2)]
    return jnp.concatenate(lines + [jnp.zeros((shape[0] - 2, shape[1]), F32)], axis=0)


def level_one_weights(
    count,
    rows,
    me_ref,
    level_ref,
    active_ref,
    sums_ref,
    small_ref,
    logit_a_ref,
    logit_b_ref,
    post_a_ref,
    post_b_ref,
    pre_a_ref,
    pre_b_ref,
    *rest,
):
    *grads_refs, flat_ref = rest
    width = level_ref.shape[1]
    lanes = width // LANES
    where_row, used_rows = first_layout(width)
    half = logit_a_ref.shape[0]
    one, two = slice(0, half), slice(half, level_ref.shape[0])
    for e in range(6):
        put_wide_rows(
            flat_ref,
            where_row["expert_in"] + e * 2 * width,
            width,
            mm_tn(level_ref[one, :], pre_a_ref[:, spot(e)])
            + mm_tn(level_ref[two, :], pre_b_ref[:, spot(e)]),
        )
        put_wide_rows(
            flat_ref,
            where_row["expert_out"] + e * 2 * H,
            H,
            mm_tn(active_ref[e, one, :], post_a_ref[e])
            + mm_tn(active_ref[e, two, :], post_b_ref[e]),
        )
    for index, name in enumerate(("expert_in_bias", "expert_out_bias", "norm_gain", "norm_bias")):
        put_wide_rows(flat_ref, where_row[name], 6, small_ref[index, :6, :])
    gate_rows = 14 * width // LANES
    gate = mm_tn(level_ref[one, :], logit_a_ref[...]) + mm_tn(level_ref[two, :], logit_b_ref[...])
    flat_ref[pl.ds(where_row["gate"], gate_rows), :] = rows_from_table(gate, gate_rows, 14)
    flat_ref[0 : 2 * lanes, :] = jnp.zeros((2 * lanes, LANES), F32)
    if used_rows < count * rows:
        flat_ref[pl.ds(used_rows, count * rows - used_rows), :] = jnp.zeros(
            (count * rows - used_rows, LANES), F32
        )
    collect_pieces(me_ref[0], count, rows, flat_ref, grads_refs)
    if len(grads_refs) > 1:
        send_sums(sums_ref[...], [grads_refs[1].at[0]])


def input_kernel(
    total_rows, grad_a_ref, grad_b_ref, masked_ref, presence_ref, entry_ref, sums_ref, out_ref
):
    width = masked_ref.shape[1]
    mask = spread_presence(presence_ref[...], width)
    inv_scale = entry_ref[1:2, :]
    gain = entry_ref[2:3, :]
    cross = sums_ref[0:1, :] * (1.0 / total_rows)
    plain = sums_ref[1:2, :] * (1.0 / total_rows)
    half = grad_a_ref.shape[0]
    for part, ref in enumerate((grad_a_ref, grad_b_ref)):
        now = slice(part * half, (part + 1) * half)
        normed = (masked_ref[now, :].astype(F32) - entry_ref[0:1, :]) * inv_scale
        out_ref[now, :] = mask[now] * ((inv_scale * gain) * (ref[...] - plain - normed * cross))


def xor_permute(value, axis, bit):
    size = lax.axis_size(axis)
    return lax.ppermute(value, axis, [(index, index ^ bit) for index in range(size)])


def hypercube_ok():
    wide, narrow = lax.axis_size("wide"), lax.axis_size("narrow")
    return wide == 8 and narrow == 4


def after(value, *others):
    return lax.optimization_barrier((value, *others))[0]


def small_kernel(kernel, inputs, out_shape, scalar=False):
    return run_kernel(kernel, inputs, out_shape, [], 8, 2**20, scalar=scalar)


def stack_kernel(*refs):
    sources, targets = refs[:4], refs[4:]
    each = 4 // len(targets)
    for index, ref in enumerate(sources):
        targets[index // each][index % each] = ref[...]


def gather_near(block):
    return [block] + [xor_permute(block, "narrow", k) for k in (1, 2, 3)]


def stack_near(near, parts):
    rows = near[0].shape[0]
    shapes = [jax.ShapeDtypeStruct((4 // parts, rows, LANES), BF16)] * parts
    return small_kernel(stack_kernel, near, shapes)


def gather_halves(first, second):
    first_y, second_x = xor_permute(first, "wide", 4), xor_permute(second, "wide", 2)
    first_x, second_y = xor_permute(first, "wide", 2), xor_permute(second, "wide", 4)
    first_xy, second_xy = xor_permute(first_y, "wide", 2), xor_permute(second_x, "wide", 4)
    own = [first, second, first_x, second_x, first_y, second_y, first_xy, second_xy]
    other = [xor_permute(piece, "wide", 1) for piece in own]
    pieces = []
    for index in range(4):
        pieces += [own[2 * index], own[2 * index + 1], other[2 * index], other[2 * index + 1]]
    return pieces


def gather_plane(stack):
    return [stack] + [xor_permute(stack, "wide", bit) for bit in (2, 4, 6)]


def gather_core(own):
    pieces = []
    for piece in own:
        pieces += [piece, xor_permute(piece, "wide", 1)]
    return pieces


def core_direct_kernel(keep_ref, got_ref, own_ref, *send_refs):
    total = keep_ref[...].astype(F32) + got_ref[...].astype(F32)
    own_ref[...] = total[0:4]
    for part, ref in enumerate(send_refs):
        ref[...] = total[4 * (part + 1) : 4 * (part + 2)].astype(BF16)


def plane_direct_kernel(own_ref, one_ref, two_ref, three_ref, keep_ref, *send_refs):
    total = own_ref[...]
    for ref in (one_ref, two_ref, three_ref):
        total = total + ref[...].astype(F32)
    keep_ref[...] = total[0]
    for part, ref in enumerate(send_refs):
        ref[...] = total[part + 1].astype(BF16)


def last_kernel(own_ref, one_ref, two_ref, three_ref, out_ref):
    total = own_ref[...]
    for ref in (one_ref, two_ref, three_ref):
        total = total + ref[...].astype(F32)
    out_ref[...] = total[: out_ref.shape[0]]


def last_head_kernel(
    me_ref, sums_ref, own_ref, one_ref, two_ref, three_ref, out_ref, total_ref
):
    last_kernel(own_ref, one_ref, two_ref, three_ref, out_ref)
    sums = sums_ref[...]
    for ref in (one_ref, two_ref, three_ref):
        sums = sums + got_sums(ref, sums.shape)
    total_ref[...] = sums
    put_head(me_ref, total_ref, out_ref)


def put_head(me_ref, sums_ref, out_ref):
    @pl.when(me_ref[0] == 0)
    def _():
        lanes = sums_ref.shape[1] // LANES
        for index in range(2 * lanes):
            part = slice(index % lanes * LANES, (index % lanes + 1) * LANES)
            row = index // lanes
            out_ref[index : index + 1, :] = sums_ref[row : row + 1, part]


def head_kernel(me_ref, sums_ref, block_ref, out_ref):
    out_ref[...] = block_ref[...]
    put_head(me_ref, sums_ref, out_ref)


def core_halves_kernel(
    keep_ref, got_ref, sums_ref, one_ref, two_ref, out_ref, send_one_ref, send_two_ref
):
    total = keep_ref[...].astype(F32) + got_ref[...].astype(F32)
    for x in range(2):
        for z in range(2):
            one_ref[2 * x + z] = total[4 * x + z]
            send_one_ref[2 * x + z] = total[8 + 4 * x + z].astype(BF16)
    for y in range(2):
        for z in range(2):
            two_ref[2 * y + z] = total[8 * y + 2 + z]
            send_two_ref[2 * y + z] = total[8 * y + 4 + 2 + z].astype(BF16)
    sums = sums_ref[...] + got_sums(got_ref.at[0], sums_ref.shape)
    out_ref[...] = sums
    send_sums(sums, [send_one_ref.at[0]])


def plane_halves_kernel(
    one_ref,
    two_ref,
    got_one_ref,
    got_two_ref,
    sums_ref,
    keep_one_ref,
    keep_two_ref,
    out_ref,
    send_one_ref,
    send_two_ref,
):
    for ref, got, keep, send in (
        (one_ref, got_one_ref, keep_one_ref, send_one_ref),
        (two_ref, got_two_ref, keep_two_ref, send_two_ref),
    ):
        total = ref[...] + got[...].astype(F32)
        keep[...] = total[0:2]
        send[...] = total[2:4].astype(BF16)
    sums = sums_ref[...] + got_sums(got_one_ref.at[0], sums_ref.shape)
    out_ref[...] = sums
    send_sums(sums, [send_one_ref.at[0]])


def near_halves_kernel(
    one_ref,
    two_ref,
    got_one_ref,
    got_two_ref,
    sums_ref,
    keep_ref,
    out_ref,
    send_one_ref,
    send_two_ref,
    send_three_ref,
):
    one = one_ref[...] + got_one_ref[...].astype(F32)
    two = two_ref[...] + got_two_ref[...].astype(F32)
    keep_ref[...] = one[0]
    send_one_ref[...] = one[1].astype(BF16)
    send_two_ref[...] = two[0].astype(BF16)
    send_three_ref[...] = two[1].astype(BF16)
    sums = sums_ref[...] + got_sums(got_one_ref.at[0], sums_ref.shape)
    out_ref[...] = sums
    send_sums(sums, [send_one_ref, send_two_ref, send_three_ref])


def scatter_plain(value):
    return lax.psum_scatter(value.astype(F32), AXES, scatter_dimension=0, tiled=True)[0]


def per_device(features, presence, first_params, second_params, cotangent):
    rows, width = features.shape
    lanes = width // LANES
    devices_all = count = lax.axis_size(AXES)
    total_rows = rows * devices_all
    cube = hypercube_ok()
    tile = math.gcd(rows, 256)
    half = rows // 2
    big = math.gcd(rows, 512)
    me = lax.axis_index(AXES).astype(jnp.int32).reshape(1)
    chunks = [first_params.shape[0] // LANES, second_params.shape[0] // LANES]
    extra = 6 * lanes
    shape = jax.ShapeDtypeStruct
    fields = presence.T
    blocks = [up(chunks[0], 16) + (16 if cube else 0), up(chunks[1], 16)]

    masked, block_one, block_two = run_kernel(
        stats_kernel,
        [
            me,
            features,
            fields,
            first_params.reshape(chunks[0], LANES),
            second_params.reshape(chunks[1], LANES),
        ],
        (
            pltpu.VMEM((rows, width), BF16),
            pltpu.VMEM((up(chunks[0] + extra, 16), LANES), BF16),
            pltpu.VMEM((blocks[1], LANES), BF16),
        ),
        [
            pltpu.VMEM((rows, width), BF16),
            pltpu.VMEM(fields.shape, jnp.int32),
            pltpu.VMEM((chunks[0], LANES), BF16),
            pltpu.VMEM((chunks[1], LANES), BF16),
            pltpu.SemaphoreType.DMA((4,)),
        ],
        60,
        rows * width * 10,
        spec=pl.BlockSpec(memory_space=pltpu.HBM),
    )
    if cube:
        origin = me
        near_one = gather_near(block_one)
        first, second = stack_near(near_one, 2)
        near_two = gather_near(after(block_two, first))
        pieces_one = gather_halves(first, second)
        near_two[3] = after(near_two[3], pieces_one[12], pieces_one[13])
        (stack_two,) = stack_near(near_two, 1)
        plane_two = gather_plane(after(stack_two, pieces_one[12], pieces_one[13]))
        masked = after(masked, stack_two)
    else:
        origin = jnp.zeros((1,), jnp.int32)
        pieces_one = [lax.all_gather(block_one, AXES)]
        plane_two = [lax.all_gather(block_two, AXES)]

    saved = run_kernel(
        functools.partial(level_one_forward, chunks[0], big, len(pieces_one)),
        [origin, masked] + pieces_one,
        [
            shape((rows, width), BF16),
            shape((6, rows, H), BF16),
            shape((6, rows, H), BF16),
            shape((6, rows, H), BF16),
            shape((6, rows, LANES), F32),
            shape((rows, LANES), F32),
            shape((3, rows, H), BF16),
            shape((width, 6 * H), BF16),
            shape((6, H, H), BF16),
            shape((4, 8, H), F32),
            shape((width, LANES), BF16),
            shape((8, width), F32),
        ],
        [
            pltpu.VMEM((count * chunks[0], LANES), F32),
            pltpu.VMEM((count, extra, LANES), F32),
            pltpu.VMEM((6, big, H), F32),
            pltpu.VMEM((big, 14 * LANES), F32),
            pltpu.VMEM((2 * LANES, 14 * LANES), BF16),
        ],
        28,
        rows * 6 * (width + H) * H * 2,
    )
    level, active, slope, normal, scale, probs, mixed, w_in, w_out, small, gate, entry = saved
    pieces_two = gather_core([after(piece, entry) for piece in plane_two]) if cube else plane_two

    outs = 2 if cube else 1
    towers, mixed_grad, *grads_two = run_kernel(
        functools.partial(level_two, count, chunks[1], tile, len(pieces_two), outs),
        [origin, mixed, cotangent] + pieces_two,
        [
            shape((rows, LANES), F32),
            shape((3, rows, H), F32),
        ]
        + [shape((count // outs, blocks[1], LANES), BF16)] * outs,
        [
            pltpu.VMEM((count * chunks[1], LANES), F32),
            pltpu.VMEM((H, 6 * H), BF16),
            pltpu.VMEM((6, H, H), BF16),
            pltpu.VMEM((4, 8, H), F32),
            pltpu.VMEM((H, LANES), BF16),
            pltpu.VMEM((2, H, TOWER1), BF16),
            pltpu.VMEM((2 * TOWER1, LANES), BF16),
            pltpu.VMEM((2 * TOWER1, LANES), F32),
            pltpu.VMEM((8, 2 * TOWER1), F32),
            pltpu.VMEM((4, 8, H), F32),
            pltpu.VMEM((2 * TOWER1, LANES), F32),
            pltpu.VMEM((8, 2 * TOWER1), F32),
            pltpu.VMEM((6, rows, H), BF16),
            pltpu.VMEM((tile, 6 * H), F32),
            pltpu.VMEM((6, tile, H), F32),
            pltpu.VMEM((6, tile, LANES), F32),
            pltpu.VMEM((6, tile, H), F32),
            pltpu.VMEM((2, rows, H), BF16),
            pltpu.VMEM((2, tile, H), F32),
            pltpu.VMEM((rows, 2 * TOWER1), BF16),
            pltpu.VMEM((rows, 2 * TOWER1), BF16),
            pltpu.VMEM((2, rows, LANES), BF16),
            pltpu.VMEM((6, rows, H), BF16),
            pltpu.VMEM((rows, 6 * H), BF16),
            pltpu.VMEM((tile, 8 * LANES), F32),
            pltpu.VMEM((2 * LANES, 8 * LANES), BF16),
            pltpu.VMEM((2 * H, 2 * LANES), BF16),
        ],
        32,
        rows * 6 * 2 * H * H * 2 * 3,
    )
    def backward(part, *before):
        return run_kernel(
            functools.partial(level_one_backward, math.gcd(big, half), part * half),
            [
                mixed_grad,
                masked,
                slope,
                normal,
                scale,
                probs,
                w_in,
                w_out,
                small,
                gate,
                entry,
                *before,
            ],
            [
                shape((half, width), F32),
                shape((8, width), F32),
                shape((4, 8, H), F32),
                shape((half, LANES), BF16),
                shape((6, half, H), BF16),
                shape((half, 6 * H), BF16),
            ],
            [
                pltpu.VMEM((math.gcd(big, half), 14 * LANES), F32),
                pltpu.VMEM((2 * LANES, 14 * LANES), BF16),
                pltpu.VMEM((2 * H, 2 * LANES), BF16),
            ],
            16,
            rows * 6 * (width + H) * H * 2,
            scalar=False,
        )

    grad_a, sums, g_small, logit_a, post_a, pre_a = backward(0)
    if cube:
        keep_two, send_two = grads_two
        own_two, *sends_two = small_kernel(
            core_direct_kernel,
            [after(keep_two, sums), xor_permute(send_two, "wide", 1)],
            [shape((4, blocks[1], LANES), F32)] + [shape((4, blocks[1], LANES), BF16)] * 3,
        )
        sums = after(sums, own_two)
    grad_b, sums, g_small, logit_b, post_b, pre_b = backward(1, sums, g_small)
    grads_one = run_kernel(
        functools.partial(level_one_weights, count, chunks[0]),
        [
            origin,
            level,
            active,
            sums,
            g_small,
            logit_a,
            logit_b,
            post_a,
            post_b,
            pre_a,
            pre_b,
        ],
        [shape((count // outs, blocks[0], LANES), BF16)] * outs,
        [pltpu.VMEM((count * chunks[0], LANES), F32)],
        12,
        rows * 6 * (width + H) * H * 2,
    )
    if cube:
        keep_two, *sends_two = small_kernel(
            plane_direct_kernel,
            [own_two]
            + [xor_permute(part, "wide", bit) for part, bit in zip(sends_two, (2, 4, 6))],
            [shape((blocks[1], LANES), F32)] + [shape((blocks[1], LANES), BF16)] * 3,
        )
        summed = shape((8, width), F32)
        low, high = shape((4, blocks[0], LANES), BF16), shape((4, blocks[0], LANES), F32)
        keep, send = grads_one
        one, two, sums, send_one, send_two = small_kernel(
            core_halves_kernel,
            [keep, xor_permute(after(send, keep_two), "wide", 1), sums],
            [high, high, summed, low, low],
        )
        second_grad = small_kernel(
            last_kernel,
            [keep_two]
            + [xor_permute(part, "narrow", k) for part, k in zip(sends_two, (1, 2, 3))],
            shape((chunks[1], LANES), F32),
        )
        low, high = shape((2, blocks[0], LANES), BF16), shape((2, blocks[0], LANES), F32)
        one, two, sums, send_one, send_two = small_kernel(
            plane_halves_kernel,
            [
                after(one, second_grad),
                two,
                xor_permute(send_one, "wide", 4),
                xor_permute(send_two, "wide", 2),
                sums,
            ],
            [high, high, summed, low, low],
        )
        low, high = shape((blocks[0], LANES), BF16), shape((blocks[0], LANES), F32)
        keep, sums, *sends = small_kernel(
            near_halves_kernel,
            [
                one,
                two,
                xor_permute(send_one, "wide", 2),
                xor_permute(send_two, "wide", 4),
                sums,
            ],
            [high, summed, low, low, low],
        )
        first_grad, sums = small_kernel(
            last_head_kernel,
            [me, sums, keep]
            + [xor_permute(part, "narrow", k) for part, k in zip(sends, (1, 2, 3))],
            [shape((chunks[0], LANES), F32), summed],
            scalar=True,
        )
    else:
        sums = lax.psum(sums, AXES)
        second_grad = scatter_plain(grads_two[0])[: chunks[1]]
        first_grad = small_kernel(
            head_kernel,
            [me, sums, scatter_plain(grads_one[0])[: chunks[0]]],
            shape((chunks[0], LANES), F32),
            scalar=True,
        )

    input_grad = run_kernel(
        functools.partial(input_kernel, float(total_rows)),
        [grad_a, grad_b, masked, fields, entry, sums],
        shape((rows, width), F32),
        [],
        8,
        rows * width * 10,
        scalar=False,
    )
    return (towers, input_grad, first_grad.reshape(-1), second_grad.reshape(-1))


def solution(mesh):
    placed = (
        P(AXES, None),
        P(AXES, None),
        P(AXES),
        P(AXES),
        P(AXES, None),
    )
    return jax.shard_map(
        per_device,
        mesh=mesh,
        in_specs=placed,
        out_specs=(P(AXES, None), P(AXES, None), P(AXES), P(AXES)),
        check_vma=False,
    )
```

```python
import functools
import math

import jax
import jax.numpy as jnp
from jax import lax
from jax.experimental import pallas as pl
from jax.experimental.pallas import tpu as pltpu
from jax.sharding import PartitionSpec as P

H = 256
TOWER1 = 128
TOWER2 = 64
LANES = 128
EPSILON = 1e-05
AXES = ("wide", "narrow")
F32 = jnp.float32
BF16 = jnp.bfloat16
GROUPS_ONE = ((0, 4), (4, 8), (8, 14))
MEMBERS_ONE = ((0, 1, 4, 5), (2, 3, 4, 5), (0, 1, 2, 3, 4, 5))
GROUPS_TWO = ((0, 4), (4, 8))
MEMBERS_TWO = ((0, 1, 4, 5), (2, 3, 4, 5))


def up(value, step):
    return -(-value // step) * step


def mm(left, right):
    return jnp.dot(left, right, preferred_element_type=F32)


def mm_nt(left, right):
    return lax.dot_general(left, right, (((1,), (1,)), ((), ())), preferred_element_type=F32)


def mm_tn(left, right):
    return lax.dot_general(left, right, (((0,), (0,)), ((), ())), preferred_element_type=F32)


def sigmoid(values):
    return 0.5 * jnp.tanh(0.5 * values) + 0.5


def group_softmax(logits, groups):
    lane = lax.broadcasted_iota(jnp.int32, logits.shape, 1)
    spread = jnp.zeros_like(logits)
    for low, high in groups:
        inside = (lane >= low) & (lane < high)
        peak = jnp.max(jnp.where(inside, logits, -jnp.inf), axis=1, keepdims=True)
        spread = jnp.where(inside, logits - peak, spread)
    raw = jnp.exp(spread)
    result = jnp.zeros_like(logits)
    for low, high in groups:
        inside = (lane >= low) & (lane < high)
        total = jnp.sum(jnp.where(inside, raw, 0.0), axis=1, keepdims=True)
        result = jnp.where(inside, raw / total, result)
    return result


def group_softmax_back(probs, grads, groups):
    lane = lax.broadcasted_iota(jnp.int32, probs.shape, 1)
    product = probs * grads
    result = jnp.zeros_like(probs)
    for low, high in groups:
        inside = (lane >= low) & (lane < high)
        total = jnp.sum(jnp.where(inside, product, 0.0), axis=1, keepdims=True)
        result = jnp.where(inside, product - probs * total, result)
    return result


def into_lane(columns):
    rows = columns[0].shape[0]
    lane = lax.broadcasted_iota(jnp.int32, (rows, LANES), 1)
    result = jnp.zeros((rows, LANES), F32)
    for position, column in enumerate(columns):
        result = jnp.where(lane == position, column, result)
    return result


def mix_parts(weights, low, members, outputs):
    running = None
    for position, member in enumerate(members):
        term = column_block(weights, low + position) * outputs[member]
        running = term if running is None else running + term
    return running


def row_sum(values):
    return jnp.sum(values, axis=1, keepdims=True)


def column_sum(values):
    return jnp.sum(values, axis=0, keepdims=True)


def norm_forward(post):
    centred = post - row_sum(post) * (1.0 / H)
    scale = lax.rsqrt(row_sum(centred * centred) * (1.0 / H) + EPSILON)
    return centred * scale, scale


def twice(values):
    return jnp.concatenate([values, values], axis=1)


def norm_backward(scaled, normal, scale, means):
    both = jnp.concatenate([scaled.astype(BF16), (scaled * normal).astype(BF16)], axis=1)
    mean = mm(both, means)
    return twice(scale) * (
        scaled - twice(mean[:, :LANES]) - normal * twice(mean[:, LANES:])
    )


def make_means():
    row = lax.broadcasted_iota(jnp.int32, (2 * H, 2 * LANES), 0)
    lane = lax.broadcasted_iota(jnp.int32, (2 * H, 2 * LANES), 1)
    return jnp.where((row < H) == (lane < LANES), 1.0 / H, 0.0).astype(BF16)


def make_spread(columns):
    row = lax.broadcasted_iota(jnp.int32, (2 * LANES, columns * LANES), 0)
    lane = lax.broadcasted_iota(jnp.int32, (2 * LANES, columns * LANES), 1)
    return jnp.where((row & (LANES - 1)) == (lane >> 7), 1.0, 0.0).astype(BF16)


def spread_columns(values, spread):
    high = values.astype(BF16)
    low = (values - high.astype(F32)).astype(BF16)
    return mm(jnp.concatenate([high, low], axis=1), spread)


def column_block(spread, column):
    return twice(spread[:, column * LANES : (column + 1) * LANES])


def first_layout(width):
    names = (
        ("in_gain", width),
        ("in_bias", width),
        ("expert_in", 6 * width * H),
        ("expert_in_bias", 6 * H),
        ("expert_out", 6 * H * H),
        ("expert_out_bias", 6 * H),
        ("norm_gain", 6 * H),
        ("norm_bias", 6 * H),
        ("gate", 14 * width),
    )
    return place_names(names)


def second_layout():
    names = (
        ("expert_in", 6 * H * H),
        ("expert_in_bias", 6 * H),
        ("expert_out", 6 * H * H),
        ("expert_out_bias", 6 * H),
        ("norm_gain", 6 * H),
        ("norm_bias", 6 * H),
        ("gate", 2 * H * 4),
        ("tower_in", 2 * H * TOWER1),
        ("tower_in_bias", 2 * TOWER1),
        ("tower_out", 2 * TOWER1 * TOWER2),
        ("tower_out_bias", 2 * TOWER2),
    )
    return place_names(names)


def place_names(names):
    rows = {}
    offset = 0
    for name, amount in names:
        rows[name] = offset // LANES
        offset += amount
    return rows, offset // LANES


def spread_pieces(me, rows, piece_refs, flat_ref, extra_ref=None):
    slot = 0
    for ref in piece_refs:
        for index in range(ref.shape[0]):
            owner = lax.bitwise_xor(me, jnp.int32(slot))
            block = ref[index].astype(F32)
            flat_ref[pl.ds(owner * rows, rows), :] = block[:rows]
            if extra_ref is not None:
                extra_ref[slot] = block[rows : rows + extra_ref.shape[1]]
            slot += 1


def wide_rows(flat_ref, row, amount):
    return jnp.concatenate(
        [flat_ref[pl.ds(row, amount, stride=2), :], flat_ref[pl.ds(row + 1, amount, stride=2), :]],
        axis=1,
    )


def put_wide_rows(flat_ref, row, amount, value):
    flat_ref[pl.ds(row, amount, stride=2), :] = value[:, :LANES]
    flat_ref[pl.ds(row + 1, amount, stride=2), :] = value[:, LANES:]


def collect_pieces(me, count, rows, flat_ref, out_refs):
    for slot in range(count):
        owner = lax.bitwise_xor(me, jnp.int32(slot))
        value = flat_ref[pl.ds(owner * rows, rows), :].astype(BF16)
        if len(out_refs) == 1:
            out_refs[0][slot, :rows, :] = value
        else:
            part, place = slot // 4 % 2, slot // 8 * 4 + slot % 4
            out_refs[part][place, :rows, :] = value


def roll_rows(value, columns, sign):
    item = lax.broadcasted_iota(jnp.int32, value.shape, 0)
    bit = 1
    while columns * bit % LANES:
        moved = pltpu.roll(value, sign * columns * bit % LANES, 1)
        value = jnp.where((item & bit) != 0, moved, value)
        bit *= 2
    return value


def table_places(width, columns, rows):
    item = lax.broadcasted_iota(jnp.int32, (width, rows), 0)
    index = lax.broadcasted_iota(jnp.int32, (width, rows), 1)
    first = (index == ((item * columns) >> 7)).astype(F32).astype(BF16)
    last = (index == ((item * columns + columns - 1) >> 7)).astype(F32).astype(BF16)
    item = lax.broadcasted_iota(jnp.int32, (width, LANES), 0)
    lane = lax.broadcasted_iota(jnp.int32, (width, LANES), 1)
    return first, last, lane >= ((item * columns) & (LANES - 1)), lane < columns


def table_from_rows(flat, width, columns):
    first, last, late, used = table_places(width, columns, flat.shape[0])
    chosen = jnp.where(late, mm(first, flat), mm(last, flat))
    return jnp.where(used, roll_rows(chosen, columns, -1), 0.0)


def rows_from_table(table, rows, columns):
    first, last, late, _ = table_places(table.shape[0], columns, rows)
    moved = roll_rows(table, columns, 1)
    return mm_tn(first, jnp.where(late, moved, 0.0).astype(BF16)) + mm_tn(
        last, jnp.where(late, 0.0, moved).astype(BF16)
    )


def full_spec():
    return pl.BlockSpec(memory_space=pltpu.VMEM)


def scalar_spec():
    return pl.BlockSpec(memory_space=pltpu.SMEM)


def run_kernel(
    kernel, inputs, out_shape, scratch, limit, flops, scalar=True, spec=None, out_spec=None
):
    specs = [spec or full_spec()] * len(inputs)
    if scalar:
        specs[0] = scalar_spec()
    several = isinstance(out_shape, (list, tuple))
    out_specs = [full_spec()] * len(out_shape) if several else out_spec or full_spec()
    return pl.pallas_call(
        kernel,
        in_specs=specs,
        out_specs=out_specs,
        out_shape=out_shape,
        scratch_shapes=scratch,
        compiler_params=pltpu.CompilerParams(vmem_limit_bytes=limit * 2**20),
        cost_estimate=pl.CostEstimate(flops=2**20, bytes_accessed=2**10, transcendentals=0),
    )(*inputs)


def spread_presence(presence, width):
    fields = presence.shape[0]
    field = lax.broadcasted_iota(jnp.int32, (fields, width), 0)
    column = lax.broadcasted_iota(jnp.int32, (fields, width), 1)
    pick = (column // (width // fields) == field).astype(F32).astype(BF16)
    return mm_tn(presence.astype(F32).astype(BF16), pick)


def split_three(values):
    parts = []
    for _ in range(3):
        part = values.astype(BF16).astype(F32)
        parts.append(part)
        values = values - part
    return parts


def stats_kernel(
    me_ref,
    features_hbm,
    presence_hbm,
    params_hbm,
    second_hbm,
    masked_ref,
    block_ref,
    block_two_ref,
    features_ref,
    presence_ref,
    params_ref,
    second_ref,
    sems,
):
    del me_ref
    copies = [
        pltpu.make_async_copy(source, target, sems.at[index])
        for index, (source, target) in enumerate(
            (
                (presence_hbm, presence_ref),
                (features_hbm, features_ref),
                (params_hbm, params_ref),
                (second_hbm, second_ref),
            )
        )
    ]
    for copy in copies:
        copy.start()
    for copy in copies:
        copy.wait()
    rows, width = features_ref.shape
    mask = spread_presence(presence_ref[...], width)
    masked = features_ref[...].astype(F32) * mask
    masked_ref[...] = masked.astype(BF16)
    mean = column_sum(masked) * (1.0 / rows)
    spread = masked - mean
    moment = column_sum(spread * spread)
    lines = [params_ref[...].astype(F32)]
    for value in (mean, moment):
        for part in split_three(value):
            for index in range(width // LANES):
                lines.append(part[:, index * LANES : (index + 1) * LANES])
    used = params_ref.shape[0] + 6 * (width // LANES)
    lines.append(jnp.zeros((block_ref.shape[0] - used, LANES), F32))
    block_ref[...] = jnp.concatenate(lines, axis=0).astype(BF16)
    second = second_ref[...].astype(F32)
    rest = jnp.zeros((block_two_ref.shape[0] - second.shape[0], LANES), F32)
    block_two_ref[...] = jnp.concatenate([second, rest], axis=0).astype(BF16)


def from_lanes(block):
    return jnp.concatenate([block[index : index + 1, :] for index in range(block.shape[0])], axis=1)


def tiles(tile):
    return lambda ref_rows, body: lax.fori_loop(
        0, ref_rows // tile, lambda step, carry: body(pl.multiple_of(step * tile, tile), carry), 0
    )


def in_turn(first, second):
    for e in range(7):
        if e < 6:
            first(e)
        if e > 0:
            second(e - 1)


def spot(e):
    return slice(e * H, (e + 1) * H)


def level_one_forward(
    rows,
    tile,
    n_pieces,
    me_ref,
    masked_ref,
    *rest,
):
    piece_refs = rest[:n_pieces]
    (
        level_ref,
        active_ref,
        slope_ref,
        normal_ref,
        scale_ref,
        probs_ref,
        mixed_ref,
        w_in_ref,
        w_out_ref,
        small_ref,
        gate_ref,
        entry_ref,
        flat_ref,
        extra_ref,
        output_ref,
        wide_ref,
        spread_ref,
    ) = rest[n_pieces:]
    width = masked_ref.shape[1]
    where_row, _ = first_layout(width)

    spread_pieces(me_ref[0], rows, piece_refs, flat_ref, extra_ref)
    spread_ref[...] = make_spread(14)
    for e in range(6):
        w_in_ref[:, spot(e)] = wide_rows(
            flat_ref, where_row["expert_in"] + e * 2 * width, width
        ).astype(BF16)
        w_out_ref[e] = wide_rows(flat_ref, where_row["expert_out"] + e * 2 * H, H).astype(BF16)
    for index, name in enumerate(("expert_in_bias", "expert_out_bias", "norm_gain", "norm_bias")):
        small_ref[index, :6, :] = wide_rows(flat_ref, where_row[name], 6)
    gate_flat = flat_ref[pl.ds(where_row["gate"], 14 * width // LANES), :].astype(BF16)
    gate_ref[...] = table_from_rows(gate_flat, width, 14).astype(BF16)
    lanes = width // LANES
    events = masked_ref.shape[0]
    count = extra_ref.shape[0]
    means = extra_ref[:, 0:lanes, :]
    for part in (1, 2):
        means = means + extra_ref[:, part * lanes : (part + 1) * lanes, :]
    mean = jnp.sum(means, axis=0) * (1.0 / count)
    away = jnp.sum(jnp.square(means - mean[None]), axis=0) * events
    for part in (3, 4, 5):
        away = away + jnp.sum(extra_ref[:, part * lanes : (part + 1) * lanes, :], axis=0)
    entry_ref[0:1, :] = from_lanes(mean)
    entry_ref[1:2, :] = from_lanes(lax.rsqrt(away * (1.0 / (events * count)) + EPSILON))
    entry_ref[2:3, :] = from_lanes(flat_ref[0:lanes, :])
    entry_ref[3:4, :] = from_lanes(flat_ref[lanes : 2 * lanes, :])

    def body(start, carry):
        now = pl.ds(start, tile)
        normed = (masked_ref[now, :].astype(F32) - entry_ref[0:1, :]) * entry_ref[1:2, :]
        level_ref[now, :] = (normed * entry_ref[2:3, :] + entry_ref[3:4, :]).astype(BF16)
        probs_ref[now, :] = group_softmax(mm(level_ref[now, :], gate_ref[...]), GROUPS_ONE)
        def first_half(e):
            pre = mm(level_ref[now, :], w_in_ref[:, spot(e)]) + small_ref[0, e : e + 1, :]
            gate = sigmoid(pre)
            silu = pre * gate
            active_ref[e, now, :] = silu.astype(BF16)
            slope_ref[e, now, :] = (gate + silu * (1.0 - gate)).astype(BF16)

        def second_half(e):
            post = mm(active_ref[e, now, :], w_out_ref[e]) + small_ref[1, e : e + 1, :]
            normal, scale = norm_forward(post)
            normal_ref[e, now, :] = normal.astype(BF16)
            scale_ref[e, now, :] = jnp.broadcast_to(scale, (tile, LANES))
            output_ref[e] = normal * small_ref[2, e : e + 1, :] + small_ref[3, e : e + 1, :]

        in_turn(first_half, second_half)
        wide_ref[...] = spread_columns(probs_ref[now, :], spread_ref[...])
        for index, (low, _) in enumerate(GROUPS_ONE):
            mixed_ref[index, now, :] = mix_parts(
                wide_ref, low, MEMBERS_ONE[index], output_ref
            ).astype(BF16)
        return carry

    tiles(tile)(masked_ref.shape[0], body)


def level_two(count, rows, tile, n_pieces, n_outs, me_ref, mixed_ref, cotangent_ref, *rest):
    piece_refs = rest[:n_pieces]
    grads_refs = rest[n_pieces + 2 : n_pieces + 2 + n_outs]
    towers_ref, mixed_grad_ref = rest[n_pieces : n_pieces + 2]
    (
        flat_ref,
        w_in_ref,
        w_out_ref,
        small_ref,
        gate_ref,
        tower_in_ref,
        tower_out_ref,
        tower_tmp_ref,
        tower_small_ref,
        g_small_ref,
        g_tower_out_ref,
        g_tower_small_ref,
        active_ref,
        slope_ref,
        normal_ref,
        scale_ref,
        output_ref,
        combined_ref,
        combined_grad_ref,
        tower_active_ref,
        tower_grad_ref,
        logit_ref,
        post_grad_ref,
        pre_grad_ref,
        wide_ref,
        spread_ref,
        means_ref,
    ) = rest[n_pieces + 2 + n_outs :]
    where_row, used_rows = second_layout()
    all_rows = mixed_ref.shape[1]

    spread_pieces(me_ref[0], rows, piece_refs, flat_ref)
    spread_ref[...] = make_spread(8)
    means_ref[...] = make_means()
    for e in range(6):
        w_in_ref[:, spot(e)] = wide_rows(flat_ref, where_row["expert_in"] + e * 2 * H, H).astype(
            BF16
        )
        w_out_ref[e] = wide_rows(flat_ref, where_row["expert_out"] + e * 2 * H, H).astype(BF16)
    for index, name in enumerate(("expert_in_bias", "expert_out_bias", "norm_gain", "norm_bias")):
        small_ref[index, :6, :] = wide_rows(flat_ref, where_row[name], 6)
    gate_rows = H * 4 // LANES
    shift_a = lax.broadcasted_iota(jnp.int32, (LANES, LANES), 0)
    shift_b = lax.broadcasted_iota(jnp.int32, (LANES, LANES), 1)
    shift = ((shift_a + 4 == shift_b) & (shift_a < 4)).astype(F32).astype(BF16)
    tables = []
    for task in range(2):
        piece = flat_ref[pl.ds(where_row["gate"] + task * gate_rows, gate_rows), :].astype(BF16)
        tables.append(table_from_rows(piece, H, 4).astype(BF16))
    gate_ref[...] = (tables[0].astype(F32) + mm(tables[1], shift)).astype(BF16)
    zero = jnp.zeros((TOWER1 // 2, TOWER2), F32)
    for task in range(2):
        tower_in_ref[task] = flat_ref[pl.ds(where_row["tower_in"] + task * H, H), :].astype(BF16)
        packed = flat_ref[pl.ds(where_row["tower_out"] + task * TOWER1 // 2, TOWER1 // 2), :]
        for half in range(2):
            pair = [packed[:, half * TOWER2 : (half + 1) * TOWER2], zero]
            if task == 1:
                pair.reverse()
            tower_tmp_ref[pl.ds(task * TOWER1 + half, TOWER1 // 2, stride=2), :] = jnp.concatenate(
                pair, axis=1
            )
    tower_out_ref[...] = tower_tmp_ref[...].astype(BF16)
    tower_small_ref[0:1, :] = from_lanes(flat_ref[pl.ds(where_row["tower_in_bias"], 2), :])
    tower_small_ref[1:2, :LANES] = flat_ref[pl.ds(where_row["tower_out_bias"], 1), :]
    g_small_ref[...] = jnp.zeros(g_small_ref.shape, F32)
    g_tower_small_ref[...] = jnp.zeros(g_tower_small_ref.shape, F32)

    def body(start, carry):
        now = pl.ds(start, tile)
        lane = lax.broadcasted_iota(jnp.int32, (tile, LANES), 1)
        def first_half(e):
            pre = mm(mixed_ref[e // 2, now, :], w_in_ref[:, spot(e)]) + small_ref[0, e : e + 1, :]
            gate = sigmoid(pre)
            silu = pre * gate
            active_ref[e, now, :] = silu.astype(BF16)
            slope_ref[:, spot(e)] = gate + silu * (1.0 - gate)

        def second_half(e):
            post = mm(active_ref[e, now, :], w_out_ref[e]) + small_ref[1, e : e + 1, :]
            normal, scale = norm_forward(post)
            normal_ref[e] = normal
            scale_ref[e] = jnp.broadcast_to(scale, (tile, LANES))
            output_ref[e] = normal * small_ref[2, e : e + 1, :] + small_ref[3, e : e + 1, :]

        in_turn(first_half, second_half)
        logits = jnp.where(
            lane < 4, mm(mixed_ref[0, now, :], gate_ref[...]), mm(mixed_ref[1, now, :], gate_ref[...])
        )
        probs = group_softmax(logits, GROUPS_TWO)
        wide_ref[...] = spread_columns(probs, spread_ref[...])
        for task in range(2):
            combined_ref[task, now, :] = mix_parts(
                wide_ref, 4 * task, MEMBERS_TWO[task], output_ref
            ).astype(BF16)
        tower_pre = (
            jnp.concatenate(
                [mm(combined_ref[task, now, :], tower_in_ref[task]) for task in range(2)], axis=1
            )
            + tower_small_ref[0:1, :]
        )
        tower_gate = sigmoid(tower_pre)
        tower_silu = tower_pre * tower_gate
        tower_active_ref[now, :] = tower_silu.astype(BF16)
        towers_ref[now, :] = (
            mm(tower_active_ref[now, :], tower_out_ref[...]) + tower_small_ref[1:2, :LANES]
        )
        cotangent = cotangent_ref[now, :]
        g_tower_small_ref[1:2, :LANES] += column_sum(cotangent.astype(F32))
        tower_slope = tower_gate + tower_silu * (1.0 - tower_gate)
        tower_grad = (mm_nt(cotangent, tower_out_ref[...]) * tower_slope).astype(BF16)
        tower_grad_ref[now, :] = tower_grad
        g_tower_small_ref[0:1, :] += column_sum(tower_grad.astype(F32))
        for task in range(2):
            combined_grad_ref[task] = mm_nt(
                tower_grad_ref[now, task * TOWER1 : (task + 1) * TOWER1], tower_in_ref[task]
            )
        prob_grads = into_lane(
            [
                row_sum(combined_grad_ref[task] * output_ref[member])
                for task in range(2)
                for member in MEMBERS_TWO[task]
            ]
        )
        logit_grad = group_softmax_back(probs, prob_grads, GROUPS_TWO)
        logit_ref[0, now, :] = jnp.where(lane < 4, logit_grad, 0.0).astype(BF16)
        logit_ref[1, now, :] = jnp.where((lane >= 4) & (lane < 8), logit_grad, 0.0).astype(BF16)
        def norm_half(e):
            out_grad = None
            for task in range(2):
                if e in MEMBERS_TWO[task]:
                    column = 4 * task + MEMBERS_TWO[task].index(e)
                    term = column_block(wide_ref, column) * combined_grad_ref[task]
                    out_grad = term if out_grad is None else out_grad + term
            normal = normal_ref[e]
            g_small_ref[2, e : e + 1, :] += column_sum(out_grad * normal)
            g_small_ref[3, e : e + 1, :] += column_sum(out_grad)
            post_grad = norm_backward(
                out_grad * small_ref[2, e : e + 1, :], normal, scale_ref[e], means_ref[...]
            )
            post_grad_ref[e, now, :] = post_grad.astype(BF16)
            g_small_ref[1, e : e + 1, :] += column_sum(post_grad)

        def active_half(e):
            act_grad = mm_nt(post_grad_ref[e, now, :], w_out_ref[e])
            pre_grad = act_grad * slope_ref[:, spot(e)]
            pre_grad_ref[now, spot(e)] = pre_grad.astype(BF16)
            g_small_ref[0, e : e + 1, :] += column_sum(pre_grad)

        in_turn(norm_half, active_half)
        for index in range(3):
            pair = slice(2 * index * H, 2 * (index + 1) * H)
            grad = mm_nt(pre_grad_ref[now, pair], w_in_ref[:, pair])
            if index < 2:
                grad = grad + mm_nt(logit_ref[index, now, :], gate_ref[...])
            mixed_grad_ref[index, now, :] = grad
        return carry

    tiles(tile)(all_rows, body)

    for e in range(6):
        put_wide_rows(
            flat_ref,
            where_row["expert_in"] + e * 2 * H,
            H,
            mm_tn(mixed_ref[e // 2], pre_grad_ref[:, spot(e)]),
        )
        put_wide_rows(
            flat_ref,
            where_row["expert_out"] + e * 2 * H,
            H,
            mm_tn(active_ref[e], post_grad_ref[e]),
        )
    for index, name in enumerate(("expert_in_bias", "expert_out_bias", "norm_gain", "norm_bias")):
        put_wide_rows(flat_ref, where_row[name], 6, g_small_ref[index, :6, :])
    back = ((shift_a == shift_b + 4) & (shift_b < 4)).astype(F32).astype(BF16)
    tables = [mm_tn(mixed_ref[task], logit_ref[task]) for task in range(2)]
    tables[1] = mm(tables[1].astype(BF16), back)
    g_tower_out_ref[...] = mm_tn(tower_active_ref[...], cotangent_ref[...])
    for task in range(2):
        flat_ref[pl.ds(where_row["gate"] + task * gate_rows, gate_rows), :] = rows_from_table(
            tables[task], gate_rows, 4
        )
        flat_ref[pl.ds(where_row["tower_in"] + task * H, H), :] = mm_tn(
            combined_ref[task], tower_grad_ref[:, task * TOWER1 : (task + 1) * TOWER1]
        )
        flat_ref[pl.ds(where_row["tower_out"] + task * TOWER1 // 2, TOWER1 // 2), :] = (
            jnp.concatenate(
                [
                    g_tower_out_ref[pl.ds(task * TOWER1 + half, TOWER1 // 2, stride=2), :][
                        :, task * TOWER2 : (task + 1) * TOWER2
                    ]
                    for half in range(2)
                ],
                axis=1,
            )
        )
        flat_ref[pl.ds(where_row["tower_in_bias"] + task, 1), :] = g_tower_small_ref[
            0:1, task * TOWER1 : (task + 1) * TOWER1
        ]
    flat_ref[pl.ds(where_row["tower_out_bias"], 1), :] = g_tower_small_ref[1:2, :LANES]
    if used_rows < count * rows:
        flat_ref[pl.ds(used_rows, count * rows - used_rows), :] = jnp.zeros(
            (count * rows - used_rows, LANES), F32
        )
    collect_pieces(me_ref[0], count, rows, flat_ref, grads_refs)


def level_one_backward(
    tile,
    begin,
    mixed_grad_ref,
    masked_ref,
    slope_ref,
    normal_ref,
    scale_ref,
    probs_ref,
    w_in_ref,
    w_out_ref,
    small_ref,
    gate_ref,
    entry_ref,
    *rest,
):
    if begin:
        before_sum_ref, before_small_ref, *rest = rest
    (
        level_grad_ref,
        g_sum_ref,
        g_small_ref,
        logit_ref,
        post_grad_ref,
        pre_grad_ref,
        wide_ref,
        spread_ref,
        means_ref,
    ) = rest
    spread_ref[...] = make_spread(14)
    means_ref[...] = make_means()
    if begin:
        g_small_ref[...] = before_small_ref[...]
        g_sum_ref[...] = before_sum_ref[...]
    else:
        g_small_ref[...] = jnp.zeros(g_small_ref.shape, F32)
        g_sum_ref[...] = jnp.zeros(g_sum_ref.shape, F32)

    def body(start, carry):
        here = pl.ds(start, tile)
        now = pl.ds(begin + start, tile)
        probs = probs_ref[now, :]
        wide_ref[...] = spread_columns(probs, spread_ref[...])
        columns = [None] * 14
        for e in range(6):
            output = (
                normal_ref[e, now, :].astype(F32) * small_ref[2, e : e + 1, :]
                + small_ref[3, e : e + 1, :]
            )
            for index, (low, _) in enumerate(GROUPS_ONE):
                if e in MEMBERS_ONE[index]:
                    columns[low + MEMBERS_ONE[index].index(e)] = row_sum(
                        mixed_grad_ref[index, now, :] * output
                    )
        logit_ref[here, :] = group_softmax_back(probs, into_lane(columns), GROUPS_ONE).astype(BF16)
        def norm_half(e):
            normal = normal_ref[e, now, :].astype(F32)
            out_grad = None
            for index, (low, _) in enumerate(GROUPS_ONE):
                if e in MEMBERS_ONE[index]:
                    column = low + MEMBERS_ONE[index].index(e)
                    term = column_block(wide_ref, column) * mixed_grad_ref[index, now, :]
                    out_grad = term if out_grad is None else out_grad + term
            g_small_ref[2, e : e + 1, :] += column_sum(out_grad * normal)
            g_small_ref[3, e : e + 1, :] += column_sum(out_grad)
            post_grad = norm_backward(
                out_grad * small_ref[2, e : e + 1, :],
                normal,
                scale_ref[e, now, :],
                means_ref[...],
            )
            post_grad_ref[e, here, :] = post_grad.astype(BF16)
            g_small_ref[1, e : e + 1, :] += column_sum(post_grad)

        def active_half(e):
            act_grad = mm_nt(post_grad_ref[e, here, :], w_out_ref[e])
            pre_grad = act_grad * slope_ref[e, now, :].astype(F32)
            pre_grad_ref[here, spot(e)] = pre_grad.astype(BF16)
            g_small_ref[0, e : e + 1, :] += column_sum(pre_grad)

        in_turn(norm_half, active_half)
        level_grad = mm_nt(pre_grad_ref[here, :], w_in_ref[...]) + mm_nt(
            logit_ref[here, :], gate_ref[...]
        )
        level_grad_ref[here, :] = level_grad
        normed = (masked_ref[now, :].astype(F32) - entry_ref[0:1, :]) * entry_ref[1:2, :]
        g_sum_ref[0:1, :] += column_sum(level_grad * normed)
        g_sum_ref[1:2, :] += column_sum(level_grad)
        return carry

    tiles(tile)(logit_ref.shape[0], body)


def send_sums(sums, block_refs):
    high = sums.astype(BF16).astype(F32)
    lines = []
    for value in (high, sums - high):
        for row in range(2):
            for index in range(value.shape[1] // LANES):
                lines.append(value[row : row + 1, index * LANES : (index + 1) * LANES])
    block = jnp.concatenate(lines, axis=0).astype(BF16)
    for ref in block_refs:
        ref[ref.shape[0] - 16 :, :] = block


def got_sums(block_ref, shape):
    rows = block_ref.shape[0]
    block = block_ref[rows - 16 :, :].astype(F32)
    block = block[:8] + block[8:]
    lanes = shape[1] // LANES
    lines = [from_lanes(block[row * lanes : (row + 1) * lanes]) for row in range(2)]
    return jnp.concatenate(lines + [jnp.zeros((shape[0] - 2, shape[1]), F32)], axis=0)


def level_one_weights(
    count,
    rows,
    me_ref,
    level_ref,
    active_ref,
    sums_ref,
    small_ref,
    logit_a_ref,
    logit_b_ref,
    post_a_ref,
    post_b_ref,
    pre_a_ref,
    pre_b_ref,
    *rest,
):
    *grads_refs, flat_ref = rest
    width = level_ref.shape[1]
    lanes = width // LANES
    where_row, used_rows = first_layout(width)
    half = logit_a_ref.shape[0]
    one, two = slice(0, half), slice(half, level_ref.shape[0])
    for e in range(6):
        put_wide_rows(
            flat_ref,
            where_row["expert_in"] + e * 2 * width,
            width,
            mm_tn(level_ref[one, :], pre_a_ref[:, spot(e)])
            + mm_tn(level_ref[two, :], pre_b_ref[:, spot(e)]),
        )
        put_wide_rows(
            flat_ref,
            where_row["expert_out"] + e * 2 * H,
            H,
            mm_tn(active_ref[e, one, :], post_a_ref[e])
            + mm_tn(active_ref[e, two, :], post_b_ref[e]),
        )
    for index, name in enumerate(("expert_in_bias", "expert_out_bias", "norm_gain", "norm_bias")):
        put_wide_rows(flat_ref, where_row[name], 6, small_ref[index, :6, :])
    gate_rows = 14 * width // LANES
    gate = mm_tn(level_ref[one, :], logit_a_ref[...]) + mm_tn(level_ref[two, :], logit_b_ref[...])
    flat_ref[pl.ds(where_row["gate"], gate_rows), :] = rows_from_table(gate, gate_rows, 14)
    flat_ref[0 : 2 * lanes, :] = jnp.zeros((2 * lanes, LANES), F32)
    if used_rows < count * rows:
        flat_ref[pl.ds(used_rows, count * rows - used_rows), :] = jnp.zeros(
            (count * rows - used_rows, LANES), F32
        )
    collect_pieces(me_ref[0], count, rows, flat_ref, grads_refs)
    if len(grads_refs) > 1:
        send_sums(sums_ref[...], [grads_refs[1].at[0]])


def input_kernel(
    total_rows,
    parts,
    grad_a_ref,
    grad_b_ref,
    masked_ref,
    presence_ref,
    entry_ref,
    sums_ref,
    out_hbm,
    out_ref,
    sems,
):
    rows, width = masked_ref.shape
    inv_scale = entry_ref[1:2, :]
    factor = inv_scale * entry_ref[2:3, :]
    cross = sums_ref[0:1, :] * (1.0 / total_rows)
    plain = sums_ref[1:2, :] * (1.0 / total_rows)
    each = rows // parts
    copies = []
    for part in range(parts):
        now = pl.ds(part * each, each)
        ref = grad_a_ref if part < parts // 2 else grad_b_ref
        grad = ref[pl.ds(part % (parts // 2) * each, each), :]
        mask = spread_presence(presence_ref[:, now], width)
        normed = (masked_ref[now, :].astype(F32) - entry_ref[0:1, :]) * inv_scale
        out_ref[now, :] = mask * (factor * (grad - plain - normed * cross))
        copies.append(pltpu.make_async_copy(out_ref.at[now], out_hbm.at[now], sems.at[part]))
        copies[-1].start()
    for copy in copies:
        copy.wait()


def xor_permute(value, axis, bit):
    size = lax.axis_size(axis)
    return lax.ppermute(value, axis, [(index, index ^ bit) for index in range(size)])


def hypercube_ok():
    wide, narrow = lax.axis_size("wide"), lax.axis_size("narrow")
    return wide == 8 and narrow == 4


def after(value, *others):
    return lax.optimization_barrier((value, *others))[0]


def small_kernel(kernel, inputs, out_shape, scalar=False):
    return run_kernel(kernel, inputs, out_shape, [], 8, 2**20, scalar=scalar)


def stack_kernel(*refs):
    sources, targets = refs[:4], refs[4:]
    each = 4 // len(targets)
    for index, ref in enumerate(sources):
        targets[index // each][index % each] = ref[...]


def gather_near(block):
    return [block] + [xor_permute(block, "narrow", k) for k in (1, 2, 3)]


def stack_near(near, parts):
    rows = near[0].shape[0]
    shapes = [jax.ShapeDtypeStruct((4 // parts, rows, LANES), BF16)] * parts
    return small_kernel(stack_kernel, near, shapes)


def gather_halves(first, second):
    first_y, second_x = xor_permute(first, "wide", 4), xor_permute(second, "wide", 2)
    first_x, second_y = xor_permute(first, "wide", 2), xor_permute(second, "wide", 4)
    first_xy, second_xy = xor_permute(first_y, "wide", 2), xor_permute(second_x, "wide", 4)
    own = [first, second, first_x, second_x, first_y, second_y, first_xy, second_xy]
    other = [xor_permute(piece, "wide", 1) for piece in own]
    pieces = []
    for index in range(4):
        pieces += [own[2 * index], own[2 * index + 1], other[2 * index], other[2 * index + 1]]
    return pieces


def gather_plane(stack):
    return [stack] + [xor_permute(stack, "wide", bit) for bit in (2, 4, 6)]


def gather_core(own):
    pieces = []
    for piece in own:
        pieces += [piece, xor_permute(piece, "wide", 1)]
    return pieces


def core_direct_kernel(keep_ref, got_ref, own_ref, *send_refs):
    total = keep_ref[...].astype(F32) + got_ref[...].astype(F32)
    own_ref[...] = total[0:4]
    for part, ref in enumerate(send_refs):
        ref[...] = total[4 * (part + 1) : 4 * (part + 2)].astype(BF16)


def plane_direct_kernel(own_ref, one_ref, two_ref, three_ref, keep_ref, *send_refs):
    total = own_ref[...]
    for ref in (one_ref, two_ref, three_ref):
        total = total + ref[...].astype(F32)
    keep_ref[...] = total[0]
    for part, ref in enumerate(send_refs):
        ref[...] = total[part + 1].astype(BF16)


def last_kernel(own_ref, one_ref, two_ref, three_ref, out_ref):
    total = own_ref[...]
    for ref in (one_ref, two_ref, three_ref):
        total = total + ref[...].astype(F32)
    out_ref[...] = total[: out_ref.shape[0]]


def last_head_kernel(
    me_ref, sums_ref, own_ref, one_ref, two_ref, three_ref, out_ref, total_ref
):
    last_kernel(own_ref, one_ref, two_ref, three_ref, out_ref)
    sums = sums_ref[...]
    for ref in (one_ref, two_ref, three_ref):
        sums = sums + got_sums(ref, sums.shape)
    total_ref[...] = sums
    put_head(me_ref, total_ref, out_ref)


def put_head(me_ref, sums_ref, out_ref):
    @pl.when(me_ref[0] == 0)
    def _():
        lanes = sums_ref.shape[1] // LANES
        for index in range(2 * lanes):
            part = slice(index % lanes * LANES, (index % lanes + 1) * LANES)
            row = index // lanes
            out_ref[index : index + 1, :] = sums_ref[row : row + 1, part]


def head_kernel(me_ref, sums_ref, block_ref, out_ref):
    out_ref[...] = block_ref[...]
    put_head(me_ref, sums_ref, out_ref)


def core_halves_kernel(
    keep_ref, got_ref, sums_ref, one_ref, two_ref, out_ref, send_one_ref, send_two_ref
):
    total = keep_ref[...].astype(F32) + got_ref[...].astype(F32)
    for x in range(2):
        for z in range(2):
            one_ref[2 * x + z] = total[4 * x + z]
            send_one_ref[2 * x + z] = total[8 + 4 * x + z].astype(BF16)
    for y in range(2):
        for z in range(2):
            two_ref[2 * y + z] = total[8 * y + 2 + z]
            send_two_ref[2 * y + z] = total[8 * y + 4 + 2 + z].astype(BF16)
    sums = sums_ref[...] + got_sums(got_ref.at[0], sums_ref.shape)
    out_ref[...] = sums
    send_sums(sums, [send_one_ref.at[0]])


def plane_halves_kernel(
    one_ref,
    two_ref,
    got_one_ref,
    got_two_ref,
    sums_ref,
    keep_one_ref,
    keep_two_ref,
    out_ref,
    send_one_ref,
    send_two_ref,
):
    for ref, got, keep, send in (
        (one_ref, got_one_ref, keep_one_ref, send_one_ref),
        (two_ref, got_two_ref, keep_two_ref, send_two_ref),
    ):
        total = ref[...] + got[...].astype(F32)
        keep[...] = total[0:2]
        send[...] = total[2:4].astype(BF16)
    sums = sums_ref[...] + got_sums(got_one_ref.at[0], sums_ref.shape)
    out_ref[...] = sums
    send_sums(sums, [send_one_ref.at[0]])


def near_halves_kernel(
    one_ref,
    two_ref,
    got_one_ref,
    got_two_ref,
    sums_ref,
    keep_ref,
    out_ref,
    send_one_ref,
    send_two_ref,
    send_three_ref,
):
    one = one_ref[...] + got_one_ref[...].astype(F32)
    two = two_ref[...] + got_two_ref[...].astype(F32)
    keep_ref[...] = one[0]
    send_one_ref[...] = one[1].astype(BF16)
    send_two_ref[...] = two[0].astype(BF16)
    send_three_ref[...] = two[1].astype(BF16)
    sums = sums_ref[...] + got_sums(got_one_ref.at[0], sums_ref.shape)
    out_ref[...] = sums
    send_sums(sums, [send_one_ref, send_two_ref, send_three_ref])


def scatter_plain(value):
    return lax.psum_scatter(value.astype(F32), AXES, scatter_dimension=0, tiled=True)[0]


def per_device(features, presence, first_params, second_params, cotangent):
    rows, width = features.shape
    lanes = width // LANES
    devices_all = count = lax.axis_size(AXES)
    total_rows = rows * devices_all
    cube = hypercube_ok()
    tile = math.gcd(rows, 256)
    half = rows // 2
    big = math.gcd(rows, 512)
    me = lax.axis_index(AXES).astype(jnp.int32).reshape(1)
    chunks = [first_params.shape[0] // LANES, second_params.shape[0] // LANES]
    extra = 6 * lanes
    shape = jax.ShapeDtypeStruct
    fields = presence.T
    blocks = [up(chunks[0], 16) + (16 if cube else 0), up(chunks[1], 16)]

    masked, block_one, block_two = run_kernel(
        stats_kernel,
        [
            me,
            features,
            fields,
            first_params.reshape(chunks[0], LANES),
            second_params.reshape(chunks[1], LANES),
        ],
        (
            pltpu.VMEM((rows, width), BF16),
            pltpu.VMEM((up(chunks[0] + extra, 16), LANES), BF16),
            pltpu.VMEM((blocks[1], LANES), BF16),
        ),
        [
            pltpu.VMEM((rows, width), BF16),
            pltpu.VMEM(fields.shape, jnp.int32),
            pltpu.VMEM((chunks[0], LANES), BF16),
            pltpu.VMEM((chunks[1], LANES), BF16),
            pltpu.SemaphoreType.DMA((4,)),
        ],
        60,
        rows * width * 10,
        spec=pl.BlockSpec(memory_space=pltpu.HBM),
    )
    if cube:
        origin = me
        near_one = gather_near(block_one)
        first, second = stack_near(near_one, 2)
        near_two = gather_near(after(block_two, first))
        pieces_one = gather_halves(first, second)
        near_two[3] = after(near_two[3], pieces_one[12], pieces_one[13])
        (stack_two,) = stack_near(near_two, 1)
        plane_two = gather_plane(after(stack_two, pieces_one[12], pieces_one[13]))
        masked = after(masked, stack_two)
    else:
        origin = jnp.zeros((1,), jnp.int32)
        pieces_one = [lax.all_gather(block_one, AXES)]
        plane_two = [lax.all_gather(block_two, AXES)]

    saved = run_kernel(
        functools.partial(level_one_forward, chunks[0], big, len(pieces_one)),
        [origin, masked] + pieces_one,
        [
            shape((rows, width), BF16),
            shape((6, rows, H), BF16),
            shape((6, rows, H), BF16),
            shape((6, rows, H), BF16),
            shape((6, rows, LANES), F32),
            shape((rows, LANES), F32),
            shape((3, rows, H), BF16),
            shape((width, 6 * H), BF16),
            shape((6, H, H), BF16),
            shape((4, 8, H), F32),
            shape((width, LANES), BF16),
            shape((8, width), F32),
        ],
        [
            pltpu.VMEM((count * chunks[0], LANES), F32),
            pltpu.VMEM((count, extra, LANES), F32),
            pltpu.VMEM((6, big, H), F32),
            pltpu.VMEM((big, 14 * LANES), F32),
            pltpu.VMEM((2 * LANES, 14 * LANES), BF16),
        ],
        28,
        rows * 6 * (width + H) * H * 2,
    )
    level, active, slope, normal, scale, probs, mixed, w_in, w_out, small, gate, entry = saved
    pieces_two = gather_core([after(piece, entry) for piece in plane_two]) if cube else plane_two

    outs = 2 if cube else 1
    towers, mixed_grad, *grads_two = run_kernel(
        functools.partial(level_two, count, chunks[1], tile, len(pieces_two), outs),
        [origin, mixed, cotangent] + pieces_two,
        [
            shape((rows, LANES), F32),
            shape((3, rows, H), F32),
        ]
        + [shape((count // outs, blocks[1], LANES), BF16)] * outs,
        [
            pltpu.VMEM((count * chunks[1], LANES), F32),
            pltpu.VMEM((H, 6 * H), BF16),
            pltpu.VMEM((6, H, H), BF16),
            pltpu.VMEM((4, 8, H), F32),
            pltpu.VMEM((H, LANES), BF16),
            pltpu.VMEM((2, H, TOWER1), BF16),
            pltpu.VMEM((2 * TOWER1, LANES), BF16),
            pltpu.VMEM((2 * TOWER1, LANES), F32),
            pltpu.VMEM((8, 2 * TOWER1), F32),
            pltpu.VMEM((4, 8, H), F32),
            pltpu.VMEM((2 * TOWER1, LANES), F32),
            pltpu.VMEM((8, 2 * TOWER1), F32),
            pltpu.VMEM((6, rows, H), BF16),
            pltpu.VMEM((tile, 6 * H), F32),
            pltpu.VMEM((6, tile, H), F32),
            pltpu.VMEM((6, tile, LANES), F32),
            pltpu.VMEM((6, tile, H), F32),
            pltpu.VMEM((2, rows, H), BF16),
            pltpu.VMEM((2, tile, H), F32),
            pltpu.VMEM((rows, 2 * TOWER1), BF16),
            pltpu.VMEM((rows, 2 * TOWER1), BF16),
            pltpu.VMEM((2, rows, LANES), BF16),
            pltpu.VMEM((6, rows, H), BF16),
            pltpu.VMEM((rows, 6 * H), BF16),
            pltpu.VMEM((tile, 8 * LANES), F32),
            pltpu.VMEM((2 * LANES, 8 * LANES), BF16),
            pltpu.VMEM((2 * H, 2 * LANES), BF16),
        ],
        28,
        rows * 6 * 2 * H * H * 2 * 3,
    )
    def backward(part, *before):
        return run_kernel(
            functools.partial(level_one_backward, math.gcd(big, half), part * half),
            [
                mixed_grad,
                masked,
                slope,
                normal,
                scale,
                probs,
                w_in,
                w_out,
                small,
                gate,
                entry,
                *before,
            ],
            [
                shape((half, width), F32),
                shape((8, width), F32),
                shape((4, 8, H), F32),
                shape((half, LANES), BF16),
                shape((6, half, H), BF16),
                shape((half, 6 * H), BF16),
            ],
            [
                pltpu.VMEM((math.gcd(big, half), 14 * LANES), F32),
                pltpu.VMEM((2 * LANES, 14 * LANES), BF16),
                pltpu.VMEM((2 * H, 2 * LANES), BF16),
            ],
            16,
            rows * 6 * (width + H) * H * 2,
            scalar=False,
        )

    grad_a, sums, g_small, logit_a, post_a, pre_a = backward(0)
    if cube:
        keep_two, send_two = grads_two
        own_two, *sends_two = small_kernel(
            core_direct_kernel,
            [after(keep_two, sums), xor_permute(send_two, "wide", 1)],
            [shape((4, blocks[1], LANES), F32)] + [shape((4, blocks[1], LANES), BF16)] * 3,
        )
        sums = after(sums, own_two)
    grad_b, sums, g_small, logit_b, post_b, pre_b = backward(1, sums, g_small)
    grads_one = run_kernel(
        functools.partial(level_one_weights, count, chunks[0]),
        [
            origin,
            level,
            active,
            sums,
            g_small,
            logit_a,
            logit_b,
            post_a,
            post_b,
            pre_a,
            pre_b,
        ],
        [shape((count // outs, blocks[0], LANES), BF16)] * outs,
        [pltpu.VMEM((count * chunks[0], LANES), F32)],
        12,
        rows * 6 * (width + H) * H * 2,
    )
    if cube:
        keep_two, *sends_two = small_kernel(
            plane_direct_kernel,
            [own_two]
            + [xor_permute(part, "wide", bit) for part, bit in zip(sends_two, (2, 4, 6))],
            [shape((blocks[1], LANES), F32)] + [shape((blocks[1], LANES), BF16)] * 3,
        )
        summed = shape((8, width), F32)
        low, high = shape((4, blocks[0], LANES), BF16), shape((4, blocks[0], LANES), F32)
        keep, send = grads_one
        one, two, sums, send_one, send_two = small_kernel(
            core_halves_kernel,
            [keep, xor_permute(after(send, keep_two), "wide", 1), sums],
            [high, high, summed, low, low],
        )
        second_grad = small_kernel(
            last_kernel,
            [keep_two]
            + [xor_permute(part, "narrow", k) for part, k in zip(sends_two, (1, 2, 3))],
            shape((chunks[1], LANES), F32),
        )
        low, high = shape((2, blocks[0], LANES), BF16), shape((2, blocks[0], LANES), F32)
        one, two, sums, send_one, send_two = small_kernel(
            plane_halves_kernel,
            [
                after(one, second_grad),
                two,
                xor_permute(send_one, "wide", 4),
                xor_permute(send_two, "wide", 2),
                sums,
            ],
            [high, high, summed, low, low],
        )
        low, high = shape((blocks[0], LANES), BF16), shape((blocks[0], LANES), F32)
        keep, sums, *sends = small_kernel(
            near_halves_kernel,
            [
                one,
                two,
                xor_permute(send_one, "wide", 2),
                xor_permute(send_two, "wide", 4),
                sums,
            ],
            [high, summed, low, low, low],
        )
        first_grad, sums = small_kernel(
            last_head_kernel,
            [me, sums, keep]
            + [xor_permute(part, "narrow", k) for part, k in zip(sends, (1, 2, 3))],
            [shape((chunks[0], LANES), F32), summed],
            scalar=True,
        )
    else:
        sums = lax.psum(sums, AXES)
        second_grad = scatter_plain(grads_two[0])[: chunks[1]]
        first_grad = small_kernel(
            head_kernel,
            [me, sums, scatter_plain(grads_one[0])[: chunks[0]]],
            shape((chunks[0], LANES), F32),
            scalar=True,
        )

    parts = 8 if rows % 1024 == 0 else 2
    input_grad = run_kernel(
        functools.partial(input_kernel, float(total_rows), parts),
        [grad_a, grad_b, masked, fields, entry, sums],
        shape((rows, width), F32),
        [pltpu.VMEM((rows, width), F32), pltpu.SemaphoreType.DMA((parts,))],
        8,
        rows * width * 10,
        scalar=False,
        out_spec=pl.BlockSpec(memory_space=pltpu.HBM),
    )
    return (towers, input_grad, first_grad.reshape(-1), second_grad.reshape(-1))


def solution(mesh):
    placed = (
        P(AXES, None),
        P(AXES, None),
        P(AXES),
        P(AXES),
        P(AXES, None),
    )
    return jax.shard_map(
        per_device,
        mesh=mesh,
        in_specs=placed,
        out_specs=(P(AXES, None), P(AXES, None), P(AXES), P(AXES)),
        check_vma=False,
    )
```

```python
import functools
import math

import jax
import jax.numpy as jnp
from jax import lax
from jax.experimental import pallas as pl
from jax.experimental.pallas import tpu as pltpu
from jax.sharding import PartitionSpec as P

H = 256
TOWER1 = 128
TOWER2 = 64
LANES = 128
EPSILON = 1e-05
AXES = ("wide", "narrow")
F32 = jnp.float32
BF16 = jnp.bfloat16
GROUPS_ONE = ((0, 4), (4, 8), (8, 14))
MEMBERS_ONE = ((0, 1, 4, 5), (2, 3, 4, 5), (0, 1, 2, 3, 4, 5))
GROUPS_TWO = ((0, 4), (4, 8))
MEMBERS_TWO = ((0, 1, 4, 5), (2, 3, 4, 5))


def up(value, step):
    return -(-value // step) * step


def mm(left, right):
    return jnp.dot(left, right, preferred_element_type=F32)


def mm_nt(left, right):
    return lax.dot_general(left, right, (((1,), (1,)), ((), ())), preferred_element_type=F32)


def mm_tn(left, right):
    return lax.dot_general(left, right, (((0,), (0,)), ((), ())), preferred_element_type=F32)


def sigmoid(values):
    return 0.5 * jnp.tanh(0.5 * values) + 0.5


def group_softmax(logits, groups):
    lane = lax.broadcasted_iota(jnp.int32, logits.shape, 1)
    spread = jnp.zeros_like(logits)
    for low, high in groups:
        inside = (lane >= low) & (lane < high)
        peak = jnp.max(jnp.where(inside, logits, -jnp.inf), axis=1, keepdims=True)
        spread = jnp.where(inside, logits - peak, spread)
    raw = jnp.exp(spread)
    result = jnp.zeros_like(logits)
    for low, high in groups:
        inside = (lane >= low) & (lane < high)
        total = jnp.sum(jnp.where(inside, raw, 0.0), axis=1, keepdims=True)
        result = jnp.where(inside, raw / total, result)
    return result


def group_softmax_back(probs, grads, groups):
    lane = lax.broadcasted_iota(jnp.int32, probs.shape, 1)
    product = probs * grads
    result = jnp.zeros_like(probs)
    for low, high in groups:
        inside = (lane >= low) & (lane < high)
        total = jnp.sum(jnp.where(inside, product, 0.0), axis=1, keepdims=True)
        result = jnp.where(inside, product - probs * total, result)
    return result


def into_lane(columns):
    rows = columns[0].shape[0]
    lane = lax.broadcasted_iota(jnp.int32, (rows, LANES), 1)
    result = jnp.zeros((rows, LANES), F32)
    for position, column in enumerate(columns):
        result = jnp.where(lane == position, column, result)
    return result


def mix_parts(weights, low, members, outputs):
    running = None
    for position, member in enumerate(members):
        term = column_block(weights, low + position) * outputs[member]
        running = term if running is None else running + term
    return running


def row_sum(values):
    return jnp.sum(values, axis=1, keepdims=True)


def column_sum(values):
    return jnp.sum(values, axis=0, keepdims=True)


def norm_forward(post):
    centred = post - row_sum(post) * (1.0 / H)
    scale = lax.rsqrt(row_sum(centred * centred) * (1.0 / H) + EPSILON)
    return centred * scale, scale


def twice(values):
    return jnp.concatenate([values, values], axis=1)


def norm_backward(scaled, normal, scale, means):
    both = jnp.concatenate([scaled.astype(BF16), (scaled * normal).astype(BF16)], axis=1)
    mean = mm(both, means)
    return twice(scale) * (
        scaled - twice(mean[:, :LANES]) - normal * twice(mean[:, LANES:])
    )


def make_means():
    row = lax.broadcasted_iota(jnp.int32, (2 * H, 2 * LANES), 0)
    lane = lax.broadcasted_iota(jnp.int32, (2 * H, 2 * LANES), 1)
    return jnp.where((row < H) == (lane < LANES), 1.0 / H, 0.0).astype(BF16)


def make_spread(columns):
    row = lax.broadcasted_iota(jnp.int32, (2 * LANES, columns * LANES), 0)
    lane = lax.broadcasted_iota(jnp.int32, (2 * LANES, columns * LANES), 1)
    return jnp.where((row & (LANES - 1)) == (lane >> 7), 1.0, 0.0).astype(BF16)


def spread_columns(values, spread):
    high = values.astype(BF16)
    low = (values - high.astype(F32)).astype(BF16)
    return mm(jnp.concatenate([high, low], axis=1), spread)


def column_block(spread, column):
    return twice(spread[:, column * LANES : (column + 1) * LANES])


def first_layout(width):
    names = (
        ("in_gain", width),
        ("in_bias", width),
        ("expert_in", 6 * width * H),
        ("expert_in_bias", 6 * H),
        ("expert_out", 6 * H * H),
        ("expert_out_bias", 6 * H),
        ("norm_gain", 6 * H),
        ("norm_bias", 6 * H),
        ("gate", 14 * width),
    )
    return place_names(names)


def second_layout():
    names = (
        ("expert_in", 6 * H * H),
        ("expert_in_bias", 6 * H),
        ("expert_out", 6 * H * H),
        ("expert_out_bias", 6 * H),
        ("norm_gain", 6 * H),
        ("norm_bias", 6 * H),
        ("gate", 2 * H * 4),
        ("tower_in", 2 * H * TOWER1),
        ("tower_in_bias", 2 * TOWER1),
        ("tower_out", 2 * TOWER1 * TOWER2),
        ("tower_out_bias", 2 * TOWER2),
    )
    return place_names(names)


def place_names(names):
    rows = {}
    offset = 0
    for name, amount in names:
        rows[name] = offset // LANES
        offset += amount
    return rows, offset // LANES


def spread_pieces(me, rows, piece_refs, flat_ref, extra_ref=None):
    slot = 0
    for ref in piece_refs:
        for index in range(ref.shape[0]):
            owner = lax.bitwise_xor(me, jnp.int32(slot))
            block = ref[index].astype(F32)
            flat_ref[pl.ds(owner * rows, rows), :] = block[:rows]
            if extra_ref is not None:
                extra_ref[slot] = block[rows : rows + extra_ref.shape[1]]
            slot += 1


def wide_rows(flat_ref, row, amount):
    return jnp.concatenate(
        [flat_ref[pl.ds(row, amount, stride=2), :], flat_ref[pl.ds(row + 1, amount, stride=2), :]],
        axis=1,
    )


def put_wide_rows(flat_ref, row, amount, value):
    flat_ref[pl.ds(row, amount, stride=2), :] = value[:, :LANES]
    flat_ref[pl.ds(row + 1, amount, stride=2), :] = value[:, LANES:]


def collect_pieces(me, count, rows, flat_ref, out_refs):
    for slot in range(count):
        owner = lax.bitwise_xor(me, jnp.int32(slot))
        value = flat_ref[pl.ds(owner * rows, rows), :].astype(BF16)
        if len(out_refs) == 1:
            out_refs[0][slot, :rows, :] = value
        else:
            part, place = slot // 4 % 2, slot // 8 * 4 + slot % 4
            out_refs[part][place, :rows, :] = value


def roll_rows(value, columns, sign):
    item = lax.broadcasted_iota(jnp.int32, value.shape, 0)
    bit = 1
    while columns * bit % LANES:
        moved = pltpu.roll(value, sign * columns * bit % LANES, 1)
        value = jnp.where((item & bit) != 0, moved, value)
        bit *= 2
    return value


def table_places(width, columns, rows):
    item = lax.broadcasted_iota(jnp.int32, (width, rows), 0)
    index = lax.broadcasted_iota(jnp.int32, (width, rows), 1)
    first = (index == ((item * columns) >> 7)).astype(F32).astype(BF16)
    last = (index == ((item * columns + columns - 1) >> 7)).astype(F32).astype(BF16)
    item = lax.broadcasted_iota(jnp.int32, (width, LANES), 0)
    lane = lax.broadcasted_iota(jnp.int32, (width, LANES), 1)
    return first, last, lane >= ((item * columns) & (LANES - 1)), lane < columns


def table_from_rows(flat, width, columns):
    first, last, late, used = table_places(width, columns, flat.shape[0])
    chosen = jnp.where(late, mm(first, flat), mm(last, flat))
    return jnp.where(used, roll_rows(chosen, columns, -1), 0.0)


def rows_from_table(table, rows, columns):
    first, last, late, _ = table_places(table.shape[0], columns, rows)
    moved = roll_rows(table, columns, 1)
    return mm_tn(first, jnp.where(late, moved, 0.0).astype(BF16)) + mm_tn(
        last, jnp.where(late, 0.0, moved).astype(BF16)
    )


def full_spec():
    return pl.BlockSpec(memory_space=pltpu.VMEM)


def scalar_spec():
    return pl.BlockSpec(memory_space=pltpu.SMEM)


def run_kernel(
    kernel, inputs, out_shape, scratch, limit, flops, scalar=True, spec=None, out_spec=None
):
    specs = [spec or full_spec()] * len(inputs)
    if scalar:
        specs[0] = scalar_spec()
    several = isinstance(out_shape, (list, tuple))
    out_specs = [full_spec()] * len(out_shape) if several else out_spec or full_spec()
    return pl.pallas_call(
        kernel,
        in_specs=specs,
        out_specs=out_specs,
        out_shape=out_shape,
        scratch_shapes=scratch,
        compiler_params=pltpu.CompilerParams(vmem_limit_bytes=limit * 2**20),
        cost_estimate=pl.CostEstimate(flops=2**20, bytes_accessed=2**10, transcendentals=0),
    )(*inputs)


def spread_presence(presence, width):
    fields = presence.shape[0]
    field = lax.broadcasted_iota(jnp.int32, (fields, width), 0)
    column = lax.broadcasted_iota(jnp.int32, (fields, width), 1)
    pick = (column // (width // fields) == field).astype(F32).astype(BF16)
    return mm_tn(presence.astype(F32).astype(BF16), pick)


def split_three(values):
    parts = []
    for _ in range(3):
        part = values.astype(BF16).astype(F32)
        parts.append(part)
        values = values - part
    return parts


def stats_kernel(
    me_ref,
    features_hbm,
    presence_hbm,
    params_hbm,
    second_hbm,
    masked_ref,
    block_ref,
    block_two_ref,
    features_ref,
    presence_ref,
    params_ref,
    second_ref,
    sems,
):
    del me_ref
    copies = [
        pltpu.make_async_copy(source, target, sems.at[index])
        for index, (source, target) in enumerate(
            (
                (presence_hbm, presence_ref),
                (features_hbm, features_ref),
                (params_hbm, params_ref),
                (second_hbm, second_ref),
            )
        )
    ]
    for copy in copies:
        copy.start()
    for copy in copies:
        copy.wait()
    rows, width = features_ref.shape
    mask = spread_presence(presence_ref[...], width)
    masked = features_ref[...].astype(F32) * mask
    masked_ref[...] = masked.astype(BF16)
    mean = column_sum(masked) * (1.0 / rows)
    spread = masked - mean
    moment = column_sum(spread * spread)
    lines = [params_ref[...].astype(F32)]
    for value in (mean, moment):
        for part in split_three(value):
            for index in range(width // LANES):
                lines.append(part[:, index * LANES : (index + 1) * LANES])
    used = params_ref.shape[0] + 6 * (width // LANES)
    lines.append(jnp.zeros((block_ref.shape[0] - used, LANES), F32))
    block_ref[...] = jnp.concatenate(lines, axis=0).astype(BF16)
    second = second_ref[...].astype(F32)
    rest = jnp.zeros((block_two_ref.shape[0] - second.shape[0], LANES), F32)
    block_two_ref[...] = jnp.concatenate([second, rest], axis=0).astype(BF16)


def from_lanes(block):
    return jnp.concatenate([block[index : index + 1, :] for index in range(block.shape[0])], axis=1)


def tiles(tile):
    return lambda ref_rows, body: lax.fori_loop(
        0, ref_rows // tile, lambda step, carry: body(pl.multiple_of(step * tile, tile), carry), 0
    )


def in_turn(first, second):
    for e in range(8):
        if e < 6:
            first(e)
        if e > 1:
            second(e - 2)


def spot(e):
    return slice(e * H, (e + 1) * H)


def level_one_forward(
    rows,
    tile,
    n_pieces,
    me_ref,
    masked_ref,
    *rest,
):
    piece_refs = rest[:n_pieces]
    (
        level_ref,
        active_ref,
        slope_ref,
        normal_ref,
        scale_ref,
        probs_ref,
        mixed_ref,
        w_in_ref,
        w_out_ref,
        small_ref,
        gate_ref,
        entry_ref,
        flat_ref,
        extra_ref,
        output_ref,
        wide_ref,
        spread_ref,
    ) = rest[n_pieces:]
    width = masked_ref.shape[1]
    where_row, _ = first_layout(width)

    spread_pieces(me_ref[0], rows, piece_refs, flat_ref, extra_ref)
    spread_ref[...] = make_spread(14)
    for e in range(6):
        w_in_ref[:, spot(e)] = wide_rows(
            flat_ref, where_row["expert_in"] + e * 2 * width, width
        ).astype(BF16)
        w_out_ref[e] = wide_rows(flat_ref, where_row["expert_out"] + e * 2 * H, H).astype(BF16)
    for index, name in enumerate(("expert_in_bias", "expert_out_bias", "norm_gain", "norm_bias")):
        small_ref[index, :6, :] = wide_rows(flat_ref, where_row[name], 6)
    gate_flat = flat_ref[pl.ds(where_row["gate"], 14 * width // LANES), :].astype(BF16)
    gate_ref[...] = table_from_rows(gate_flat, width, 14).astype(BF16)
    lanes = width // LANES
    events = masked_ref.shape[0]
    count = extra_ref.shape[0]
    means = extra_ref[:, 0:lanes, :]
    for part in (1, 2):
        means = means + extra_ref[:, part * lanes : (part + 1) * lanes, :]
    mean = jnp.sum(means, axis=0) * (1.0 / count)
    away = jnp.sum(jnp.square(means - mean[None]), axis=0) * events
    for part in (3, 4, 5):
        away = away + jnp.sum(extra_ref[:, part * lanes : (part + 1) * lanes, :], axis=0)
    entry_ref[0:1, :] = from_lanes(mean)
    entry_ref[1:2, :] = from_lanes(lax.rsqrt(away * (1.0 / (events * count)) + EPSILON))
    entry_ref[2:3, :] = from_lanes(flat_ref[0:lanes, :])
    entry_ref[3:4, :] = from_lanes(flat_ref[lanes : 2 * lanes, :])

    def body(start, carry):
        now = pl.ds(start, tile)
        normed = (masked_ref[now, :].astype(F32) - entry_ref[0:1, :]) * entry_ref[1:2, :]
        level_ref[now, :] = (normed * entry_ref[2:3, :] + entry_ref[3:4, :]).astype(BF16)
        probs_ref[now, :] = group_softmax(mm(level_ref[now, :], gate_ref[...]), GROUPS_ONE)
        def first_half(e):
            pre = mm(level_ref[now, :], w_in_ref[:, spot(e)]) + small_ref[0, e : e + 1, :]
            gate = sigmoid(pre)
            silu = pre * gate
            active_ref[e, now, :] = silu.astype(BF16)
            slope_ref[e, now, :] = (gate + silu * (1.0 - gate)).astype(BF16)

        def second_half(e):
            post = mm(active_ref[e, now, :], w_out_ref[e]) + small_ref[1, e : e + 1, :]
            normal, scale = norm_forward(post)
            normal_ref[e, now, :] = normal.astype(BF16)
            scale_ref[e, now, :] = jnp.broadcast_to(scale, (tile, LANES))
            output_ref[e] = normal * small_ref[2, e : e + 1, :] + small_ref[3, e : e + 1, :]

        in_turn(first_half, second_half)
        wide_ref[...] = spread_columns(probs_ref[now, :], spread_ref[...])
        for index, (low, _) in enumerate(GROUPS_ONE):
            mixed_ref[index, now, :] = mix_parts(
                wide_ref, low, MEMBERS_ONE[index], output_ref
            ).astype(BF16)
        return carry

    tiles(tile)(masked_ref.shape[0], body)


def level_two(count, rows, tile, n_pieces, n_outs, me_ref, mixed_ref, cotangent_ref, *rest):
    piece_refs = rest[:n_pieces]
    grads_refs = rest[n_pieces + 2 : n_pieces + 2 + n_outs]
    towers_ref, mixed_grad_ref = rest[n_pieces : n_pieces + 2]
    (
        flat_ref,
        w_in_ref,
        w_out_ref,
        small_ref,
        gate_ref,
        tower_in_ref,
        tower_out_ref,
        tower_tmp_ref,
        tower_small_ref,
        g_small_ref,
        g_tower_out_ref,
        g_tower_small_ref,
        active_ref,
        slope_ref,
        normal_ref,
        scale_ref,
        output_ref,
        combined_ref,
        combined_grad_ref,
        tower_active_ref,
        tower_grad_ref,
        logit_ref,
        post_grad_ref,
        pre_grad_ref,
        wide_ref,
        spread_ref,
        means_ref,
    ) = rest[n_pieces + 2 + n_outs :]
    where_row, used_rows = second_layout()
    all_rows = mixed_ref.shape[1]

    spread_pieces(me_ref[0], rows, piece_refs, flat_ref)
    spread_ref[...] = make_spread(8)
    means_ref[...] = make_means()
    for e in range(6):
        w_in_ref[:, spot(e)] = wide_rows(flat_ref, where_row["expert_in"] + e * 2 * H, H).astype(
            BF16
        )
        w_out_ref[e] = wide_rows(flat_ref, where_row["expert_out"] + e * 2 * H, H).astype(BF16)
    for index, name in enumerate(("expert_in_bias", "expert_out_bias", "norm_gain", "norm_bias")):
        small_ref[index, :6, :] = wide_rows(flat_ref, where_row[name], 6)
    gate_rows = H * 4 // LANES
    shift_a = lax.broadcasted_iota(jnp.int32, (LANES, LANES), 0)
    shift_b = lax.broadcasted_iota(jnp.int32, (LANES, LANES), 1)
    shift = ((shift_a + 4 == shift_b) & (shift_a < 4)).astype(F32).astype(BF16)
    tables = []
    for task in range(2):
        piece = flat_ref[pl.ds(where_row["gate"] + task * gate_rows, gate_rows), :].astype(BF16)
        tables.append(table_from_rows(piece, H, 4).astype(BF16))
    gate_ref[...] = (tables[0].astype(F32) + mm(tables[1], shift)).astype(BF16)
    zero = jnp.zeros((TOWER1 // 2, TOWER2), F32)
    for task in range(2):
        tower_in_ref[task] = flat_ref[pl.ds(where_row["tower_in"] + task * H, H), :].astype(BF16)
        packed = flat_ref[pl.ds(where_row["tower_out"] + task * TOWER1 // 2, TOWER1 // 2), :]
        for half in range(2):
            pair = [packed[:, half * TOWER2 : (half + 1) * TOWER2], zero]
            if task == 1:
                pair.reverse()
            tower_tmp_ref[pl.ds(task * TOWER1 + half, TOWER1 // 2, stride=2), :] = jnp.concatenate(
                pair, axis=1
            )
    tower_out_ref[...] = tower_tmp_ref[: 2 * TOWER1, :].astype(BF16)
    tower_small_ref[0:1, :] = from_lanes(flat_ref[pl.ds(where_row["tower_in_bias"], 2), :])
    tower_small_ref[1:2, :LANES] = flat_ref[pl.ds(where_row["tower_out_bias"], 1), :]
    g_small_ref[...] = jnp.zeros(g_small_ref.shape, F32)
    g_tower_small_ref[...] = jnp.zeros(g_tower_small_ref.shape, F32)

    def body(start, carry):
        now = pl.ds(start, tile)
        lane = lax.broadcasted_iota(jnp.int32, (tile, LANES), 1)
        def first_half(e):
            pre = mm(mixed_ref[e // 2, now, :], w_in_ref[:, spot(e)]) + small_ref[0, e : e + 1, :]
            gate = sigmoid(pre)
            silu = pre * gate
            active_ref[e, now, :] = silu.astype(BF16)
            slope_ref[:, spot(e)] = gate + silu * (1.0 - gate)

        def second_half(e):
            post = mm(active_ref[e, now, :], w_out_ref[e]) + small_ref[1, e : e + 1, :]
            normal, scale = norm_forward(post)
            normal_ref[e] = normal
            scale_ref[e] = jnp.broadcast_to(scale, (tile, LANES))
            output_ref[e] = normal * small_ref[2, e : e + 1, :] + small_ref[3, e : e + 1, :]

        in_turn(first_half, second_half)
        logits = jnp.where(
            lane < 4, mm(mixed_ref[0, now, :], gate_ref[...]), mm(mixed_ref[1, now, :], gate_ref[...])
        )
        probs = group_softmax(logits, GROUPS_TWO)
        wide_ref[...] = spread_columns(probs, spread_ref[...])
        for task in range(2):
            combined_ref[task, now, :] = mix_parts(
                wide_ref, 4 * task, MEMBERS_TWO[task], output_ref
            ).astype(BF16)
        tower_pre = (
            jnp.concatenate(
                [mm(combined_ref[task, now, :], tower_in_ref[task]) for task in range(2)], axis=1
            )
            + tower_small_ref[0:1, :]
        )
        tower_gate = sigmoid(tower_pre)
        tower_silu = tower_pre * tower_gate
        tower_active_ref[now, :] = tower_silu.astype(BF16)
        towers_ref[now, :] = (
            mm(tower_active_ref[now, :], tower_out_ref[...]) + tower_small_ref[1:2, :LANES]
        )
        cotangent = cotangent_ref[now, :]
        g_tower_small_ref[1:2, :LANES] += column_sum(cotangent.astype(F32))
        tower_slope = tower_gate + tower_silu * (1.0 - tower_gate)
        tower_grad = (mm_nt(cotangent, tower_out_ref[...]) * tower_slope).astype(BF16)
        tower_grad_ref[now, :] = tower_grad
        g_tower_small_ref[0:1, :] += column_sum(tower_grad.astype(F32))
        for task in range(2):
            combined_grad_ref[task] = mm_nt(
                tower_grad_ref[now, task * TOWER1 : (task + 1) * TOWER1], tower_in_ref[task]
            )
        prob_grads = into_lane(
            [
                row_sum(combined_grad_ref[task] * output_ref[member])
                for task in range(2)
                for member in MEMBERS_TWO[task]
            ]
        )
        logit_grad = group_softmax_back(probs, prob_grads, GROUPS_TWO)
        logit_ref[0, now, :] = jnp.where(lane < 4, logit_grad, 0.0).astype(BF16)
        logit_ref[1, now, :] = jnp.where((lane >= 4) & (lane < 8), logit_grad, 0.0).astype(BF16)
        def norm_half(e):
            out_grad = None
            for task in range(2):
                if e in MEMBERS_TWO[task]:
                    column = 4 * task + MEMBERS_TWO[task].index(e)
                    term = column_block(wide_ref, column) * combined_grad_ref[task]
                    out_grad = term if out_grad is None else out_grad + term
            normal = normal_ref[e]
            g_small_ref[2, e : e + 1, :] += column_sum(out_grad * normal)
            g_small_ref[3, e : e + 1, :] += column_sum(out_grad)
            post_grad = norm_backward(
                out_grad * small_ref[2, e : e + 1, :], normal, scale_ref[e], means_ref[...]
            )
            post_grad_ref[e, now, :] = post_grad.astype(BF16)
            g_small_ref[1, e : e + 1, :] += column_sum(post_grad)

        def active_half(e):
            act_grad = mm_nt(post_grad_ref[e, now, :], w_out_ref[e])
            pre_grad = act_grad * slope_ref[:, spot(e)]
            pre_grad_ref[now, spot(e)] = pre_grad.astype(BF16)
            g_small_ref[0, e : e + 1, :] += column_sum(pre_grad)

        in_turn(norm_half, active_half)
        for index in range(3):
            pair = slice(2 * index * H, 2 * (index + 1) * H)
            grad = mm_nt(pre_grad_ref[now, pair], w_in_ref[:, pair])
            if index < 2:
                grad = grad + mm_nt(logit_ref[index, now, :], gate_ref[...])
            mixed_grad_ref[index, now, :] = grad
        return carry

    tiles(tile)(all_rows, body)

    for e in range(6):
        put_wide_rows(
            flat_ref,
            where_row["expert_in"] + e * 2 * H,
            H,
            mm_tn(mixed_ref[e // 2], pre_grad_ref[:, spot(e)]),
        )
        put_wide_rows(
            flat_ref,
            where_row["expert_out"] + e * 2 * H,
            H,
            mm_tn(active_ref[e], post_grad_ref[e]),
        )
    for index, name in enumerate(("expert_in_bias", "expert_out_bias", "norm_gain", "norm_bias")):
        put_wide_rows(flat_ref, where_row[name], 6, g_small_ref[index, :6, :])
    back = ((shift_a == shift_b + 4) & (shift_b < 4)).astype(F32).astype(BF16)
    tables = [mm_tn(mixed_ref[task], logit_ref[task]) for task in range(2)]
    tables[1] = mm(tables[1].astype(BF16), back)
    g_tower_out_ref[: 2 * TOWER1, :] = mm_tn(tower_active_ref[...], cotangent_ref[...])
    for task in range(2):
        flat_ref[pl.ds(where_row["gate"] + task * gate_rows, gate_rows), :] = rows_from_table(
            tables[task], gate_rows, 4
        )
        flat_ref[pl.ds(where_row["tower_in"] + task * H, H), :] = mm_tn(
            combined_ref[task], tower_grad_ref[:, task * TOWER1 : (task + 1) * TOWER1]
        )
        flat_ref[pl.ds(where_row["tower_out"] + task * TOWER1 // 2, TOWER1 // 2), :] = (
            jnp.concatenate(
                [
                    g_tower_out_ref[pl.ds(task * TOWER1 + half, TOWER1 // 2, stride=2), :][
                        :, task * TOWER2 : (task + 1) * TOWER2
                    ]
                    for half in range(2)
                ],
                axis=1,
            )
        )
        flat_ref[pl.ds(where_row["tower_in_bias"] + task, 1), :] = g_tower_small_ref[
            0:1, task * TOWER1 : (task + 1) * TOWER1
        ]
    flat_ref[pl.ds(where_row["tower_out_bias"], 1), :] = g_tower_small_ref[1:2, :LANES]
    if used_rows < count * rows:
        flat_ref[pl.ds(used_rows, count * rows - used_rows), :] = jnp.zeros(
            (count * rows - used_rows, LANES), F32
        )
    collect_pieces(me_ref[0], count, rows, flat_ref, grads_refs)


def level_one_backward(
    tile,
    begin,
    mixed_grad_ref,
    masked_ref,
    slope_ref,
    normal_ref,
    scale_ref,
    probs_ref,
    w_in_ref,
    w_out_ref,
    small_ref,
    gate_ref,
    entry_ref,
    *rest,
):
    if begin:
        before_sum_ref, before_small_ref, *rest = rest
    (
        level_grad_ref,
        g_sum_ref,
        g_small_ref,
        logit_ref,
        post_grad_ref,
        pre_grad_ref,
        wide_ref,
        spread_ref,
        means_ref,
    ) = rest
    spread_ref[...] = make_spread(14)
    means_ref[...] = make_means()
    if begin:
        g_small_ref[...] = before_small_ref[...]
        g_sum_ref[...] = before_sum_ref[...]
    else:
        g_small_ref[...] = jnp.zeros(g_small_ref.shape, F32)
        g_sum_ref[...] = jnp.zeros(g_sum_ref.shape, F32)

    def body(start, carry):
        here = pl.ds(start, tile)
        now = pl.ds(begin + start, tile)
        probs = probs_ref[now, :]
        wide_ref[...] = spread_columns(probs, spread_ref[...])
        columns = [None] * 14
        for e in range(6):
            output = (
                normal_ref[e, now, :].astype(F32) * small_ref[2, e : e + 1, :]
                + small_ref[3, e : e + 1, :]
            )
            for index, (low, _) in enumerate(GROUPS_ONE):
                if e in MEMBERS_ONE[index]:
                    columns[low + MEMBERS_ONE[index].index(e)] = row_sum(
                        mixed_grad_ref[index, now, :] * output
                    )
        logit_ref[here, :] = group_softmax_back(probs, into_lane(columns), GROUPS_ONE).astype(BF16)
        def norm_half(e):
            normal = normal_ref[e, now, :].astype(F32)
            out_grad = None
            for index, (low, _) in enumerate(GROUPS_ONE):
                if e in MEMBERS_ONE[index]:
                    column = low + MEMBERS_ONE[index].index(e)
                    term = column_block(wide_ref, column) * mixed_grad_ref[index, now, :]
                    out_grad = term if out_grad is None else out_grad + term
            g_small_ref[2, e : e + 1, :] += column_sum(out_grad * normal)
            g_small_ref[3, e : e + 1, :] += column_sum(out_grad)
            post_grad = norm_backward(
                out_grad * small_ref[2, e : e + 1, :],
                normal,
                scale_ref[e, now, :],
                means_ref[...],
            )
            post_grad_ref[e, here, :] = post_grad.astype(BF16)
            g_small_ref[1, e : e + 1, :] += column_sum(post_grad)

        def active_half(e):
            act_grad = mm_nt(post_grad_ref[e, here, :], w_out_ref[e])
            pre_grad = act_grad * slope_ref[e, now, :].astype(F32)
            pre_grad_ref[here, spot(e)] = pre_grad.astype(BF16)
            g_small_ref[0, e : e + 1, :] += column_sum(pre_grad)

        in_turn(norm_half, active_half)
        level_grad = mm_nt(pre_grad_ref[here, :], w_in_ref[...]) + mm_nt(
            logit_ref[here, :], gate_ref[...]
        )
        level_grad_ref[here, :] = level_grad
        normed = (masked_ref[now, :].astype(F32) - entry_ref[0:1, :]) * entry_ref[1:2, :]
        g_sum_ref[0:1, :] += column_sum(level_grad * normed)
        g_sum_ref[1:2, :] += column_sum(level_grad)
        return carry

    tiles(tile)(logit_ref.shape[0], body)


def send_sums(sums, block_refs):
    high = sums.astype(BF16).astype(F32)
    lines = []
    for value in (high, sums - high):
        for row in range(2):
            for index in range(value.shape[1] // LANES):
                lines.append(value[row : row + 1, index * LANES : (index + 1) * LANES])
    block = jnp.concatenate(lines, axis=0).astype(BF16)
    for ref in block_refs:
        ref[ref.shape[0] - 16 :, :] = block


def got_sums(block_ref, shape):
    rows = block_ref.shape[0]
    block = block_ref[rows - 16 :, :].astype(F32)
    block = block[:8] + block[8:]
    lanes = shape[1] // LANES
    lines = [from_lanes(block[row * lanes : (row + 1) * lanes]) for row in range(2)]
    return jnp.concatenate(lines + [jnp.zeros((shape[0] - 2, shape[1]), F32)], axis=0)


def level_one_weights(
    count,
    rows,
    me_ref,
    level_ref,
    active_ref,
    sums_ref,
    small_ref,
    logit_a_ref,
    logit_b_ref,
    post_a_ref,
    post_b_ref,
    pre_a_ref,
    pre_b_ref,
    *rest,
):
    *grads_refs, flat_ref = rest
    width = level_ref.shape[1]
    lanes = width // LANES
    where_row, used_rows = first_layout(width)
    half = logit_a_ref.shape[0]
    one, two = slice(0, half), slice(half, level_ref.shape[0])
    for e in range(6):
        put_wide_rows(
            flat_ref,
            where_row["expert_in"] + e * 2 * width,
            width,
            mm_tn(level_ref[one, :], pre_a_ref[:, spot(e)])
            + mm_tn(level_ref[two, :], pre_b_ref[:, spot(e)]),
        )
        put_wide_rows(
            flat_ref,
            where_row["expert_out"] + e * 2 * H,
            H,
            mm_tn(active_ref[e, one, :], post_a_ref[e])
            + mm_tn(active_ref[e, two, :], post_b_ref[e]),
        )
    for index, name in enumerate(("expert_in_bias", "expert_out_bias", "norm_gain", "norm_bias")):
        put_wide_rows(flat_ref, where_row[name], 6, small_ref[index, :6, :])
    gate_rows = 14 * width // LANES
    gate = mm_tn(level_ref[one, :], logit_a_ref[...]) + mm_tn(level_ref[two, :], logit_b_ref[...])
    flat_ref[pl.ds(where_row["gate"], gate_rows), :] = rows_from_table(gate, gate_rows, 14)
    flat_ref[0 : 2 * lanes, :] = jnp.zeros((2 * lanes, LANES), F32)
    if used_rows < count * rows:
        flat_ref[pl.ds(used_rows, count * rows - used_rows), :] = jnp.zeros(
            (count * rows - used_rows, LANES), F32
        )
    collect_pieces(me_ref[0], count, rows, flat_ref, grads_refs)
    if len(grads_refs) > 1:
        send_sums(sums_ref[...], [grads_refs[1].at[0]])


def input_kernel(
    total_rows,
    parts,
    grad_a_ref,
    grad_b_ref,
    masked_ref,
    presence_ref,
    entry_ref,
    sums_ref,
    out_hbm,
    out_ref,
    sems,
):
    rows, width = masked_ref.shape
    inv_scale = entry_ref[1:2, :]
    factor = inv_scale * entry_ref[2:3, :]
    cross = sums_ref[0:1, :] * (1.0 / total_rows)
    plain = sums_ref[1:2, :] * (1.0 / total_rows)
    each = rows // parts
    copies = []
    for part in range(parts):
        now = pl.ds(part * each, each)
        ref = grad_a_ref if part < parts // 2 else grad_b_ref
        grad = ref[pl.ds(part % (parts // 2) * each, each), :]
        mask = spread_presence(presence_ref[:, now], width)
        normed = (masked_ref[now, :].astype(F32) - entry_ref[0:1, :]) * inv_scale
        out_ref[now, :] = mask * (factor * (grad - plain - normed * cross))
        copies.append(pltpu.make_async_copy(out_ref.at[now], out_hbm.at[now], sems.at[part]))
        copies[-1].start()
    for copy in copies:
        copy.wait()


def xor_permute(value, axis, bit):
    size = lax.axis_size(axis)
    return lax.ppermute(value, axis, [(index, index ^ bit) for index in range(size)])


def hypercube_ok():
    wide, narrow = lax.axis_size("wide"), lax.axis_size("narrow")
    return wide == 8 and narrow == 4


def after(value, *others):
    return lax.optimization_barrier((value, *others))[0]


def small_kernel(kernel, inputs, out_shape, scalar=False):
    return run_kernel(kernel, inputs, out_shape, [], 8, 2**20, scalar=scalar)


def stack_kernel(*refs):
    sources, targets = refs[:4], refs[4:]
    each = 4 // len(targets)
    for index, ref in enumerate(sources):
        targets[index // each][index % each] = ref[...]


def gather_near(block):
    return [block] + [xor_permute(block, "narrow", k) for k in (1, 2, 3)]


def stack_near(near, parts):
    rows = near[0].shape[0]
    shapes = [jax.ShapeDtypeStruct((4 // parts, rows, LANES), BF16)] * parts
    return small_kernel(stack_kernel, near, shapes)


def gather_halves(first, second):
    first_y, second_x = xor_permute(first, "wide", 4), xor_permute(second, "wide", 2)
    first_x, second_y = xor_permute(first, "wide", 2), xor_permute(second, "wide", 4)
    first_xy, second_xy = xor_permute(first_y, "wide", 2), xor_permute(second_x, "wide", 4)
    own = [first, second, first_x, second_x, first_y, second_y, first_xy, second_xy]
    other = [xor_permute(piece, "wide", 1) for piece in own]
    pieces = []
    for index in range(4):
        pieces += [own[2 * index], own[2 * index + 1], other[2 * index], other[2 * index + 1]]
    return pieces


def gather_plane(stack):
    return [stack] + [xor_permute(stack, "wide", bit) for bit in (2, 4, 6)]


def gather_core(own):
    pieces = []
    for piece in own:
        pieces += [piece, xor_permute(piece, "wide", 1)]
    return pieces


def core_direct_kernel(keep_ref, got_ref, own_ref, *send_refs):
    total = keep_ref[...].astype(F32) + got_ref[...].astype(F32)
    own_ref[...] = total[0:4]
    for part, ref in enumerate(send_refs):
        ref[...] = total[4 * (part + 1) : 4 * (part + 2)].astype(BF16)


def plane_direct_kernel(own_ref, one_ref, two_ref, three_ref, keep_ref, *send_refs):
    total = own_ref[...]
    for ref in (one_ref, two_ref, three_ref):
        total = total + ref[...].astype(F32)
    keep_ref[...] = total[0]
    for part, ref in enumerate(send_refs):
        ref[...] = total[part + 1].astype(BF16)


def last_kernel(own_ref, one_ref, two_ref, three_ref, out_ref):
    total = own_ref[...]
    for ref in (one_ref, two_ref, three_ref):
        total = total + ref[...].astype(F32)
    out_ref[...] = total[: out_ref.shape[0]]


def last_head_kernel(
    me_ref, sums_ref, own_ref, one_ref, two_ref, three_ref, out_ref, total_ref
):
    last_kernel(own_ref, one_ref, two_ref, three_ref, out_ref)
    sums = sums_ref[...]
    for ref in (one_ref, two_ref, three_ref):
        sums = sums + got_sums(ref, sums.shape)
    total_ref[...] = sums
    put_head(me_ref, total_ref, out_ref)


def put_head(me_ref, sums_ref, out_ref):
    @pl.when(me_ref[0] == 0)
    def _():
        lanes = sums_ref.shape[1] // LANES
        for index in range(2 * lanes):
            part = slice(index % lanes * LANES, (index % lanes + 1) * LANES)
            row = index // lanes
            out_ref[index : index + 1, :] = sums_ref[row : row + 1, part]


def head_kernel(me_ref, sums_ref, block_ref, out_ref):
    out_ref[...] = block_ref[...]
    put_head(me_ref, sums_ref, out_ref)


def core_halves_kernel(
    keep_ref, got_ref, sums_ref, one_ref, two_ref, out_ref, send_one_ref, send_two_ref
):
    total = keep_ref[...].astype(F32) + got_ref[...].astype(F32)
    for x in range(2):
        for z in range(2):
            one_ref[2 * x + z] = total[4 * x + z]
            send_one_ref[2 * x + z] = total[8 + 4 * x + z].astype(BF16)
    for y in range(2):
        for z in range(2):
            two_ref[2 * y + z] = total[8 * y + 2 + z]
            send_two_ref[2 * y + z] = total[8 * y + 4 + 2 + z].astype(BF16)
    sums = sums_ref[...] + got_sums(got_ref.at[0], sums_ref.shape)
    out_ref[...] = sums
    send_sums(sums, [send_one_ref.at[0]])


def plane_halves_kernel(
    one_ref,
    two_ref,
    got_one_ref,
    got_two_ref,
    sums_ref,
    keep_one_ref,
    keep_two_ref,
    out_ref,
    send_one_ref,
    send_two_ref,
):
    for ref, got, keep, send in (
        (one_ref, got_one_ref, keep_one_ref, send_one_ref),
        (two_ref, got_two_ref, keep_two_ref, send_two_ref),
    ):
        total = ref[...] + got[...].astype(F32)
        keep[...] = total[0:2]
        send[...] = total[2:4].astype(BF16)
    sums = sums_ref[...] + got_sums(got_one_ref.at[0], sums_ref.shape)
    out_ref[...] = sums
    send_sums(sums, [send_one_ref.at[0]])


def near_halves_kernel(
    one_ref,
    two_ref,
    got_one_ref,
    got_two_ref,
    sums_ref,
    keep_ref,
    out_ref,
    send_one_ref,
    send_two_ref,
    send_three_ref,
):
    one = one_ref[...] + got_one_ref[...].astype(F32)
    two = two_ref[...] + got_two_ref[...].astype(F32)
    keep_ref[...] = one[0]
    send_one_ref[...] = one[1].astype(BF16)
    send_two_ref[...] = two[0].astype(BF16)
    send_three_ref[...] = two[1].astype(BF16)
    sums = sums_ref[...] + got_sums(got_one_ref.at[0], sums_ref.shape)
    out_ref[...] = sums
    send_sums(sums, [send_one_ref, send_two_ref, send_three_ref])


def scatter_plain(value):
    return lax.psum_scatter(value.astype(F32), AXES, scatter_dimension=0, tiled=True)[0]


def per_device(features, presence, first_params, second_params, cotangent):
    rows, width = features.shape
    lanes = width // LANES
    devices_all = count = lax.axis_size(AXES)
    total_rows = rows * devices_all
    cube = hypercube_ok()
    tile = math.gcd(rows, 256)
    half = rows // 2
    big = math.gcd(rows, 512)
    me = lax.axis_index(AXES).astype(jnp.int32).reshape(1)
    chunks = [first_params.shape[0] // LANES, second_params.shape[0] // LANES]
    extra = 6 * lanes
    shape = jax.ShapeDtypeStruct
    fields = presence.T
    blocks = [up(chunks[0], 16) + (16 if cube else 0), up(chunks[1], 16)]

    masked, block_one, block_two = run_kernel(
        stats_kernel,
        [
            me,
            features,
            fields,
            first_params.reshape(chunks[0], LANES),
            second_params.reshape(chunks[1], LANES),
        ],
        (
            pltpu.VMEM((rows, width), BF16),
            pltpu.VMEM((up(chunks[0] + extra, 16), LANES), BF16),
            pltpu.VMEM((blocks[1], LANES), BF16),
        ),
        [
            pltpu.VMEM((rows, width), BF16),
            pltpu.VMEM(fields.shape, jnp.int32),
            pltpu.VMEM((chunks[0], LANES), BF16),
            pltpu.VMEM((chunks[1], LANES), BF16),
            pltpu.SemaphoreType.DMA((4,)),
        ],
        60,
        rows * width * 10,
        spec=pl.BlockSpec(memory_space=pltpu.HBM),
    )
    if cube:
        origin = me
        near_one = gather_near(block_one)
        first, second = stack_near(near_one, 2)
        near_two = gather_near(after(block_two, first))
        pieces_one = gather_halves(first, second)
        near_two[3] = after(near_two[3], pieces_one[12], pieces_one[13])
        (stack_two,) = stack_near(near_two, 1)
        plane_two = gather_plane(after(stack_two, pieces_one[12], pieces_one[13]))
        masked = after(masked, stack_two)
    else:
        origin = jnp.zeros((1,), jnp.int32)
        pieces_one = [lax.all_gather(block_one, AXES)]
        plane_two = [lax.all_gather(block_two, AXES)]

    saved = run_kernel(
        functools.partial(level_one_forward, chunks[0], big, len(pieces_one)),
        [origin, masked] + pieces_one,
        [
            shape((rows, width), BF16),
            shape((6, rows, H), BF16),
            shape((6, rows, H), BF16),
            shape((6, rows, H), BF16),
            shape((6, rows, LANES), F32),
            shape((rows, LANES), F32),
            shape((3, rows, H), BF16),
            shape((width, 6 * H), BF16),
            shape((6, H, H), BF16),
            shape((4, 8, H), F32),
            shape((width, LANES), BF16),
            shape((8, width), F32),
        ],
        [
            pltpu.VMEM((up(count * chunks[0], 8) + 16, LANES), F32),
            pltpu.VMEM((count, extra, LANES), F32),
            pltpu.VMEM((6, big, H), F32),
            pltpu.VMEM((big, 14 * LANES), F32),
            pltpu.VMEM((2 * LANES, 14 * LANES), BF16),
        ],
        28,
        rows * 6 * (width + H) * H * 2,
    )
    level, active, slope, normal, scale, probs, mixed, w_in, w_out, small, gate, entry = saved
    pieces_two = gather_core([after(piece, entry) for piece in plane_two]) if cube else plane_two

    outs = 2 if cube else 1
    towers, mixed_grad, *grads_two = run_kernel(
        functools.partial(level_two, count, chunks[1], tile, len(pieces_two), outs),
        [origin, mixed, cotangent] + pieces_two,
        [
            shape((rows, LANES), F32),
            shape((3, rows, H), F32),
        ]
        + [shape((count // outs, blocks[1], LANES), BF16)] * outs,
        [
            pltpu.VMEM((up(count * chunks[1], 8) + 16, LANES), F32),
            pltpu.VMEM((H, 6 * H), BF16),
            pltpu.VMEM((6, H, H), BF16),
            pltpu.VMEM((4, 8, H), F32),
            pltpu.VMEM((H, LANES), BF16),
            pltpu.VMEM((2, H, TOWER1), BF16),
            pltpu.VMEM((2 * TOWER1, LANES), BF16),
            pltpu.VMEM((2 * TOWER1 + 16, LANES), F32),
            pltpu.VMEM((8, 2 * TOWER1), F32),
            pltpu.VMEM((4, 8, H), F32),
            pltpu.VMEM((2 * TOWER1 + 16, LANES), F32),
            pltpu.VMEM((8, 2 * TOWER1), F32),
            pltpu.VMEM((6, rows, H), BF16),
            pltpu.VMEM((tile, 6 * H), F32),
            pltpu.VMEM((6, tile, H), F32),
            pltpu.VMEM((6, tile, LANES), F32),
            pltpu.VMEM((6, tile, H), F32),
            pltpu.VMEM((2, rows, H), BF16),
            pltpu.VMEM((2, tile, H), F32),
            pltpu.VMEM((rows, 2 * TOWER1), BF16),
            pltpu.VMEM((rows, 2 * TOWER1), BF16),
            pltpu.VMEM((2, rows, LANES), BF16),
            pltpu.VMEM((6, rows, H), BF16),
            pltpu.VMEM((rows, 6 * H), BF16),
            pltpu.VMEM((tile, 8 * LANES), F32),
            pltpu.VMEM((2 * LANES, 8 * LANES), BF16),
            pltpu.VMEM((2 * H, 2 * LANES), BF16),
        ],
        28,
        rows * 6 * 2 * H * H * 2 * 3,
    )
    def backward(part, *before):
        return run_kernel(
            functools.partial(level_one_backward, math.gcd(big, half), part * half),
            [
                mixed_grad,
                masked,
                slope,
                normal,
                scale,
                probs,
                w_in,
                w_out,
                small,
                gate,
                entry,
                *before,
            ],
            [
                shape((half, width), F32),
                shape((8, width), F32),
                shape((4, 8, H), F32),
                shape((half, LANES), BF16),
                shape((6, half, H), BF16),
                shape((half, 6 * H), BF16),
            ],
            [
                pltpu.VMEM((math.gcd(big, half), 14 * LANES), F32),
                pltpu.VMEM((2 * LANES, 14 * LANES), BF16),
                pltpu.VMEM((2 * H, 2 * LANES), BF16),
            ],
            16,
            rows * 6 * (width + H) * H * 2,
            scalar=False,
        )

    grad_a, sums, g_small, logit_a, post_a, pre_a = backward(0)
    if cube:
        keep_two, send_two = grads_two
        own_two, *sends_two = small_kernel(
            core_direct_kernel,
            [after(keep_two, sums), xor_permute(send_two, "wide", 1)],
            [shape((4, blocks[1], LANES), F32)] + [shape((4, blocks[1], LANES), BF16)] * 3,
        )
        sums = after(sums, own_two)
    grad_b, sums, g_small, logit_b, post_b, pre_b = backward(1, sums, g_small)
    grads_one = run_kernel(
        functools.partial(level_one_weights, count, chunks[0]),
        [
            origin,
            level,
            active,
            sums,
            g_small,
            logit_a,
            logit_b,
            post_a,
            post_b,
            pre_a,
            pre_b,
        ],
        [shape((count // outs, blocks[0], LANES), BF16)] * outs,
        [pltpu.VMEM((up(count * chunks[0], 8) + 16, LANES), F32)],
        12,
        rows * 6 * (width + H) * H * 2,
    )
    if cube:
        keep_two, *sends_two = small_kernel(
            plane_direct_kernel,
            [own_two]
            + [xor_permute(part, "wide", bit) for part, bit in zip(sends_two, (2, 4, 6))],
            [shape((blocks[1], LANES), F32)] + [shape((blocks[1], LANES), BF16)] * 3,
        )
        summed = shape((8, width), F32)
        low, high = shape((4, blocks[0], LANES), BF16), shape((4, blocks[0], LANES), F32)
        keep, send = grads_one
        one, two, sums, send_one, send_two = small_kernel(
            core_halves_kernel,
            [keep, xor_permute(after(send, keep_two), "wide", 1), sums],
            [high, high, summed, low, low],
        )
        second_grad = small_kernel(
            last_kernel,
            [keep_two]
            + [xor_permute(part, "narrow", k) for part, k in zip(sends_two, (1, 2, 3))],
            shape((chunks[1], LANES), F32),
        )
        low, high = shape((2, blocks[0], LANES), BF16), shape((2, blocks[0], LANES), F32)
        one, two, sums, send_one, send_two = small_kernel(
            plane_halves_kernel,
            [
                after(one, second_grad),
                two,
                xor_permute(send_one, "wide", 4),
                xor_permute(send_two, "wide", 2),
                sums,
            ],
            [high, high, summed, low, low],
        )
        low, high = shape((blocks[0], LANES), BF16), shape((blocks[0], LANES), F32)
        keep, sums, *sends = small_kernel(
            near_halves_kernel,
            [
                one,
                two,
                xor_permute(send_one, "wide", 2),
                xor_permute(send_two, "wide", 4),
                sums,
            ],
            [high, summed, low, low, low],
        )
        first_grad, sums = small_kernel(
            last_head_kernel,
            [me, sums, keep]
            + [xor_permute(part, "narrow", k) for part, k in zip(sends, (1, 2, 3))],
            [shape((chunks[0], LANES), F32), summed],
            scalar=True,
        )
    else:
        sums = lax.psum(sums, AXES)
        second_grad = scatter_plain(grads_two[0])[: chunks[1]]
        first_grad = small_kernel(
            head_kernel,
            [me, sums, scatter_plain(grads_one[0])[: chunks[0]]],
            shape((chunks[0], LANES), F32),
            scalar=True,
        )

    parts = 8 if rows % 1024 == 0 else 2
    input_grad = run_kernel(
        functools.partial(input_kernel, float(total_rows), parts),
        [grad_a, grad_b, masked, fields, entry, sums],
        shape((rows, width), F32),
        [pltpu.VMEM((rows, width), F32), pltpu.SemaphoreType.DMA((parts,))],
        8,
        rows * width * 10,
        scalar=False,
        out_spec=pl.BlockSpec(memory_space=pltpu.HBM),
    )
    return (towers, input_grad, first_grad.reshape(-1), second_grad.reshape(-1))


def solution(mesh):
    placed = (
        P(AXES, None),
        P(AXES, None),
        P(AXES),
        P(AXES),
        P(AXES, None),
    )
    return jax.shard_map(
        per_device,
        mesh=mesh,
        in_specs=placed,
        out_specs=(P(AXES, None), P(AXES, None), P(AXES), P(AXES)),
        check_vma=False,
    )
```

```python
import functools
import math

import jax
import jax.numpy as jnp
from jax import lax
from jax.experimental import pallas as pl
from jax.experimental.pallas import tpu as pltpu
from jax.sharding import PartitionSpec as P

H = 256
TOWER1 = 128
TOWER2 = 64
LANES = 128
EPSILON = 1e-05
AXES = ("wide", "narrow")
F32 = jnp.float32
BF16 = jnp.bfloat16
GROUPS_ONE = ((0, 4), (4, 8), (8, 14))
MEMBERS_ONE = ((0, 1, 4, 5), (2, 3, 4, 5), (0, 1, 2, 3, 4, 5))
GROUPS_TWO = ((0, 4), (4, 8))
MEMBERS_TWO = ((0, 1, 4, 5), (2, 3, 4, 5))


def up(value, step):
    return -(-value // step) * step


def mm(left, right):
    return jnp.dot(left, right, preferred_element_type=F32)


def mm_nt(left, right):
    return lax.dot_general(left, right, (((1,), (1,)), ((), ())), preferred_element_type=F32)


def mm_tn(left, right):
    return lax.dot_general(left, right, (((0,), (0,)), ((), ())), preferred_element_type=F32)


def sigmoid(values):
    return 0.5 * jnp.tanh(0.5 * values) + 0.5


def group_softmax(logits, groups):
    lane = lax.broadcasted_iota(jnp.int32, logits.shape, 1)
    spread = jnp.zeros_like(logits)
    for low, high in groups:
        inside = (lane >= low) & (lane < high)
        peak = jnp.max(jnp.where(inside, logits, -jnp.inf), axis=1, keepdims=True)
        spread = jnp.where(inside, logits - peak, spread)
    raw = jnp.exp(spread)
    result = jnp.zeros_like(logits)
    for low, high in groups:
        inside = (lane >= low) & (lane < high)
        total = jnp.sum(jnp.where(inside, raw, 0.0), axis=1, keepdims=True)
        result = jnp.where(inside, raw / total, result)
    return result


def group_softmax_back(probs, grads, groups):
    lane = lax.broadcasted_iota(jnp.int32, probs.shape, 1)
    product = probs * grads
    result = jnp.zeros_like(probs)
    for low, high in groups:
        inside = (lane >= low) & (lane < high)
        total = jnp.sum(jnp.where(inside, product, 0.0), axis=1, keepdims=True)
        result = jnp.where(inside, product - probs * total, result)
    return result


def into_lane(columns):
    rows = columns[0].shape[0]
    lane = lax.broadcasted_iota(jnp.int32, (rows, LANES), 1)
    result = jnp.zeros((rows, LANES), F32)
    for position, column in enumerate(columns):
        result = jnp.where(lane == position, column, result)
    return result


def mix_parts(weights, low, members, outputs):
    running = None
    for position, member in enumerate(members):
        term = column_block(weights, low + position) * outputs[member]
        running = term if running is None else running + term
    return running


def row_sum(values):
    return jnp.sum(values, axis=1, keepdims=True)


def column_sum(values):
    return jnp.sum(values, axis=0, keepdims=True)


def norm_forward(post):
    centred = post - row_sum(post) * (1.0 / H)
    scale = lax.rsqrt(row_sum(centred * centred) * (1.0 / H) + EPSILON)
    return centred * scale, scale


def twice(values):
    return jnp.concatenate([values, values], axis=1)


def norm_backward(scaled, normal, scale, means):
    both = jnp.concatenate([scaled.astype(BF16), (scaled * normal).astype(BF16)], axis=1)
    mean = mm(both, means)
    return twice(scale) * (
        scaled - twice(mean[:, :LANES]) - normal * twice(mean[:, LANES:])
    )


def make_means():
    row = lax.broadcasted_iota(jnp.int32, (2 * H, 2 * LANES), 0)
    lane = lax.broadcasted_iota(jnp.int32, (2 * H, 2 * LANES), 1)
    return jnp.where((row < H) == (lane < LANES), 1.0 / H, 0.0).astype(BF16)


def make_spread(columns):
    row = lax.broadcasted_iota(jnp.int32, (2 * LANES, columns * LANES), 0)
    lane = lax.broadcasted_iota(jnp.int32, (2 * LANES, columns * LANES), 1)
    return jnp.where((row & (LANES - 1)) == (lane >> 7), 1.0, 0.0).astype(BF16)


def spread_columns(values, spread):
    high = values.astype(BF16)
    low = (values - high.astype(F32)).astype(BF16)
    return mm(jnp.concatenate([high, low], axis=1), spread)


def column_block(spread, column):
    return twice(spread[:, column * LANES : (column + 1) * LANES])


def first_layout(width):
    names = (
        ("in_gain", width),
        ("in_bias", width),
        ("expert_in", 6 * width * H),
        ("expert_in_bias", 6 * H),
        ("expert_out", 6 * H * H),
        ("expert_out_bias", 6 * H),
        ("norm_gain", 6 * H),
        ("norm_bias", 6 * H),
        ("gate", 14 * width),
    )
    return place_names(names)


def second_layout():
    names = (
        ("expert_in", 6 * H * H),
        ("expert_in_bias", 6 * H),
        ("expert_out", 6 * H * H),
        ("expert_out_bias", 6 * H),
        ("norm_gain", 6 * H),
        ("norm_bias", 6 * H),
        ("gate", 2 * H * 4),
        ("tower_in", 2 * H * TOWER1),
        ("tower_in_bias", 2 * TOWER1),
        ("tower_out", 2 * TOWER1 * TOWER2),
        ("tower_out_bias", 2 * TOWER2),
    )
    return place_names(names)


def place_names(names):
    rows = {}
    offset = 0
    for name, amount in names:
        rows[name] = offset // LANES
        offset += amount
    return rows, offset // LANES


def spread_pieces(me, rows, piece_refs, flat_ref, extra_ref=None):
    slot = 0
    for ref in piece_refs:
        for index in range(ref.shape[0]):
            owner = lax.bitwise_xor(me, jnp.int32(slot))
            block = ref[index].astype(F32)
            flat_ref[pl.ds(owner * rows, rows), :] = block[:rows]
            if extra_ref is not None:
                extra_ref[slot] = block[rows : rows + extra_ref.shape[1]]
            slot += 1


def wide_rows(flat_ref, row, amount):
    return jnp.concatenate(
        [flat_ref[pl.ds(row, amount, stride=2), :], flat_ref[pl.ds(row + 1, amount, stride=2), :]],
        axis=1,
    )


def put_wide_rows(flat_ref, row, amount, value):
    flat_ref[pl.ds(row, amount, stride=2), :] = value[:, :LANES]
    flat_ref[pl.ds(row + 1, amount, stride=2), :] = value[:, LANES:]


def collect_pieces(me, count, rows, flat_ref, out_refs):
    for slot in range(count):
        owner = lax.bitwise_xor(me, jnp.int32(slot))
        value = flat_ref[pl.ds(owner * rows, rows), :].astype(BF16)
        if len(out_refs) == 1:
            out_refs[0][slot, :rows, :] = value
        else:
            part, place = slot // 4 % 2, slot // 8 * 4 + slot % 4
            out_refs[part][place, :rows, :] = value


def roll_rows(value, columns, sign):
    item = lax.broadcasted_iota(jnp.int32, value.shape, 0)
    bit = 1
    while columns * bit % LANES:
        moved = pltpu.roll(value, sign * columns * bit % LANES, 1)
        value = jnp.where((item & bit) != 0, moved, value)
        bit *= 2
    return value


def table_places(width, columns, rows):
    item = lax.broadcasted_iota(jnp.int32, (width, rows), 0)
    index = lax.broadcasted_iota(jnp.int32, (width, rows), 1)
    first = (index == ((item * columns) >> 7)).astype(F32).astype(BF16)
    last = (index == ((item * columns + columns - 1) >> 7)).astype(F32).astype(BF16)
    item = lax.broadcasted_iota(jnp.int32, (width, LANES), 0)
    lane = lax.broadcasted_iota(jnp.int32, (width, LANES), 1)
    return first, last, lane >= ((item * columns) & (LANES - 1)), lane < columns


def table_from_rows(flat, width, columns):
    first, last, late, used = table_places(width, columns, flat.shape[0])
    chosen = jnp.where(late, mm(first, flat), mm(last, flat))
    return jnp.where(used, roll_rows(chosen, columns, -1), 0.0)


def rows_from_table(table, rows, columns):
    first, last, late, _ = table_places(table.shape[0], columns, rows)
    moved = roll_rows(table, columns, 1)
    return mm_tn(first, jnp.where(late, moved, 0.0).astype(BF16)) + mm_tn(
        last, jnp.where(late, 0.0, moved).astype(BF16)
    )


def full_spec():
    return pl.BlockSpec(memory_space=pltpu.VMEM)


def scalar_spec():
    return pl.BlockSpec(memory_space=pltpu.SMEM)


def run_kernel(
    kernel, inputs, out_shape, scratch, limit, flops, scalar=True, spec=None, out_spec=None
):
    specs = [spec or full_spec()] * len(inputs)
    if scalar:
        specs[0] = scalar_spec()
    several = isinstance(out_shape, (list, tuple))
    out_specs = [full_spec()] * len(out_shape) if several else out_spec or full_spec()
    return pl.pallas_call(
        kernel,
        in_specs=specs,
        out_specs=out_specs,
        out_shape=out_shape,
        scratch_shapes=scratch,
        compiler_params=pltpu.CompilerParams(vmem_limit_bytes=limit * 2**20),
        cost_estimate=pl.CostEstimate(flops=2**20, bytes_accessed=2**10, transcendentals=0),
    )(*inputs)


def spread_presence(presence, width):
    fields = presence.shape[0]
    field = lax.broadcasted_iota(jnp.int32, (fields, width), 0)
    column = lax.broadcasted_iota(jnp.int32, (fields, width), 1)
    pick = (column // (width // fields) == field).astype(F32).astype(BF16)
    return mm_tn(presence.astype(F32).astype(BF16), pick)


def split_three(values):
    parts = []
    for _ in range(3):
        part = values.astype(BF16).astype(F32)
        parts.append(part)
        values = values - part
    return parts


def stats_kernel(
    me_ref,
    features_hbm,
    presence_hbm,
    params_hbm,
    second_hbm,
    masked_ref,
    block_ref,
    block_two_ref,
    features_ref,
    presence_ref,
    params_ref,
    second_ref,
    sems,
):
    del me_ref
    copies = [
        pltpu.make_async_copy(source, target, sems.at[index])
        for index, (source, target) in enumerate(
            (
                (presence_hbm, presence_ref),
                (features_hbm, features_ref),
                (params_hbm, params_ref),
                (second_hbm, second_ref),
            )
        )
    ]
    for copy in copies:
        copy.start()
    for copy in copies:
        copy.wait()
    rows, width = features_ref.shape
    mask = spread_presence(presence_ref[...], width)
    masked = features_ref[...].astype(F32) * mask
    masked_ref[...] = masked.astype(BF16)
    mean = column_sum(masked) * (1.0 / rows)
    spread = masked - mean
    moment = column_sum(spread * spread)
    lines = [params_ref[...].astype(F32)]
    for value in (mean, moment):
        for part in split_three(value):
            for index in range(width // LANES):
                lines.append(part[:, index * LANES : (index + 1) * LANES])
    used = params_ref.shape[0] + 6 * (width // LANES)
    lines.append(jnp.zeros((block_ref.shape[0] - used, LANES), F32))
    block_ref[...] = jnp.concatenate(lines, axis=0).astype(BF16)
    second = second_ref[...].astype(F32)
    rest = jnp.zeros((block_two_ref.shape[0] - second.shape[0], LANES), F32)
    block_two_ref[...] = jnp.concatenate([second, rest], axis=0).astype(BF16)


def from_lanes(block):
    return jnp.concatenate([block[index : index + 1, :] for index in range(block.shape[0])], axis=1)


def tiles(tile):
    return lambda ref_rows, body: lax.fori_loop(
        0, ref_rows // tile, lambda step, carry: body(pl.multiple_of(step * tile, tile), carry), 0
    )


def in_turn(first, second):
    for e in range(8):
        if e < 6:
            first(e)
        if e > 1:
            second(e - 2)


def spot(e):
    return slice(e * H, (e + 1) * H)


def level_one_forward(
    rows,
    tile,
    n_pieces,
    me_ref,
    masked_ref,
    *rest,
):
    piece_refs = rest[:n_pieces]
    (
        level_ref,
        active_ref,
        slope_ref,
        normal_ref,
        scale_ref,
        probs_ref,
        mixed_ref,
        w_in_ref,
        w_out_ref,
        small_ref,
        gate_ref,
        entry_ref,
        flat_ref,
        extra_ref,
        output_ref,
        wide_ref,
        spread_ref,
    ) = rest[n_pieces:]
    width = masked_ref.shape[1]
    where_row, _ = first_layout(width)

    spread_pieces(me_ref[0], rows, piece_refs, flat_ref, extra_ref)
    spread_ref[...] = make_spread(14)
    for e in range(6):
        w_in_ref[:, spot(e)] = wide_rows(
            flat_ref, where_row["expert_in"] + e * 2 * width, width
        ).astype(BF16)
        w_out_ref[e] = wide_rows(flat_ref, where_row["expert_out"] + e * 2 * H, H).astype(BF16)
    for index, name in enumerate(("expert_in_bias", "expert_out_bias", "norm_gain", "norm_bias")):
        small_ref[index, :6, :] = wide_rows(flat_ref, where_row[name], 6)
    gate_flat = flat_ref[pl.ds(where_row["gate"], 14 * width // LANES), :].astype(BF16)
    gate_ref[...] = table_from_rows(gate_flat, width, 14).astype(BF16)
    lanes = width // LANES
    events = masked_ref.shape[0]
    count = extra_ref.shape[0]
    means = extra_ref[:, 0:lanes, :]
    for part in (1, 2):
        means = means + extra_ref[:, part * lanes : (part + 1) * lanes, :]
    mean = jnp.sum(means, axis=0) * (1.0 / count)
    away = jnp.sum(jnp.square(means - mean[None]), axis=0) * events
    for part in (3, 4, 5):
        away = away + jnp.sum(extra_ref[:, part * lanes : (part + 1) * lanes, :], axis=0)
    entry_ref[0:1, :] = from_lanes(mean)
    entry_ref[1:2, :] = from_lanes(lax.rsqrt(away * (1.0 / (events * count)) + EPSILON))
    entry_ref[2:3, :] = from_lanes(flat_ref[0:lanes, :])
    entry_ref[3:4, :] = from_lanes(flat_ref[lanes : 2 * lanes, :])

    def body(start, carry):
        now = pl.ds(start, tile)
        normed = (masked_ref[now, :].astype(F32) - entry_ref[0:1, :]) * entry_ref[1:2, :]
        level_ref[now, :] = (normed * entry_ref[2:3, :] + entry_ref[3:4, :]).astype(BF16)
        probs_ref[now, :] = group_softmax(mm(level_ref[now, :], gate_ref[...]), GROUPS_ONE)
        def first_half(e):
            pre = mm(level_ref[now, :], w_in_ref[:, spot(e)]) + small_ref[0, e : e + 1, :]
            gate = sigmoid(pre)
            silu = pre * gate
            active_ref[e, now, :] = silu.astype(BF16)
            slope_ref[e, now, :] = (gate + silu * (1.0 - gate)).astype(BF16)

        def second_half(e):
            post = mm(active_ref[e, now, :], w_out_ref[e]) + small_ref[1, e : e + 1, :]
            normal, scale = norm_forward(post)
            normal_ref[e, now, :] = normal.astype(BF16)
            scale_ref[e, now, :] = jnp.broadcast_to(scale, (tile, LANES))
            output_ref[e] = normal * small_ref[2, e : e + 1, :] + small_ref[3, e : e + 1, :]

        in_turn(first_half, second_half)
        wide_ref[...] = spread_columns(probs_ref[now, :], spread_ref[...])
        for index, (low, _) in enumerate(GROUPS_ONE):
            mixed_ref[index, now, :] = mix_parts(
                wide_ref, low, MEMBERS_ONE[index], output_ref
            ).astype(BF16)
        return carry

    tiles(tile)(masked_ref.shape[0], body)


def level_two(count, rows, tile, n_pieces, n_outs, me_ref, mixed_ref, cotangent_ref, *rest):
    piece_refs = rest[:n_pieces]
    grads_refs = rest[n_pieces + 2 : n_pieces + 2 + n_outs]
    towers_ref, mixed_grad_ref = rest[n_pieces : n_pieces + 2]
    (
        flat_ref,
        w_in_ref,
        w_out_ref,
        small_ref,
        gate_ref,
        tower_in_ref,
        tower_out_ref,
        tower_tmp_ref,
        tower_small_ref,
        g_small_ref,
        g_tower_out_ref,
        g_tower_small_ref,
        active_ref,
        slope_ref,
        normal_ref,
        scale_ref,
        output_ref,
        combined_ref,
        combined_grad_ref,
        tower_active_ref,
        tower_grad_ref,
        logit_ref,
        post_grad_ref,
        pre_grad_ref,
        wide_ref,
        spread_ref,
        means_ref,
    ) = rest[n_pieces + 2 + n_outs :]
    where_row, used_rows = second_layout()
    all_rows = mixed_ref.shape[1]

    spread_pieces(me_ref[0], rows, piece_refs, flat_ref)
    spread_ref[...] = make_spread(8)
    means_ref[...] = make_means()
    for e in range(6):
        w_in_ref[:, spot(e)] = wide_rows(flat_ref, where_row["expert_in"] + e * 2 * H, H).astype(
            BF16
        )
        w_out_ref[e] = wide_rows(flat_ref, where_row["expert_out"] + e * 2 * H, H).astype(BF16)
    for index, name in enumerate(("expert_in_bias", "expert_out_bias", "norm_gain", "norm_bias")):
        small_ref[index, :6, :] = wide_rows(flat_ref, where_row[name], 6)
    gate_rows = H * 4 // LANES
    shift_a = lax.broadcasted_iota(jnp.int32, (LANES, LANES), 0)
    shift_b = lax.broadcasted_iota(jnp.int32, (LANES, LANES), 1)
    shift = ((shift_a + 4 == shift_b) & (shift_a < 4)).astype(F32).astype(BF16)
    tables = []
    for task in range(2):
        piece = flat_ref[pl.ds(where_row["gate"] + task * gate_rows, gate_rows), :].astype(BF16)
        tables.append(table_from_rows(piece, H, 4).astype(BF16))
    gate_ref[...] = (tables[0].astype(F32) + mm(tables[1], shift)).astype(BF16)
    zero = jnp.zeros((TOWER1 // 2, TOWER2), F32)
    for task in range(2):
        tower_in_ref[task] = flat_ref[pl.ds(where_row["tower_in"] + task * H, H), :].astype(BF16)
        packed = flat_ref[pl.ds(where_row["tower_out"] + task * TOWER1 // 2, TOWER1 // 2), :]
        for half in range(2):
            pair = [packed[:, half * TOWER2 : (half + 1) * TOWER2], zero]
            if task == 1:
                pair.reverse()
            tower_tmp_ref[pl.ds(task * TOWER1 + half, TOWER1 // 2, stride=2), :] = jnp.concatenate(
                pair, axis=1
            )
    tower_out_ref[...] = tower_tmp_ref[: 2 * TOWER1, :].astype(BF16)
    tower_small_ref[0:1, :] = from_lanes(flat_ref[pl.ds(where_row["tower_in_bias"], 2), :])
    tower_small_ref[1:2, :LANES] = flat_ref[pl.ds(where_row["tower_out_bias"], 1), :]
    g_small_ref[...] = jnp.zeros(g_small_ref.shape, F32)
    g_tower_small_ref[...] = jnp.zeros(g_tower_small_ref.shape, F32)

    def body(start, carry):
        now = pl.ds(start, tile)
        lane = lax.broadcasted_iota(jnp.int32, (tile, LANES), 1)
        def first_half(e):
            pre = mm(mixed_ref[e // 2, now, :], w_in_ref[:, spot(e)]) + small_ref[0, e : e + 1, :]
            gate = sigmoid(pre)
            silu = pre * gate
            active_ref[e, now, :] = silu.astype(BF16)
            slope_ref[:, spot(e)] = gate + silu * (1.0 - gate)

        def second_half(e):
            post = mm(active_ref[e, now, :], w_out_ref[e]) + small_ref[1, e : e + 1, :]
            normal, scale = norm_forward(post)
            normal_ref[e] = normal
            scale_ref[e] = jnp.broadcast_to(scale, (tile, LANES))
            output_ref[e] = normal * small_ref[2, e : e + 1, :] + small_ref[3, e : e + 1, :]

        in_turn(first_half, second_half)
        logits = jnp.where(
            lane < 4, mm(mixed_ref[0, now, :], gate_ref[...]), mm(mixed_ref[1, now, :], gate_ref[...])
        )
        probs = group_softmax(logits, GROUPS_TWO)
        wide_ref[...] = spread_columns(probs, spread_ref[...])
        for task in range(2):
            combined_ref[task, now, :] = mix_parts(
                wide_ref, 4 * task, MEMBERS_TWO[task], output_ref
            ).astype(BF16)
        tower_pre = (
            jnp.concatenate(
                [mm(combined_ref[task, now, :], tower_in_ref[task]) for task in range(2)], axis=1
            )
            + tower_small_ref[0:1, :]
        )
        tower_gate = sigmoid(tower_pre)
        tower_silu = tower_pre * tower_gate
        tower_active_ref[now, :] = tower_silu.astype(BF16)
        towers_ref[now, :] = (
            mm(tower_active_ref[now, :], tower_out_ref[...]) + tower_small_ref[1:2, :LANES]
        )
        cotangent = cotangent_ref[now, :]
        g_tower_small_ref[1:2, :LANES] += column_sum(cotangent.astype(F32))
        tower_slope = tower_gate + tower_silu * (1.0 - tower_gate)
        tower_grad = (mm_nt(cotangent, tower_out_ref[...]) * tower_slope).astype(BF16)
        tower_grad_ref[now, :] = tower_grad
        g_tower_small_ref[0:1, :] += column_sum(tower_grad.astype(F32))
        for task in range(2):
            combined_grad_ref[task] = mm_nt(
                tower_grad_ref[now, task * TOWER1 : (task + 1) * TOWER1], tower_in_ref[task]
            )
        prob_grads = into_lane(
            [
                row_sum(combined_grad_ref[task] * output_ref[member])
                for task in range(2)
                for member in MEMBERS_TWO[task]
            ]
        )
        logit_grad = group_softmax_back(probs, prob_grads, GROUPS_TWO)
        logit_ref[0, now, :] = jnp.where(lane < 4, logit_grad, 0.0).astype(BF16)
        logit_ref[1, now, :] = jnp.where((lane >= 4) & (lane < 8), logit_grad, 0.0).astype(BF16)
        def norm_half(e):
            out_grad = None
            for task in range(2):
                if e in MEMBERS_TWO[task]:
                    column = 4 * task + MEMBERS_TWO[task].index(e)
                    term = column_block(wide_ref, column) * combined_grad_ref[task]
                    out_grad = term if out_grad is None else out_grad + term
            normal = normal_ref[e]
            g_small_ref[2, e : e + 1, :] += column_sum(out_grad * normal)
            g_small_ref[3, e : e + 1, :] += column_sum(out_grad)
            post_grad = norm_backward(
                out_grad * small_ref[2, e : e + 1, :], normal, scale_ref[e], means_ref[...]
            )
            post_grad_ref[e, now, :] = post_grad.astype(BF16)
            g_small_ref[1, e : e + 1, :] += column_sum(post_grad)

        def active_half(e):
            act_grad = mm_nt(post_grad_ref[e, now, :], w_out_ref[e])
            pre_grad = act_grad * slope_ref[:, spot(e)]
            pre_grad_ref[now, spot(e)] = pre_grad.astype(BF16)
            g_small_ref[0, e : e + 1, :] += column_sum(pre_grad)

        in_turn(norm_half, active_half)
        for index in range(3):
            pair = slice(2 * index * H, 2 * (index + 1) * H)
            grad = mm_nt(pre_grad_ref[now, pair], w_in_ref[:, pair])
            if index < 2:
                grad = grad + mm_nt(logit_ref[index, now, :], gate_ref[...])
            mixed_grad_ref[index, now, :] = grad
        return carry

    tiles(tile)(all_rows, body)

    for e in range(6):
        put_wide_rows(
            flat_ref,
            where_row["expert_in"] + e * 2 * H,
            H,
            mm_tn(mixed_ref[e // 2], pre_grad_ref[:, spot(e)]),
        )
        put_wide_rows(
            flat_ref,
            where_row["expert_out"] + e * 2 * H,
            H,
            mm_tn(active_ref[e], post_grad_ref[e]),
        )
    for index, name in enumerate(("expert_in_bias", "expert_out_bias", "norm_gain", "norm_bias")):
        put_wide_rows(flat_ref, where_row[name], 6, g_small_ref[index, :6, :])
    back = ((shift_a == shift_b + 4) & (shift_b < 4)).astype(F32).astype(BF16)
    tables = [mm_tn(mixed_ref[task], logit_ref[task]) for task in range(2)]
    tables[1] = mm(tables[1].astype(BF16), back)
    g_tower_out_ref[: 2 * TOWER1, :] = mm_tn(tower_active_ref[...], cotangent_ref[...])
    for task in range(2):
        flat_ref[pl.ds(where_row["gate"] + task * gate_rows, gate_rows), :] = rows_from_table(
            tables[task], gate_rows, 4
        )
        flat_ref[pl.ds(where_row["tower_in"] + task * H, H), :] = mm_tn(
            combined_ref[task], tower_grad_ref[:, task * TOWER1 : (task + 1) * TOWER1]
        )
        flat_ref[pl.ds(where_row["tower_out"] + task * TOWER1 // 2, TOWER1 // 2), :] = (
            jnp.concatenate(
                [
                    g_tower_out_ref[pl.ds(task * TOWER1 + half, TOWER1 // 2, stride=2), :][
                        :, task * TOWER2 : (task + 1) * TOWER2
                    ]
                    for half in range(2)
                ],
                axis=1,
            )
        )
        flat_ref[pl.ds(where_row["tower_in_bias"] + task, 1), :] = g_tower_small_ref[
            0:1, task * TOWER1 : (task + 1) * TOWER1
        ]
    flat_ref[pl.ds(where_row["tower_out_bias"], 1), :] = g_tower_small_ref[1:2, :LANES]
    if used_rows < count * rows:
        flat_ref[pl.ds(used_rows, count * rows - used_rows), :] = jnp.zeros(
            (count * rows - used_rows, LANES), F32
        )
    collect_pieces(me_ref[0], count, rows, flat_ref, grads_refs)


def level_one_backward(
    tile,
    begin,
    mixed_grad_ref,
    masked_ref,
    slope_ref,
    normal_ref,
    scale_ref,
    probs_ref,
    w_in_ref,
    w_out_ref,
    small_ref,
    gate_ref,
    entry_ref,
    *rest,
):
    if begin:
        before_sum_ref, before_small_ref, *rest = rest
    (
        level_grad_ref,
        g_sum_ref,
        g_small_ref,
        logit_ref,
        post_grad_ref,
        pre_grad_ref,
        wide_ref,
        spread_ref,
        means_ref,
    ) = rest
    spread_ref[...] = make_spread(14)
    means_ref[...] = make_means()
    if begin:
        g_small_ref[...] = before_small_ref[...]
        g_sum_ref[...] = before_sum_ref[...]
    else:
        g_small_ref[...] = jnp.zeros(g_small_ref.shape, F32)
        g_sum_ref[...] = jnp.zeros(g_sum_ref.shape, F32)

    def body(start, carry):
        here = pl.ds(start, tile)
        now = pl.ds(begin + start, tile)
        probs = probs_ref[now, :]
        wide_ref[...] = spread_columns(probs, spread_ref[...])
        columns = [None] * 14
        for e in range(6):
            output = (
                normal_ref[e, now, :].astype(F32) * small_ref[2, e : e + 1, :]
                + small_ref[3, e : e + 1, :]
            )
            for index, (low, _) in enumerate(GROUPS_ONE):
                if e in MEMBERS_ONE[index]:
                    columns[low + MEMBERS_ONE[index].index(e)] = row_sum(
                        mixed_grad_ref[index, now, :] * output
                    )
        logit_ref[here, :] = group_softmax_back(probs, into_lane(columns), GROUPS_ONE).astype(BF16)
        def norm_half(e):
            normal = normal_ref[e, now, :].astype(F32)
            out_grad = None
            for index, (low, _) in enumerate(GROUPS_ONE):
                if e in MEMBERS_ONE[index]:
                    column = low + MEMBERS_ONE[index].index(e)
                    term = column_block(wide_ref, column) * mixed_grad_ref[index, now, :]
                    out_grad = term if out_grad is None else out_grad + term
            g_small_ref[2, e : e + 1, :] += column_sum(out_grad * normal)
            g_small_ref[3, e : e + 1, :] += column_sum(out_grad)
            post_grad = norm_backward(
                out_grad * small_ref[2, e : e + 1, :],
                normal,
                scale_ref[e, now, :],
                means_ref[...],
            )
            post_grad_ref[e, here, :] = post_grad.astype(BF16)
            g_small_ref[1, e : e + 1, :] += column_sum(post_grad)

        def active_half(e):
            act_grad = mm_nt(post_grad_ref[e, here, :], w_out_ref[e])
            pre_grad = act_grad * slope_ref[e, now, :].astype(F32)
            pre_grad_ref[here, spot(e)] = pre_grad.astype(BF16)
            g_small_ref[0, e : e + 1, :] += column_sum(pre_grad)

        in_turn(norm_half, active_half)
        level_grad = mm_nt(pre_grad_ref[here, :], w_in_ref[...]) + mm_nt(
            logit_ref[here, :], gate_ref[...]
        )
        level_grad_ref[here, :] = level_grad
        normed = (masked_ref[now, :].astype(F32) - entry_ref[0:1, :]) * entry_ref[1:2, :]
        g_sum_ref[0:1, :] += column_sum(level_grad * normed)
        g_sum_ref[1:2, :] += column_sum(level_grad)
        return carry

    tiles(tile)(logit_ref.shape[0], body)


def send_sums(sums, block_refs):
    high = sums.astype(BF16).astype(F32)
    lines = []
    for value in (high, sums - high):
        for row in range(2):
            for index in range(value.shape[1] // LANES):
                lines.append(value[row : row + 1, index * LANES : (index + 1) * LANES])
    block = jnp.concatenate(lines, axis=0).astype(BF16)
    for ref in block_refs:
        ref[ref.shape[0] - 16 :, :] = block


def got_sums(block_ref, shape):
    rows = block_ref.shape[0]
    block = block_ref[rows - 16 :, :].astype(F32)
    block = block[:8] + block[8:]
    lanes = shape[1] // LANES
    lines = [from_lanes(block[row * lanes : (row + 1) * lanes]) for row in range(2)]
    return jnp.concatenate(lines + [jnp.zeros((shape[0] - 2, shape[1]), F32)], axis=0)


def level_one_weights(
    count,
    rows,
    me_ref,
    level_ref,
    active_ref,
    sums_ref,
    small_ref,
    logit_a_ref,
    logit_b_ref,
    post_a_ref,
    post_b_ref,
    pre_a_ref,
    pre_b_ref,
    *rest,
):
    *grads_refs, flat_ref = rest
    width = level_ref.shape[1]
    lanes = width // LANES
    where_row, used_rows = first_layout(width)
    half = logit_a_ref.shape[0]
    one, two = slice(0, half), slice(half, level_ref.shape[0])
    for e in range(6):
        put_wide_rows(
            flat_ref,
            where_row["expert_in"] + e * 2 * width,
            width,
            mm_tn(level_ref[one, :], pre_a_ref[:, spot(e)])
            + mm_tn(level_ref[two, :], pre_b_ref[:, spot(e)]),
        )
        put_wide_rows(
            flat_ref,
            where_row["expert_out"] + e * 2 * H,
            H,
            mm_tn(active_ref[e, one, :], post_a_ref[e])
            + mm_tn(active_ref[e, two, :], post_b_ref[e]),
        )
    for index, name in enumerate(("expert_in_bias", "expert_out_bias", "norm_gain", "norm_bias")):
        put_wide_rows(flat_ref, where_row[name], 6, small_ref[index, :6, :])
    gate_rows = 14 * width // LANES
    gate = mm_tn(level_ref[one, :], logit_a_ref[...]) + mm_tn(level_ref[two, :], logit_b_ref[...])
    flat_ref[pl.ds(where_row["gate"], gate_rows), :] = rows_from_table(gate, gate_rows, 14)
    flat_ref[0 : 2 * lanes, :] = jnp.zeros((2 * lanes, LANES), F32)
    if used_rows < count * rows:
        flat_ref[pl.ds(used_rows, count * rows - used_rows), :] = jnp.zeros(
            (count * rows - used_rows, LANES), F32
        )
    collect_pieces(me_ref[0], count, rows, flat_ref, grads_refs)
    if len(grads_refs) > 1:
        send_sums(sums_ref[...], [grads_refs[1].at[0]])


def input_kernel(
    total_rows,
    parts,
    grad_a_ref,
    grad_b_ref,
    masked_ref,
    presence_ref,
    entry_ref,
    sums_ref,
    out_hbm,
    out_ref,
    sems,
):
    rows, width = masked_ref.shape
    inv_scale = entry_ref[1:2, :]
    factor = inv_scale * entry_ref[2:3, :]
    cross = sums_ref[0:1, :] * (1.0 / total_rows)
    plain = sums_ref[1:2, :] * (1.0 / total_rows)
    each = rows // parts
    copies = []
    for part in range(parts):
        now = pl.ds(part * each, each)
        first = grad_a_ref.shape[0] // each
        ref = grad_a_ref if part < first else grad_b_ref
        grad = ref[pl.ds((part if part < first else part - first) * each, each), :]
        mask = spread_presence(presence_ref[:, now], width)
        normed = (masked_ref[now, :].astype(F32) - entry_ref[0:1, :]) * inv_scale
        out_ref[now, :] = mask * (factor * (grad - plain - normed * cross))
        copies.append(pltpu.make_async_copy(out_ref.at[now], out_hbm.at[now], sems.at[part]))
        copies[-1].start()
    for copy in copies:
        copy.wait()


def xor_permute(value, axis, bit):
    size = lax.axis_size(axis)
    return lax.ppermute(value, axis, [(index, index ^ bit) for index in range(size)])


def hypercube_ok():
    wide, narrow = lax.axis_size("wide"), lax.axis_size("narrow")
    return wide == 8 and narrow == 4


def after(value, *others):
    return lax.optimization_barrier((value, *others))[0]


def small_kernel(kernel, inputs, out_shape, scalar=False):
    return run_kernel(kernel, inputs, out_shape, [], 8, 2**20, scalar=scalar)


def stack_kernel(*refs):
    sources, targets = refs[:4], refs[4:]
    each = 4 // len(targets)
    for index, ref in enumerate(sources):
        targets[index // each][index % each] = ref[...]


def gather_near(block):
    return [block] + [xor_permute(block, "narrow", k) for k in (1, 2, 3)]


def stack_near(near, parts):
    rows = near[0].shape[0]
    shapes = [jax.ShapeDtypeStruct((4 // parts, rows, LANES), BF16)] * parts
    return small_kernel(stack_kernel, near, shapes)


def gather_halves(first, second):
    first_y, second_x = xor_permute(first, "wide", 4), xor_permute(second, "wide", 2)
    first_x, second_y = xor_permute(first, "wide", 2), xor_permute(second, "wide", 4)
    first_xy, second_xy = xor_permute(first_y, "wide", 2), xor_permute(second_x, "wide", 4)
    own = [first, second, first_x, second_x, first_y, second_y, first_xy, second_xy]
    other = [xor_permute(piece, "wide", 1) for piece in own]
    pieces = []
    for index in range(4):
        pieces += [own[2 * index], own[2 * index + 1], other[2 * index], other[2 * index + 1]]
    return pieces


def gather_plane(stack):
    return [stack] + [xor_permute(stack, "wide", bit) for bit in (2, 4, 6)]


def gather_core(own):
    pieces = []
    for piece in own:
        pieces += [piece, xor_permute(piece, "wide", 1)]
    return pieces


def core_direct_kernel(keep_ref, got_ref, own_ref, *send_refs):
    total = keep_ref[...].astype(F32) + got_ref[...].astype(F32)
    own_ref[...] = total[0:4]
    for part, ref in enumerate(send_refs):
        ref[...] = total[4 * (part + 1) : 4 * (part + 2)].astype(BF16)


def plane_direct_kernel(own_ref, one_ref, two_ref, three_ref, keep_ref, *send_refs):
    total = own_ref[...]
    for ref in (one_ref, two_ref, three_ref):
        total = total + ref[...].astype(F32)
    keep_ref[...] = total[0]
    for part, ref in enumerate(send_refs):
        ref[...] = total[part + 1].astype(BF16)


def last_kernel(own_ref, one_ref, two_ref, three_ref, out_ref):
    total = own_ref[...]
    for ref in (one_ref, two_ref, three_ref):
        total = total + ref[...].astype(F32)
    out_ref[...] = total[: out_ref.shape[0]]


def last_head_kernel(
    me_ref, sums_ref, own_ref, one_ref, two_ref, three_ref, out_ref, total_ref
):
    last_kernel(own_ref, one_ref, two_ref, three_ref, out_ref)
    sums = sums_ref[...]
    for ref in (one_ref, two_ref, three_ref):
        sums = sums + got_sums(ref, sums.shape)
    total_ref[...] = sums
    put_head(me_ref, total_ref, out_ref)


def put_head(me_ref, sums_ref, out_ref):
    @pl.when(me_ref[0] == 0)
    def _():
        lanes = sums_ref.shape[1] // LANES
        for index in range(2 * lanes):
            part = slice(index % lanes * LANES, (index % lanes + 1) * LANES)
            row = index // lanes
            out_ref[index : index + 1, :] = sums_ref[row : row + 1, part]


def head_kernel(me_ref, sums_ref, block_ref, out_ref):
    out_ref[...] = block_ref[...]
    put_head(me_ref, sums_ref, out_ref)


def core_halves_kernel(
    keep_ref, got_ref, sums_ref, one_ref, two_ref, out_ref, send_one_ref, send_two_ref
):
    total = keep_ref[...].astype(F32) + got_ref[...].astype(F32)
    for x in range(2):
        for z in range(2):
            one_ref[2 * x + z] = total[4 * x + z]
            send_one_ref[2 * x + z] = total[8 + 4 * x + z].astype(BF16)
    for y in range(2):
        for z in range(2):
            two_ref[2 * y + z] = total[8 * y + 2 + z]
            send_two_ref[2 * y + z] = total[8 * y + 4 + 2 + z].astype(BF16)
    sums = sums_ref[...] + got_sums(got_ref.at[0], sums_ref.shape)
    out_ref[...] = sums
    send_sums(sums, [send_one_ref.at[0]])


def plane_halves_kernel(
    one_ref,
    two_ref,
    got_one_ref,
    got_two_ref,
    sums_ref,
    keep_one_ref,
    keep_two_ref,
    out_ref,
    send_one_ref,
    send_two_ref,
):
    for ref, got, keep, send in (
        (one_ref, got_one_ref, keep_one_ref, send_one_ref),
        (two_ref, got_two_ref, keep_two_ref, send_two_ref),
    ):
        total = ref[...] + got[...].astype(F32)
        keep[...] = total[0:2]
        send[...] = total[2:4].astype(BF16)
    sums = sums_ref[...] + got_sums(got_one_ref.at[0], sums_ref.shape)
    out_ref[...] = sums
    send_sums(sums, [send_one_ref.at[0]])


def near_halves_kernel(
    one_ref,
    two_ref,
    got_one_ref,
    got_two_ref,
    sums_ref,
    keep_ref,
    out_ref,
    send_one_ref,
    send_two_ref,
    send_three_ref,
):
    one = one_ref[...] + got_one_ref[...].astype(F32)
    two = two_ref[...] + got_two_ref[...].astype(F32)
    keep_ref[...] = one[0]
    send_one_ref[...] = one[1].astype(BF16)
    send_two_ref[...] = two[0].astype(BF16)
    send_three_ref[...] = two[1].astype(BF16)
    sums = sums_ref[...] + got_sums(got_one_ref.at[0], sums_ref.shape)
    out_ref[...] = sums
    send_sums(sums, [send_one_ref, send_two_ref, send_three_ref])


def scatter_plain(value):
    return lax.psum_scatter(value.astype(F32), AXES, scatter_dimension=0, tiled=True)[0]


def per_device(features, presence, first_params, second_params, cotangent):
    rows, width = features.shape
    lanes = width // LANES
    devices_all = count = lax.axis_size(AXES)
    total_rows = rows * devices_all
    cube = hypercube_ok()
    tile = math.gcd(rows, 256)
    sizes = (rows // 4, rows - rows // 4)
    big = math.gcd(rows, 512)
    me = lax.axis_index(AXES).astype(jnp.int32).reshape(1)
    chunks = [first_params.shape[0] // LANES, second_params.shape[0] // LANES]
    extra = 6 * lanes
    shape = jax.ShapeDtypeStruct
    fields = presence.T
    blocks = [up(chunks[0], 16) + (16 if cube else 0), up(chunks[1], 16)]

    masked, block_one, block_two = run_kernel(
        stats_kernel,
        [
            me,
            features,
            fields,
            first_params.reshape(chunks[0], LANES),
            second_params.reshape(chunks[1], LANES),
        ],
        (
            pltpu.VMEM((rows, width), BF16),
            pltpu.VMEM((up(chunks[0] + extra, 16), LANES), BF16),
            pltpu.VMEM((blocks[1], LANES), BF16),
        ),
        [
            pltpu.VMEM((rows, width), BF16),
            pltpu.VMEM(fields.shape, jnp.int32),
            pltpu.VMEM((chunks[0], LANES), BF16),
            pltpu.VMEM((chunks[1], LANES), BF16),
            pltpu.SemaphoreType.DMA((4,)),
        ],
        60,
        rows * width * 10,
        spec=pl.BlockSpec(memory_space=pltpu.HBM),
    )
    if cube:
        origin = me
        near_one = gather_near(block_one)
        first, second = stack_near(near_one, 2)
        near_two = gather_near(after(block_two, first))
        pieces_one = gather_halves(first, second)
        near_two[3] = after(near_two[3], pieces_one[12], pieces_one[13])
        (stack_two,) = stack_near(near_two, 1)
        plane_two = gather_plane(after(stack_two, pieces_one[12], pieces_one[13]))
        masked = after(masked, stack_two)
    else:
        origin = jnp.zeros((1,), jnp.int32)
        pieces_one = [lax.all_gather(block_one, AXES)]
        plane_two = [lax.all_gather(block_two, AXES)]

    saved = run_kernel(
        functools.partial(level_one_forward, chunks[0], big, len(pieces_one)),
        [origin, masked] + pieces_one,
        [
            shape((rows, width), BF16),
            shape((6, rows, H), BF16),
            shape((6, rows, H), BF16),
            shape((6, rows, H), BF16),
            shape((6, rows, LANES), F32),
            shape((rows, LANES), F32),
            shape((3, rows, H), BF16),
            shape((width, 6 * H), BF16),
            shape((6, H, H), BF16),
            shape((4, 8, H), F32),
            shape((width, LANES), BF16),
            shape((8, width), F32),
        ],
        [
            pltpu.VMEM((up(count * chunks[0], 8) + 16, LANES), F32),
            pltpu.VMEM((count, extra, LANES), F32),
            pltpu.VMEM((6, big, H), F32),
            pltpu.VMEM((big, 14 * LANES), F32),
            pltpu.VMEM((2 * LANES, 14 * LANES), BF16),
        ],
        28,
        rows * 6 * (width + H) * H * 2,
    )
    level, active, slope, normal, scale, probs, mixed, w_in, w_out, small, gate, entry = saved
    pieces_two = gather_core([after(piece, entry) for piece in plane_two]) if cube else plane_two

    outs = 2 if cube else 1
    towers, mixed_grad, *grads_two = run_kernel(
        functools.partial(level_two, count, chunks[1], tile, len(pieces_two), outs),
        [origin, mixed, cotangent] + pieces_two,
        [
            shape((rows, LANES), F32),
            shape((3, rows, H), F32),
        ]
        + [shape((count // outs, blocks[1], LANES), BF16)] * outs,
        [
            pltpu.VMEM((up(count * chunks[1], 8) + 16, LANES), F32),
            pltpu.VMEM((H, 6 * H), BF16),
            pltpu.VMEM((6, H, H), BF16),
            pltpu.VMEM((4, 8, H), F32),
            pltpu.VMEM((H, LANES), BF16),
            pltpu.VMEM((2, H, TOWER1), BF16),
            pltpu.VMEM((2 * TOWER1, LANES), BF16),
            pltpu.VMEM((2 * TOWER1 + 16, LANES), F32),
            pltpu.VMEM((8, 2 * TOWER1), F32),
            pltpu.VMEM((4, 8, H), F32),
            pltpu.VMEM((2 * TOWER1 + 16, LANES), F32),
            pltpu.VMEM((8, 2 * TOWER1), F32),
            pltpu.VMEM((6, rows, H), BF16),
            pltpu.VMEM((tile, 6 * H), F32),
            pltpu.VMEM((6, tile, H), F32),
            pltpu.VMEM((6, tile, LANES), F32),
            pltpu.VMEM((6, tile, H), F32),
            pltpu.VMEM((2, rows, H), BF16),
            pltpu.VMEM((2, tile, H), F32),
            pltpu.VMEM((rows, 2 * TOWER1), BF16),
            pltpu.VMEM((rows, 2 * TOWER1), BF16),
            pltpu.VMEM((2, rows, LANES), BF16),
            pltpu.VMEM((6, rows, H), BF16),
            pltpu.VMEM((rows, 6 * H), BF16),
            pltpu.VMEM((tile, 8 * LANES), F32),
            pltpu.VMEM((2 * LANES, 8 * LANES), BF16),
            pltpu.VMEM((2 * H, 2 * LANES), BF16),
        ],
        28,
        rows * 6 * 2 * H * H * 2 * 3,
    )
    def backward(part, *before):
        return run_kernel(
            functools.partial(level_one_backward, math.gcd(big, sizes[part]), part * sizes[0]),
            [
                mixed_grad,
                masked,
                slope,
                normal,
                scale,
                probs,
                w_in,
                w_out,
                small,
                gate,
                entry,
                *before,
            ],
            [
                shape((sizes[part], width), F32),
                shape((8, width), F32),
                shape((4, 8, H), F32),
                shape((sizes[part], LANES), BF16),
                shape((6, sizes[part], H), BF16),
                shape((sizes[part], 6 * H), BF16),
            ],
            [
                pltpu.VMEM((math.gcd(big, sizes[part]), 14 * LANES), F32),
                pltpu.VMEM((2 * LANES, 14 * LANES), BF16),
                pltpu.VMEM((2 * H, 2 * LANES), BF16),
            ],
            16,
            rows * 6 * (width + H) * H * 2,
            scalar=False,
        )

    grad_a, sums, g_small, logit_a, post_a, pre_a = backward(0)
    if cube:
        keep_two, send_two = grads_two
        own_two, *sends_two = small_kernel(
            core_direct_kernel,
            [after(keep_two, sums), xor_permute(send_two, "wide", 1)],
            [shape((4, blocks[1], LANES), F32)] + [shape((4, blocks[1], LANES), BF16)] * 3,
        )
        sums = after(sums, own_two)
    grad_b, sums, g_small, logit_b, post_b, pre_b = backward(1, sums, g_small)
    grads_one = run_kernel(
        functools.partial(level_one_weights, count, chunks[0]),
        [
            origin,
            level,
            active,
            sums,
            g_small,
            logit_a,
            logit_b,
            post_a,
            post_b,
            pre_a,
            pre_b,
        ],
        [shape((count // outs, blocks[0], LANES), BF16)] * outs,
        [pltpu.VMEM((up(count * chunks[0], 8) + 16, LANES), F32)],
        12,
        rows * 6 * (width + H) * H * 2,
    )
    if cube:
        keep_two, *sends_two = small_kernel(
            plane_direct_kernel,
            [own_two]
            + [xor_permute(part, "wide", bit) for part, bit in zip(sends_two, (2, 4, 6))],
            [shape((blocks[1], LANES), F32)] + [shape((blocks[1], LANES), BF16)] * 3,
        )
        summed = shape((8, width), F32)
        low, high = shape((4, blocks[0], LANES), BF16), shape((4, blocks[0], LANES), F32)
        keep, send = grads_one
        one, two, sums, send_one, send_two = small_kernel(
            core_halves_kernel,
            [keep, xor_permute(after(send, keep_two), "wide", 1), sums],
            [high, high, summed, low, low],
        )
        second_grad = small_kernel(
            last_kernel,
            [keep_two]
            + [xor_permute(part, "narrow", k) for part, k in zip(sends_two, (1, 2, 3))],
            shape((chunks[1], LANES), F32),
        )
        low, high = shape((2, blocks[0], LANES), BF16), shape((2, blocks[0], LANES), F32)
        one, two, sums, send_one, send_two = small_kernel(
            plane_halves_kernel,
            [
                after(one, second_grad),
                two,
                xor_permute(send_one, "wide", 4),
                xor_permute(send_two, "wide", 2),
                sums,
            ],
            [high, high, summed, low, low],
        )
        low, high = shape((blocks[0], LANES), BF16), shape((blocks[0], LANES), F32)
        keep, sums, *sends = small_kernel(
            near_halves_kernel,
            [
                one,
                two,
                xor_permute(send_one, "wide", 2),
                xor_permute(send_two, "wide", 4),
                sums,
            ],
            [high, summed, low, low, low],
        )
        first_grad, sums = small_kernel(
            last_head_kernel,
            [me, sums, keep]
            + [xor_permute(part, "narrow", k) for part, k in zip(sends, (1, 2, 3))],
            [shape((chunks[0], LANES), F32), summed],
            scalar=True,
        )
    else:
        sums = lax.psum(sums, AXES)
        second_grad = scatter_plain(grads_two[0])[: chunks[1]]
        first_grad = small_kernel(
            head_kernel,
            [me, sums, scatter_plain(grads_one[0])[: chunks[0]]],
            shape((chunks[0], LANES), F32),
            scalar=True,
        )

    parts = 8 if rows % 1024 == 0 else 4
    input_grad = run_kernel(
        functools.partial(input_kernel, float(total_rows), parts),
        [grad_a, grad_b, masked, fields, entry, sums],
        shape((rows, width), F32),
        [pltpu.VMEM((rows, width), F32), pltpu.SemaphoreType.DMA((parts,))],
        8,
        rows * width * 10,
        scalar=False,
        out_spec=pl.BlockSpec(memory_space=pltpu.HBM),
    )
    return (towers, input_grad, first_grad.reshape(-1), second_grad.reshape(-1))


def solution(mesh):
    placed = (
        P(AXES, None),
        P(AXES, None),
        P(AXES),
        P(AXES),
        P(AXES, None),
    )
    return jax.shard_map(
        per_device,
        mesh=mesh,
        in_specs=placed,
        out_specs=(P(AXES, None), P(AXES, None), P(AXES), P(AXES)),
        check_vma=False,
    )
```
